32 devices in a mesh: seq: 8 (over y, x, core), head: 4 (over z).
Axes of the slice: x: 2, y: 2, z: 4, core: 2. Of those that a mesh axis runs over, the one named last changes fastest.
Arguments:
- queries: bfloat16 [2048, 2560], P('seq', 'head'), may hold values from -16 to 16
- keys: bfloat16 [2048, 2560], P('seq', 'head'), may hold values from -16 to 16
- values: bfloat16 [2048, 2560], P('seq', 'head'), may hold values from -6 to 6
- grad_out: bfloat16 [2048, 2560], P(('seq', 'head')), may hold values from -6 to 6
Outputs:
- grad_queries: bfloat16 [2048, 2560], P('seq', 'head')
- grad_keys: bfloat16 [2048, 2560], P('seq', 'head')
- grad_values: bfloat16 [2048, 2560], P('seq', 'head')
The draws below stay inside these ranges and needn't reach their ends.
All inputs are finite; a program needn't handle non-finite values.
Results may differ from the reference program's by a relative error of at most 0.0079.
Values may be sent and summed in bfloat16 or wider, within the bound.
No kernel may reach another device: no remote copies, remote signals or barrier semaphores. Data moves between devices by JAX's collectives and lax.ppermute only.
A program may use at most 64 MiB of HBM per device.

```python
import jax
import jax.numpy as jnp
from jax import lax

HEADS = 32
HD = 80
D = 2560
TOKENS_PER_INDEX = 256
LEVEL1_SPAN = 4
LEVEL1_DILATION = 4
LEVEL2_SPAN = 8
LEVEL2_DILATION = 8
TOKENS = 2048


def draw_queries(key, part):
    key = jax.random.fold_in(key, 5)
    field = jax.random.normal(key, (TOKENS, D), jnp.float32)
    return jnp.clip(field, -16.0, 16.0).astype(jnp.bfloat16)


def draw_keys(key, part):
    key = jax.random.fold_in(key, 7)
    field = jax.random.normal(key, (TOKENS, D), jnp.float32)
    return jnp.clip(field, -16.0, 16.0).astype(jnp.bfloat16)


def steps_of(key, dims, shards, least, high):
    factor_of = 1.0
    for axis_at, shards_of in shards:
        steps = jax.random.uniform(jax.random.fold_in(jax.random.fold_in(key, 6), axis_at), (shards_of,), jnp.float32, least / len(shards), high / len(shards))
        factor_of = factor_of * jnp.repeat(jnp.exp(steps), dims[axis_at] // shards_of).reshape((-1,) + (1,) * (len(dims) - 1 - axis_at))
    return factor_of


def bell_draw(stream_key, extent, scale, limit, shards=(), held_as=jnp.bfloat16):
    result = jax.random.normal(stream_key, extent, jnp.float32) * scale
    if len(shards) > 0:
        result = steps_of(stream_key, extent, shards, -0.22, 0.18) * result
    return jnp.clip(result, min=-limit, max=limit).astype(held_as)


def setup_inputs(seed: int = 0) -> dict:
    splits = jax.random.split(jax.random.key(seed), 5)
    queries = draw_queries(jax.random.fold_in(splits[4], 71), 0)
    keys = draw_keys(jax.random.fold_in(splits[4], 71), 0)
    values = bell_draw(splits[2], (TOKENS, D), 1.0, 6.0, ((0, 8), (1, 4)))
    grad_out = bell_draw(splits[3], (TOKENS, D), 1.0, 6.0, ((0, 32),))
    return {"queries": queries, "keys": keys, "values": values, "grad_out": grad_out}


def level_plan():
    return ((TOKENS_PER_INDEX, 1), (LEVEL1_SPAN * TOKENS_PER_INDEX, LEVEL1_DILATION), (LEVEL2_SPAN * TOKENS_PER_INDEX, LEVEL2_DILATION))


def pick_rows(field, width, stride, offset):
    shaped = field.reshape(TOKENS // width, width // stride, stride, field.shape[-1])
    return jnp.take(shaped, offset, axis=2)


def place_rows(sparse, stride, offset, fill):
    lanes = jnp.arange(stride, dtype=jnp.int32) == offset
    widened = jnp.where(lanes[None, None, :, None], sparse[:, :, None, :], fill)
    return widened.reshape(TOKENS, sparse.shape[-1])


def causal_scores(query_rows, key_rows):
    scale = HD ** -0.5
    scores = jnp.einsum("nid,njd->nij", query_rows, key_rows) * scale
    length = query_rows.shape[1]
    later = jnp.arange(length)[:, None] >= jnp.arange(length)[None, :]
    return jnp.where(later[None], scores, -jnp.inf)


def one_head(operands):
    head, queries, keys, values, grads = operands
    single = jnp.float32
    picked = []
    lse_rows = []
    for width, stride in level_plan():
        offset = head % stride
        level_rows = [pick_rows(field, width, stride, offset).astype(single) for field in (queries, keys, values, grads)]
        scores = causal_scores(level_rows[0], level_rows[1])
        top = jnp.max(scores, axis=-1)
        lse = top + jnp.log(jnp.sum(jnp.exp(scores - top[..., None]), axis=-1))
        lse_rows.append(place_rows(lse[..., None], stride, offset, -jnp.inf)[:, 0])
        picked.append((width, stride, offset, level_rows, scores))
    stacked = jnp.stack(lse_rows)
    peak = jnp.max(stacked, axis=0)
    total = peak + jnp.log(jnp.sum(jnp.exp(stacked - peak[None]), axis=0))
    merged = jnp.zeros((TOKENS, HD), single)
    kept_probs = []
    for width, stride, offset, level_rows, scores in picked:
        level_total = pick_rows(total[:, None], width, stride, offset)[..., 0]
        prob = jnp.exp(scores - level_total[..., None])
        weight = lax.optimization_barrier(prob.astype(jnp.bfloat16)).astype(single)
        partial_out = jnp.einsum("nij,njd->nid", weight, level_rows[2])
        merged = merged + place_rows(partial_out, stride, offset, 0.0)
        kept_probs.append((prob, weight))
    delta = jnp.sum(grads.astype(single) * merged, axis=-1)
    grad_q = jnp.zeros((TOKENS, HD), single)
    grad_k = jnp.zeros((TOKENS, HD), single)
    grad_v = jnp.zeros((TOKENS, HD), single)
    for (width, stride, offset, level_rows, scores), (prob, weight) in zip(picked, kept_probs):
        level_delta = pick_rows(delta[:, None], width, stride, offset)[..., 0]
        dprob = jnp.einsum("nid,njd->nij", level_rows[3], level_rows[2])
        dscore = prob * (dprob - level_delta[..., None]) * (HD ** -0.5)
        dscore = lax.optimization_barrier(dscore.astype(jnp.bfloat16)).astype(single)
        grad_q = grad_q + place_rows(jnp.einsum("nij,njd->nid", dscore, level_rows[1]), stride, offset, 0.0)
        grad_k = grad_k + place_rows(jnp.einsum("nij,nid->njd", dscore, level_rows[0]), stride, offset, 0.0)
        grad_v = grad_v + place_rows(jnp.einsum("nij,nid->njd", weight, level_rows[3]), stride, offset, 0.0)
    return grad_q.astype(jnp.bfloat16), grad_k.astype(jnp.bfloat16), grad_v.astype(jnp.bfloat16)


def by_head(field):
    return field.reshape(TOKENS, HEADS, HD).transpose(1, 0, 2)


def from_heads(field):
    return field.transpose(1, 0, 2).reshape(TOKENS, D)


def reference(queries, keys, values, grad_out):
    head_ids = jnp.arange(HEADS, dtype=jnp.int32)
    grad_q, grad_k, grad_v = lax.map(one_head, (head_ids, by_head(queries), by_head(keys), by_head(values), by_head(grad_out)))
    return from_heads(grad_q), from_heads(grad_k), from_heads(grad_v)
```

```python
import functools
import math

import jax
import jax.numpy as jnp
from jax import lax
from jax.experimental import pallas as pl
from jax.experimental.pallas import tpu as pltpu
from jax.sharding import PartitionSpec as P

HD = 80
SPAN1 = 4
DIL1 = 4
WIDEST = 32
LANES = 128
BF16 = jnp.bfloat16
F32 = jnp.float32
SCALE = HD**-0.5
SCALE2 = SCALE * math.log2(math.e)
VMEM_BYTES = 48 * 2**20


class Plan:
    def __init__(self, tokens, width, seq_count, head_count):
        self.tokens = tokens
        self.width = width
        self.heads = width // HD
        self.g1 = SPAN1
        self.g2 = min(WIDEST, seq_count)
        self.r2 = self.g2
        self.n1 = tokens // DIL1
        self.n2 = tokens // self.r2
        self.turns = self.r2 // DIL1
        self.zcount = head_count
        self.rows = [2 * (self.n1 if b < self.g1 else self.n2) for b in range(self.g2)]


def nt(a, b):
    return lax.dot_general(a, b, (((1,), (1,)), ((), ())), preferred_element_type=F32)


def nn(a, b):
    return lax.dot_general(a, b, (((1,), (0,)), ((), ())), preferred_element_type=F32)


def tn(a, b):
    return lax.dot_general(a, b, (((0,), (0,)), ((), ())), preferred_element_type=F32)


def iota(shape, dim):
    return lax.broadcasted_iota(jnp.int32, shape, dim)


def phase_order(p, inverse=False):
    shape = (p.tokens, p.tokens)
    row, col = (iota(shape, 1), iota(shape, 0)) if inverse else (iota(shape, 0), iota(shape, 1))
    return jnp.where(col == p.r2 * (row % p.n2) + row // p.n2, 1.0, 0.0).astype(BF16)


def first_head(p):
    return lax.axis_index("head") * p.heads


def column_class(p):
    return (first_head(p) + iota((1, p.width), 1) // HD) % p.r2


def lane_class(p):
    return (first_head(p) + iota((1, LANES), 1)) % p.r2


def pick(p, whole, label):
    parts = []
    for t in range(p.turns):
        want = (label + DIL1 * t) % p.r2
        part = jnp.zeros((p.n2, whole.shape[1]), F32)
        for c in range(p.r2):
            part = jnp.where(want == c, whole[c * p.n2 : (c + 1) * p.n2], part)
        parts.append(part)
    return jnp.concatenate(parts, axis=0)


def spread(p, kept, label, base):
    parts = []
    for c in range(p.r2):
        part = base[c * p.n2 : (c + 1) * p.n2]
        for t in range(p.turns):
            hit = (label + DIL1 * t) % p.r2 == c
            part = jnp.where(hit, kept[t * p.n2 : (t + 1) * p.n2], part)
        parts.append(part)
    return jnp.concatenate(parts, axis=0)


def window(h):
    low = h * HD // LANES * LANES
    high = -(-(h + 1) * HD // LANES) * LANES
    return low, high


def window_mask(h, low, high):
    lane = low + iota((1, high - low), 1)
    return (lane >= h * HD) & (lane < (h + 1) * HD)


def head_mask(p, h):
    lane = iota((1, p.width), 1)
    return (lane >= h * HD) & (lane < (h + 1) * HD)


def own_bias(p):
    shape = (p.tokens, p.tokens)
    row, col = iota(shape, 0), iota(shape, 1)
    qpos = p.r2 * (row % p.n2) + row // p.n2
    kpos = p.r2 * (col % p.n2) + col // p.n2
    return jnp.where(qpos >= kpos, 0.0, -jnp.inf)


def call(kernel, outs, scratch=(), flops=0):
    return pl.pallas_call(
        kernel,
        out_shape=[jax.ShapeDtypeStruct(s, d) for s, d in outs],
        scratch_shapes=[pltpu.VMEM(s, d) for s, d in scratch],
        compiler_params=pltpu.CompilerParams(vmem_limit_bytes=VMEM_BYTES),
        cost_estimate=pl.CostEstimate(flops=flops, bytes_accessed=2**20, transcendentals=0),
    )


def pack_kernel(p, q_ref, k_ref, v_ref, g_ref, qp, kp, vp, q1, kv1, kv2, *gz):
    z = lax.axis_index("head")
    for b in range(p.zcount):
        start = pl.multiple_of(jnp.bitwise_xor(z, b) * p.width, LANES)
        gz[b][...] = g_ref[:, pl.ds(start, p.width)]
    order = phase_order(p)
    label = column_class(p)
    k = nn(order, k_ref[...])
    kp[...] = k.astype(BF16)
    k_kept = pick(p, k, label)
    v = nn(order, v_ref[...])
    vp[...] = v.astype(BF16)
    v_kept = pick(p, v, label)
    kv1[...] = jnp.concatenate([k_kept, v_kept], axis=0).astype(BF16)
    kv2[...] = jnp.concatenate([k_kept[: p.n2], v_kept[: p.n2]], axis=0).astype(BF16)
    q = nn(order, q_ref[...])
    qp[...] = q.astype(BF16)
    q1[...] = pick(p, q, label).astype(BF16)


def own_kernel(p, qp, kp, vp, *refs):
    gz, (gp, g1, lse0, d0, lse01, d01, natural) = refs[: p.zcount], refs[p.zcount :]
    z = lax.axis_index("head")
    share = p.tokens // p.zcount
    for b in range(p.zcount):
        start = pl.multiple_of(jnp.bitwise_xor(z, b) * share, share)
        natural[pl.ds(start, share), :] = gz[b][...]
    g = nn(phase_order(p), natural[...])
    gp[...] = g.astype(BF16)
    g1[...] = pick(p, g, column_class(p)).astype(BF16)
    bias = own_bias(p)
    lane = iota((1, LANES), 1)
    lse_all = jnp.zeros((p.tokens, LANES), F32)
    d_all = jnp.zeros((p.tokens, LANES), F32)
    for h in range(p.heads):
        low, high = window(h)
        mask = jnp.where(window_mask(h, low, high), 1.0, 0.0).astype(BF16)
        s = nt(qp[:, low:high] * mask, kp[:, low:high]) * SCALE2 + bias
        top = jnp.max(s, axis=1, keepdims=True)
        e = jnp.exp2(s - top)
        denom = jnp.sum(e, axis=1, keepdims=True)
        dp = nt(gp[:, low:high] * mask, vp[:, low:high])
        d = jnp.sum(e * dp, axis=1, keepdims=True) / denom
        lse_all = jnp.where(lane == h, top + jnp.log2(denom), lse_all)
        d_all = jnp.where(lane == h, d, d_all)
    lse0[...] = lse_all
    d0[...] = d_all
    label = lane_class(p)
    lse01[...] = pick(p, lse_all, label)
    d01[...] = pick(p, d_all, label)


def columns(p, stat):
    return jnp.concatenate([stat[:, h : h + 1] for h in range(p.heads)], axis=0)


def to_lanes(p, column):
    lane = iota((1, LANES), 1)
    out = jnp.zeros((p.n1, LANES), F32)
    for h in range(p.heads):
        out = jnp.where(lane == h, column[h * p.n1 : (h + 1) * p.n1], out)
    return out


def wide_rows(p, column):
    return jnp.concatenate([column[h * p.n1 : h * p.n1 + p.n2] for h in range(p.heads)], axis=0)


def widen(p, column, fill):
    rest = jnp.full((p.n1 - p.n2, column.shape[1]), fill, F32)
    parts = []
    for h in range(p.heads):
        parts += [column[h * p.n2 : (h + 1) * p.n2], rest]
    return jnp.concatenate(parts, axis=0)


def by_head(p, rows):
    parts = [jnp.where(head_mask(p, h), rows, 0.0) for h in range(p.heads)]
    return jnp.concatenate(parts, axis=0).astype(BF16)


def merge_heads(p, rows, count):
    out = jnp.zeros((count, p.width), F32)
    for h in range(p.heads):
        out = jnp.where(head_mask(p, h), rows[h * count : (h + 1) * count], out)
    return out


def levels_kernel(p, q1, g1, lse01, d01, *refs):
    kv = refs[: p.g2]
    dq1, total1, delta1, keep, send = refs[p.g2 :]
    d = lax.axis_index("seq")
    n1, n2 = p.n1, p.n2
    blocks = [ref[...].astype(F32) for ref in kv]
    k1 = jnp.concatenate([blocks[b][:n1] for b in range(p.g1)], axis=0).astype(BF16)
    v1 = jnp.concatenate([blocks[b][n1:] for b in range(p.g1)], axis=0).astype(BF16)
    k2 = jnp.concatenate([block[:n2] for block in blocks], axis=0).astype(BF16)
    v2 = jnp.concatenate(
        [block[half : half + n2] for block, half in zip(blocks, [r // 2 for r in p.rows])], axis=0
    ).astype(BF16)
    q_rows, g_rows = q1[...].astype(F32), g1[...].astype(F32)
    q1b, g1b = by_head(p, q_rows), by_head(p, g_rows)
    q2b, g2b = by_head(p, q_rows[:n2]), by_head(p, g_rows[:n2])

    shape1 = (p.heads * n1, p.g1 * n1)
    row = iota((shape1[0], 1), 0)
    col = iota((1, shape1[1]), 1)
    head = first_head(p) + row // n1
    own = row % n1
    qpos = p.tokens * d + p.r2 * (own % n2) + (head + DIL1 * (own // n2)) % p.r2
    other = col % n1
    kbase = p.tokens * jnp.bitwise_xor(d, col // n1) + p.r2 * (other % n2)
    kpos = kbase + jnp.bitwise_and(head + DIL1 * (other // n2), p.r2 - 1)
    s1 = jnp.where(kpos <= qpos, nt(q1b, k1) * SCALE2, -jnp.inf)
    top1 = jnp.max(s1, axis=1, keepdims=True)
    lse1 = top1 + jnp.log2(jnp.sum(jnp.exp2(s1 - top1), axis=1, keepdims=True))

    row2 = d * n2 + iota((p.heads * n2, 1), 0) % n2
    col2 = iota((1, p.g2 * n2), 1)
    col2 = jnp.bitwise_xor(d, col2 // n2) * n2 + col2 % n2
    s2 = jnp.where(col2 <= row2, nt(q2b, k2) * SCALE2, -jnp.inf)
    top2 = jnp.max(s2, axis=1, keepdims=True)
    lse2 = top2 + jnp.log2(jnp.sum(jnp.exp2(s2 - top2), axis=1, keepdims=True))

    lse0 = columns(p, lse01[...])
    lse2 = widen(p, lse2, -jnp.inf)
    peak = jnp.maximum(jnp.maximum(lse0, lse1), lse2)
    share0 = jnp.exp2(lse0 - peak)
    total = peak + jnp.log2(share0 + jnp.exp2(lse1 - peak) + jnp.exp2(lse2 - peak))
    p1 = jnp.exp2(s1 - total)
    p2 = jnp.exp2(s2 - wide_rows(p, total))
    dp1 = nt(g1b, v1)
    dp2 = nt(g2b, v2)
    delta = jnp.exp2(lse0 - total) * columns(p, d01[...])
    delta += jnp.sum(p1 * dp1, axis=1, keepdims=True)
    delta += widen(p, jnp.sum(p2 * dp2, axis=1, keepdims=True), 0.0)
    ds1 = (p1 * (dp1 - delta) * SCALE).astype(BF16)
    ds2 = (p2 * (dp2 - wide_rows(p, delta)) * SCALE).astype(BF16)
    p1, p2 = p1.astype(BF16), p2.astype(BF16)

    dk1, dk2 = tn(ds1, q1b), tn(ds2, q2b)
    dv1, dv2 = tn(p1, g1b), tn(p2, g2b)
    at = [0, 0]
    for b in range(p.g2):
        rows = slice(b * n2, (b + 1) * n2)
        if b < p.g1:
            first = slice(b * n1, b * n1 + n2)
            rest = slice(b * n1 + n2, (b + 1) * n1)
            part = [dk1[first] + dk2[rows], dk1[rest], dv1[first] + dv2[rows], dv1[rest]]
        else:
            part = [dk2[rows], dv2[rows]]
        part = jnp.concatenate(part, axis=0)
        odd = b % 2
        ref = send if odd else keep
        ref[at[odd] : at[odd] + p.rows[b], :] = part.astype(ref.dtype)
        at[odd] += p.rows[b]
    dq = merge_heads(p, nn(ds1, k1), n1)
    wide = merge_heads(p, nn(ds2, k2), n2)
    dq1[...] = jnp.concatenate([dq[:n2] + wide, dq[n2:]], axis=0)
    total1[...] = to_lanes(p, total)
    delta1[...] = to_lanes(p, delta)


def chip_kernel(p, keep, came, own, *outs):
    at = 0
    for index, b in enumerate(range(0, p.g2, 2)):
        rows = slice(at, at + p.rows[b])
        block = keep[rows, :] + came[rows, :].astype(F32)
        if b == 0:
            own[...] = block
        else:
            outs[index - 1][...] = block.astype(BF16)
        at += p.rows[b]


def own_grad_kernel(p, qp, kp, vp, gp, lse0, d0, total1, delta1, dq1, grad_q, dk0, dv0, dq):
    label = lane_class(p)
    total = spread(p, total1[...], label, lse0[...])
    delta = spread(p, delta1[...], label, d0[...])
    bias = own_bias(p)
    for ref in (dq, dk0, dv0):
        ref[...] = jnp.zeros_like(ref)
    for h in range(p.heads):
        low, high = window(h)
        hit = window_mask(h, low, high)
        mask = jnp.where(hit, 1.0, 0.0).astype(BF16)
        q = qp[:, low:high] * mask
        g = gp[:, low:high] * mask
        k = kp[:, low:high]
        prob = jnp.exp2(nt(q, k) * SCALE2 + bias - total[:, h : h + 1])
        dp = nt(g, vp[:, low:high])
        ds = (prob * (dp - delta[:, h : h + 1]) * SCALE).astype(BF16)
        dq[:, low:high] = jnp.where(hit, nn(ds, k), dq[:, low:high])
        dk0[:, low:high] += tn(ds, q)
        dv0[:, low:high] += tn(prob.astype(BF16), g)
    zero = jnp.zeros((p.tokens, p.width), F32)
    all_q = dq[...] + spread(p, dq1[...], column_class(p), zero)
    grad_q[...] = nn(phase_order(p, True), all_q.astype(BF16)).astype(BF16)


def last_kernel(p, dk0, dv0, own, *refs):
    came, (grad_k, grad_v) = refs[:-2], refs[-2:]
    order = phase_order(p, True)
    label = column_class(p)
    zero = jnp.zeros((p.tokens, p.width), F32)
    sums = own[...]
    wide = []
    for ref, b in zip(came, range(2, p.g2, 2)):
        block = ref[...].astype(F32)
        if b < p.g1:
            sums = sums + block
        else:
            wide.append(block)
    for index, (base, grad) in enumerate(((dk0, grad_k), (dv0, grad_v))):
        kept = sums[index * p.n1 : (index + 1) * p.n1]
        if wide:
            first = kept[: p.n2]
            for block in wide:
                first = first + block[index * p.n2 : (index + 1) * p.n2]
            kept = jnp.concatenate([first, kept[p.n2 :]], axis=0)
        whole = base[...] + spread(p, kept, label, zero)
        grad[...] = nn(order, whole.astype(BF16)).astype(BF16)


def swap(block, axis, bits):
    count = lax.axis_size(axis)
    return lax.ppermute(block, axis, [(i, i ^ bits) for i in range(count)])


def body(queries, keys, values, grad_out):
    tokens, width = queries.shape
    p = Plan(tokens, width, lax.axis_size("seq"), lax.axis_size("head"))
    n1, n2 = p.n1, p.n2
    run = lambda kernel: functools.partial(kernel, p)
    row, kept = (tokens, width), (n1, width)
    share = (tokens // p.zcount, width)

    outs = call(
        run(pack_kernel),
        [(row, BF16)] * 3
        + [(kept, BF16), ((2 * n1, width), BF16), ((2 * n2, width), BF16)]
        + [(share, BF16)] * p.zcount,
    )(queries, keys, values, grad_out)
    qp, kp, vp, q1, kv1, kv2 = outs[:6]
    gz = outs[6:]
    gz = [gz[0]] + [swap(gz[b], "head", b) for b in range(1, p.zcount)]

    kv = {0: kv1}
    for b in range(2, p.g2, 2):
        kv[b] = swap(kv1 if b < p.g1 else kv2, "seq", b)
    for b in range(0, p.g2, 2):
        kv[b + 1] = swap(kv[b], "seq", 1)

    stat, stat1 = (tokens, LANES), (n1, LANES)
    gp, g1, lse0, d0, lse01, d01 = call(
        run(own_kernel),
        [(row, BF16), (kept, BF16), (stat, F32), (stat, F32), (stat1, F32), (stat1, F32)],
        [(row, BF16)],
    )(qp, kp, vp, *gz)
    half_rows = sum(p.rows[::2])
    dq1, total1, delta1, keep, send = call(
        run(levels_kernel),
        [
            (kept, F32),
            (stat1, F32),
            (stat1, F32),
            ((half_rows, width), F32),
            ((half_rows, width), BF16),
        ],
    )(q1, g1, lse01, d01, *[kv[b] for b in range(p.g2)])
    came = swap(send, "seq", 1)
    grad_q, dk0, dv0 = call(
        run(own_grad_kernel), [(row, BF16), (row, F32), (row, F32)], [(row, F32)]
    )(qp, kp, vp, gp, lse0, d0, total1, delta1, dq1)
    sums = call(
        run(chip_kernel),
        [((p.rows[0], width), F32)] + [((p.rows[b], width), BF16) for b in range(2, p.g2, 2)],
    )(keep, came)
    parts = [swap(s, "seq", b) for s, b in zip(sums[1:], range(2, p.g2, 2))]
    grad_k, grad_v = call(run(last_kernel), [(row, BF16)] * 2)(dk0, dv0, sums[0], *parts)
    return grad_q, grad_k, grad_v


def solution(mesh):
    return jax.shard_map(
        body,
        mesh=mesh,
        in_specs=(P("seq", "head"), P("seq", "head"), P("seq", "head"), P(("seq", "head"), None)),
        out_specs=(P("seq", "head"), P("seq", "head"), P("seq", "head")),
        check_vma=False,
    )
```

```python
import functools
import math

import jax
import jax.numpy as jnp
from jax import lax
from jax.experimental import pallas as pl
from jax.experimental.pallas import tpu as pltpu
from jax.sharding import PartitionSpec as P

HD = 80
SPAN1 = 4
DIL1 = 4
WIDEST = 32
LANES = 128
BF16 = jnp.bfloat16
F32 = jnp.float32
SCALE = HD**-0.5
SCALE2 = SCALE * math.log2(math.e)
VMEM_BYTES = 28 * 2**20


class Plan:
    def __init__(self, tokens, width, seq_count, head_count):
        self.tokens = tokens
        self.width = width
        self.heads = width // HD
        self.g1 = SPAN1
        self.g2 = min(WIDEST, seq_count)
        self.r2 = self.g2
        self.n1 = tokens // DIL1
        self.n2 = tokens // self.r2
        self.turns = self.r2 // DIL1
        self.zcount = head_count
        self.rows = [2 * (self.n1 if b < self.g1 else self.n2) for b in range(self.g2)]


def nt(a, b):
    return lax.dot_general(a, b, (((1,), (1,)), ((), ())), preferred_element_type=F32)


def nn(a, b):
    return lax.dot_general(a, b, (((1,), (0,)), ((), ())), preferred_element_type=F32)


def tn(a, b):
    return lax.dot_general(a, b, (((0,), (0,)), ((), ())), preferred_element_type=F32)


def iota(shape, dim):
    return lax.broadcasted_iota(jnp.int32, shape, dim)


def phase_order(p, inverse=False):
    shape = (p.tokens, p.tokens)
    row, col = (iota(shape, 1), iota(shape, 0)) if inverse else (iota(shape, 0), iota(shape, 1))
    return jnp.where(col == p.r2 * (row % p.n2) + row // p.n2, 1.0, 0.0).astype(BF16)


def first_head(p):
    return lax.axis_index("head") * p.heads


def column_class(p):
    return (first_head(p) + iota((1, p.width), 1) // HD) % p.r2


def lane_class(p):
    return (first_head(p) + iota((1, LANES), 1)) % p.r2


def pick(p, whole, label):
    parts = []
    for t in range(p.turns):
        want = (label + DIL1 * t) % p.r2
        part = jnp.zeros((p.n2, whole.shape[1]), F32)
        for c in range(p.r2):
            part = jnp.where(want == c, whole[c * p.n2 : (c + 1) * p.n2], part)
        parts.append(part)
    return jnp.concatenate(parts, axis=0)


def spread(p, kept, label, base):
    parts = []
    for c in range(p.r2):
        part = base[c * p.n2 : (c + 1) * p.n2]
        for t in range(p.turns):
            hit = (label + DIL1 * t) % p.r2 == c
            part = jnp.where(hit, kept[t * p.n2 : (t + 1) * p.n2], part)
        parts.append(part)
    return jnp.concatenate(parts, axis=0)


def window(h):
    low = h * HD // LANES * LANES
    high = -(-(h + 1) * HD // LANES) * LANES
    return low, high


def window_mask(h, low, high):
    lane = low + iota((1, high - low), 1)
    return (lane >= h * HD) & (lane < (h + 1) * HD)


def head_mask(p, h):
    lane = iota((1, p.width), 1)
    return (lane >= h * HD) & (lane < (h + 1) * HD)


def own_bias(p):
    shape = (p.tokens, p.tokens)
    row, col = iota(shape, 0), iota(shape, 1)
    qpos = p.r2 * (row % p.n2) + row // p.n2
    kpos = p.r2 * (col % p.n2) + col // p.n2
    return jnp.where(qpos >= kpos, 0.0, -jnp.inf)


def call(kernel, outs, scratch=(), flops=0, specs=None):
    return pl.pallas_call(
        kernel,
        out_shape=[jax.ShapeDtypeStruct(s, d) for s, d in outs],
        **({} if specs is None else {"in_specs": specs}),
        scratch_shapes=[pltpu.VMEM(*s) if isinstance(s, tuple) else s for s in scratch],
        compiler_params=pltpu.CompilerParams(vmem_limit_bytes=VMEM_BYTES),
        cost_estimate=pl.CostEstimate(flops=flops, bytes_accessed=2**20, transcendentals=0),
    )


def slab(p, g_ref, b):
    start = pl.multiple_of(jnp.bitwise_xor(lax.axis_index("head"), b) * p.width, LANES)
    return g_ref.at[:, pl.ds(start, p.width)]


def far_kernel(p, g_ref, out, sem):
    copy = pltpu.make_async_copy(slab(p, g_ref, p.zcount - 1), out, sem)
    copy.start()
    copy.wait()


def pack_kernel(p, q_ref, k_ref, v_ref, g_ref, qp, kp, vp, q1, kv1, kv2, *refs):
    gz, (q_in, k_in, v_in, sems) = refs[: p.zcount - 1], refs[p.zcount - 1 :]
    loads = [(k_ref, k_in), (v_ref, v_in), (q_ref, q_in)]
    loads += [(slab(p, g_ref, b), gz[b]) for b in range(p.zcount - 1)]
    copies = [pltpu.make_async_copy(src, dst, sems.at[i]) for i, (src, dst) in enumerate(loads)]
    for copy in copies:
        copy.start()
    order = phase_order(p)
    label = column_class(p)
    copies[0].wait()
    k = nn(order, k_in[...])
    kp[...] = k.astype(BF16)
    k_kept = pick(p, k, label)
    copies[1].wait()
    v = nn(order, v_in[...])
    vp[...] = v.astype(BF16)
    v_kept = pick(p, v, label)
    kv1[...] = jnp.concatenate([k_kept, v_kept], axis=0).astype(BF16)
    kv2[...] = jnp.concatenate([k_kept[: p.n2], v_kept[: p.n2]], axis=0).astype(BF16)
    copies[2].wait()
    q = nn(order, q_in[...])
    qp[...] = q.astype(BF16)
    q1[...] = pick(p, q, label).astype(BF16)
    for copy in copies[3:]:
        copy.wait()


def own_scores_kernel(p, qp, kp, weight, lse0, lse01):
    bias = own_bias(p)
    lane = iota((1, LANES), 1)
    lse_all = jnp.zeros((p.tokens, LANES), F32)
    for h in range(p.heads):
        low, high = window(h)
        mask = jnp.where(window_mask(h, low, high), 1.0, 0.0).astype(BF16)
        s = nt(qp[:, low:high] * mask, kp[:, low:high]) * SCALE2 + bias
        top = jnp.max(s, axis=1, keepdims=True)
        e = jnp.exp2(s - top)
        denom = jnp.sum(e, axis=1, keepdims=True)
        weight[h * p.tokens : (h + 1) * p.tokens, :] = e * (1.0 / denom)
        lse_all = jnp.where(lane == h, top + jnp.log2(denom), lse_all)
    lse0[...] = lse_all
    lse01[...] = pick(p, lse_all, lane_class(p))


def own_delta_kernel(p, vp, weight, *refs):
    gz, (gp, g1, dprob, d0, d01, natural) = refs[: p.zcount], refs[p.zcount :]
    z = lax.axis_index("head")
    share = p.tokens // p.zcount
    for b in range(p.zcount):
        start = pl.multiple_of(jnp.bitwise_xor(z, b) * share, share)
        natural[pl.ds(start, share), :] = gz[b][...]
    g = nn(phase_order(p), natural[...])
    gp[...] = g.astype(BF16)
    g1[...] = pick(p, g, column_class(p)).astype(BF16)
    lane = iota((1, LANES), 1)
    d_all = jnp.zeros((p.tokens, LANES), F32)
    for h in range(p.heads):
        low, high = window(h)
        rows = slice(h * p.tokens, (h + 1) * p.tokens)
        mask = jnp.where(window_mask(h, low, high), 1.0, 0.0).astype(BF16)
        dp = nt(gp[:, low:high] * mask, vp[:, low:high])
        dprob[rows, :] = dp
        d = jnp.sum(weight[rows, :] * dp, axis=1, keepdims=True)
        d_all = jnp.where(lane == h, d, d_all)
    d0[...] = d_all
    d01[...] = pick(p, d_all, lane_class(p))


def merge_kernel(p, *refs):
    out = refs[-1]
    at = 0
    for ref in refs[:-1]:
        out[at : at + ref.shape[0], :] = ref[...]
        at += ref.shape[0]


def columns(p, stat):
    return jnp.concatenate([stat[:, h : h + 1] for h in range(p.heads)], axis=0)


def to_lanes(p, column):
    lane = iota((1, LANES), 1)
    out = jnp.zeros((p.n1, LANES), F32)
    for h in range(p.heads):
        out = jnp.where(lane == h, column[h * p.n1 : (h + 1) * p.n1], out)
    return out


def wide_rows(p, column):
    return jnp.concatenate([column[h * p.n1 : h * p.n1 + p.n2] for h in range(p.heads)], axis=0)


def widen(p, column, fill):
    rest = jnp.full((p.n1 - p.n2, column.shape[1]), fill, F32)
    parts = []
    for h in range(p.heads):
        parts += [column[h * p.n2 : (h + 1) * p.n2], rest]
    return jnp.concatenate(parts, axis=0)


def by_head(p, rows):
    if rows.shape[0] % 16:
        rows = rows.astype(F32)
    parts = []
    for h in range(p.heads):
        mask = jnp.where(head_mask(p, h), 1.0, 0.0).astype(rows.dtype)
        parts.append(rows * mask)
    return jnp.concatenate(parts, axis=0).astype(BF16)


def cut(p, block, start, count):
    if start % 16 or count % 16:
        block = block.astype(F32)
    return block[start : start + count]


def merge_heads(p, rows, count):
    out = jnp.zeros((count, p.width), F32)
    for h in range(p.heads):
        out = jnp.where(head_mask(p, h), rows[h * count : (h + 1) * count], out)
    return out


def scores_kernel(p, q1, lse01, came, *refs):
    even = refs[: p.g2 // 2]
    k1, v1, k2, v2, p1, p2, total1, share1 = refs[p.g2 // 2 :]
    d = lax.axis_index("seq")
    n1, n2 = p.n1, p.n2
    blocks, at = [], 0
    for b in range(p.g2):
        if b % 2 == 0:
            blocks.append(even[b // 2][...])
        else:
            blocks.append(came[at : at + p.rows[b], :])
            at += p.rows[b]
    for half, (out1, out2) in enumerate(((k1, k2), (v1, v2))):
        parts = [cut(p, blocks[b], half * n1, n1) for b in range(p.g1)]
        out1[...] = jnp.concatenate(parts, axis=0).astype(BF16)
        parts = [cut(p, blocks[b], half * p.rows[b] // 2, n2) for b in range(p.g2)]
        out2[...] = jnp.concatenate(parts, axis=0).astype(BF16)
    q_rows = q1[...]
    q1b, q2b = by_head(p, q_rows), by_head(p, cut(p, q_rows, 0, n2))

    shape1 = (p.heads * n1, p.g1 * n1)
    row = iota((shape1[0], 1), 0)
    col = iota((1, shape1[1]), 1)
    head = first_head(p) + row // n1
    own = row % n1
    qpos = p.tokens * d + p.r2 * (own % n2) + (head + DIL1 * (own // n2)) % p.r2
    other = col % n1
    kbase = p.tokens * jnp.bitwise_xor(d, col // n1) + p.r2 * (other % n2)
    kpos = kbase + jnp.bitwise_and(head + DIL1 * (other // n2), p.r2 - 1)
    s1 = jnp.where(kpos <= qpos, nt(q1b, k1[...]) * SCALE2, -jnp.inf)
    top1 = jnp.max(s1, axis=1, keepdims=True)
    e1 = jnp.exp2(s1 - top1)
    lse1 = top1 + jnp.log2(jnp.sum(e1, axis=1, keepdims=True))

    row2 = d * n2 + iota((p.heads * n2, 1), 0) % n2
    col2 = iota((1, p.g2 * n2), 1)
    col2 = jnp.bitwise_xor(d, col2 // n2) * n2 + col2 % n2
    s2 = jnp.where(col2 <= row2, nt(q2b, k2[...]) * SCALE2, -jnp.inf)
    top2 = jnp.max(s2, axis=1, keepdims=True)
    e2 = jnp.exp2(s2 - top2)
    lse2 = top2 + jnp.log2(jnp.sum(e2, axis=1, keepdims=True))

    lse0 = columns(p, lse01[...])
    lse2 = widen(p, lse2, -jnp.inf)
    peak = jnp.maximum(jnp.maximum(lse0, lse1), lse2)
    total = peak + jnp.log2(jnp.exp2(lse0 - peak) + jnp.exp2(lse1 - peak) + jnp.exp2(lse2 - peak))
    p1[...] = e1 * jnp.exp2(top1 - total)
    p2[...] = e2 * jnp.exp2(top2 - wide_rows(p, total))
    total1[...] = to_lanes(p, total)
    share1[...] = to_lanes(p, jnp.exp2(lse0 - total))


def levels_kernel(p, q1, g1, k1, v1, k2, v2, p1, p2, share1, d01, dq1, delta1, keep, send):
    n1, n2 = p.n1, p.n2
    q_rows, g_rows = q1[...], g1[...]
    q1b, g1b = by_head(p, q_rows), by_head(p, g_rows)
    q2b, g2b = by_head(p, cut(p, q_rows, 0, n2)), by_head(p, cut(p, g_rows, 0, n2))
    prob1, prob2 = p1[...], p2[...]
    dp1 = nt(g1b, v1[...])
    dp2 = nt(g2b, v2[...])
    delta = columns(p, share1[...] * d01[...])
    delta += jnp.sum(prob1 * dp1, axis=1, keepdims=True)
    delta += widen(p, jnp.sum(prob2 * dp2, axis=1, keepdims=True), 0.0)
    ds1 = (prob1 * (dp1 - delta) * SCALE).astype(BF16)
    ds2 = (prob2 * (dp2 - wide_rows(p, delta)) * SCALE).astype(BF16)

    dk1, dk2 = tn(ds1, q1b), tn(ds2, q2b)
    dv1, dv2 = tn(prob1.astype(BF16), g1b), tn(prob2.astype(BF16), g2b)
    at = [0, 0]
    for b in range(p.g2):
        rows = slice(b * n2, (b + 1) * n2)
        if b < p.g1:
            first = slice(b * n1, b * n1 + n2)
            rest = slice(b * n1 + n2, (b + 1) * n1)
            part = [dk1[first] + dk2[rows], dk1[rest], dv1[first] + dv2[rows], dv1[rest]]
        else:
            part = [dk2[rows], dv2[rows]]
        part = jnp.concatenate(part, axis=0)
        odd = b % 2
        ref = send if odd else keep
        ref[at[odd] : at[odd] + p.rows[b], :] = part.astype(ref.dtype)
        at[odd] += p.rows[b]
    dq = merge_heads(p, nn(ds1, k1[...]), n1)
    wide = merge_heads(p, nn(ds2, k2[...]), n2)
    dq1[...] = jnp.concatenate([dq[:n2] + wide, dq[n2:]], axis=0)
    delta1[...] = to_lanes(p, delta)


def chip_kernel(p, keep, came, own, *outs):
    at = 0
    for index, b in enumerate(range(0, p.g2, 2)):
        rows = slice(at, at + p.rows[b])
        block = keep[rows, :] + came[rows, :].astype(F32)
        if b == 0:
            own[...] = block
        else:
            outs[index - 1][...] = block.astype(BF16)
        at += p.rows[b]


def own_grad_kernel(
    p, qp, kp, gp, weight, dprob, lse0, d0, total1, delta1, dq1, grad_q, dk0, dv0, dq
):
    label = lane_class(p)
    lse = lse0[...]
    share = jnp.exp2(lse - spread(p, total1[...], label, lse))
    delta = spread(p, delta1[...], label, d0[...])
    for ref in (dk0, dv0):
        ref[...] = jnp.zeros_like(ref)
    for h in range(p.heads):
        low, high = window(h)
        rows = slice(h * p.tokens, (h + 1) * p.tokens)
        hit = window_mask(h, low, high)
        mask = jnp.where(hit, 1.0, 0.0).astype(BF16)
        prob = weight[rows, :] * share[:, h : h + 1]
        ds = (prob * (dprob[rows, :] - delta[:, h : h + 1]) * SCALE).astype(BF16)
        dq[:, low:high] = jnp.where(hit, nn(ds, kp[:, low:high]), dq[:, low:high])
        dk0[:, low:high] += tn(ds, qp[:, low:high] * mask)
        dv0[:, low:high] += tn(prob.astype(BF16), gp[:, low:high] * mask)
    zero = jnp.zeros((p.tokens, p.width), F32)
    all_q = dq[...] + spread(p, dq1[...], column_class(p), zero)
    grad_q[...] = nn(phase_order(p, True), all_q.astype(BF16)).astype(BF16)


def last_kernel(p, dk0, dv0, own, *refs):
    came, (grad_k, grad_v) = refs[:-2], refs[-2:]
    order = phase_order(p, True)
    label = column_class(p)
    zero = jnp.zeros((p.tokens, p.width), F32)
    sums = own[...]
    wide = []
    for ref, b in zip(came, range(2, p.g2, 2)):
        block = ref[...].astype(F32)
        if b < p.g1:
            sums = sums + block
        else:
            wide.append(block)
    for index, (base, grad) in enumerate(((dk0, grad_k), (dv0, grad_v))):
        kept = sums[index * p.n1 : (index + 1) * p.n1]
        if wide:
            first = kept[: p.n2]
            for block in wide:
                first = first + block[index * p.n2 : (index + 1) * p.n2]
            kept = jnp.concatenate([first, kept[p.n2 :]], axis=0)
        whole = base[...] + spread(p, kept, label, zero)
        grad[...] = nn(order, whole.astype(BF16)).astype(BF16)


def swap(block, axis, bits):
    count = lax.axis_size(axis)
    return lax.ppermute(block, axis, [(i, i ^ bits) for i in range(count)])


def body(queries, keys, values, grad_out):
    tokens, width = queries.shape
    queries, keys, values, grad_out = (
        pltpu.with_memory_space_constraint(field, pltpu.HBM)
        for field in (queries, keys, values, grad_out)
    )
    p = Plan(tokens, width, lax.axis_size("seq"), lax.axis_size("head"))
    n1, n2 = p.n1, p.n2
    run = lambda kernel: functools.partial(kernel, p)
    row, kept = (tokens, width), (n1, width)
    share = (tokens // p.zcount, width)
    stat, stat1 = (tokens, LANES), (n1, LANES)
    flat = lambda count: (count, tokens)
    even = range(0, p.g2, 2)
    half_rows = sum(p.rows[::2])
    hbm = pl.BlockSpec(memory_space=pltpu.HBM)

    (far,) = call(run(far_kernel), [(share, BF16)], [pltpu.SemaphoreType.DMA], specs=[hbm])(grad_out)
    outs = call(
        run(pack_kernel),
        [(row, BF16)] * 3
        + [(kept, BF16), ((2 * n1, width), BF16), ((2 * n2, width), BF16)]
        + [(share, BF16)] * (p.zcount - 1),
        [(row, BF16)] * 3 + [pltpu.SemaphoreType.DMA((p.zcount + 2,))],
        specs=[hbm] * 4,
    )(queries, keys, values, grad_out)
    qp, kp, vp, q1, kv1, kv2 = outs[:6]
    gz = [*outs[6:], far]
    gz = [gz[0]] + [swap(gz[b], "head", b) for b in range(1, p.zcount)]

    kv = [kv1] + [swap(kv1 if b < p.g1 else kv2, "seq", b) for b in even[1:]]
    (sent,) = call(run(merge_kernel), [((half_rows, width), BF16)])(*kv)
    came = swap(sent, "seq", 1)

    weight, lse0, lse01 = call(
        run(own_scores_kernel), [(flat(p.heads * tokens), F32), (stat, F32), (stat1, F32)]
    )(qp, kp)
    k1, v1, k2, v2, p1, p2, total1, share1 = call(
        run(scores_kernel),
        [(row, BF16)] * 4
        + [(flat(p.heads * n1), F32), (flat(p.heads * n2), F32), (stat1, F32), (stat1, F32)],
    )(q1, lse01, came, *kv)
    gp, g1, dprob, d0, d01 = call(
        run(own_delta_kernel),
        [(row, BF16), (kept, BF16), (flat(p.heads * tokens), F32), (stat, F32), (stat1, F32)],
        [(row, BF16)],
        flops=2 * 10**10,
    )(vp, weight, *gz)
    dq1, delta1, keep, send = call(
        run(levels_kernel),
        [
            (kept, F32),
            (stat1, F32),
            ((half_rows, width), F32),
            ((half_rows, width), BF16),
        ],
    )(q1, g1, k1, v1, k2, v2, p1, p2, share1, d01)
    returned = swap(send, "seq", 1)
    grad_q, dk0, dv0 = call(
        run(own_grad_kernel), [(row, BF16), (row, F32), (row, F32)], [(row, F32)]
    )(qp, kp, gp, weight, dprob, lse0, d0, total1, delta1, dq1)
    sums = call(
        run(chip_kernel),
        [((p.rows[0], width), F32)] + [((p.rows[b], width), BF16) for b in even[1:]],
    )(keep, returned)
    parts = [swap(s, "seq", b) for s, b in zip(sums[1:], even[1:])]
    grad_k, grad_v = call(run(last_kernel), [(row, BF16)] * 2)(dk0, dv0, sums[0], *parts)
    return grad_q, grad_k, grad_v


def solution(mesh):
    return jax.shard_map(
        body,
        mesh=mesh,
        in_specs=(P("seq", "head"), P("seq", "head"), P("seq", "head"), P(("seq", "head"), None)),
        out_specs=(P("seq", "head"), P("seq", "head"), P("seq", "head")),
        check_vma=False,
    )
```

```python
import functools
import math

import jax
import jax.numpy as jnp
from jax import lax
from jax.experimental import pallas as pl
from jax.experimental.pallas import tpu as pltpu
from jax.sharding import PartitionSpec as P

HD = 80
SPAN1 = 4
DIL1 = 4
WIDEST = 32
LANES = 128
BF16 = jnp.bfloat16
F32 = jnp.float32
SCALE = HD**-0.5
SCALE2 = SCALE * math.log2(math.e)
VMEM_BYTES = 28 * 2**20
LOWEST = -1e30
TINY = 1e-30


class Plan:
    def __init__(self, tokens, width, seq_count, head_count):
        self.tokens = tokens
        self.width = width
        self.heads = width // HD
        self.g1 = SPAN1
        self.g2 = min(WIDEST, seq_count)
        self.r2 = self.g2
        self.n1 = tokens // DIL1
        self.n2 = tokens // self.r2
        self.turns = self.r2 // DIL1
        self.zcount = head_count
        self.rows = [2 * (self.n1 if b < self.g1 else self.n2) for b in range(self.g2)]


def nt(a, b):
    return lax.dot_general(a, b, (((1,), (1,)), ((), ())), preferred_element_type=F32)


def nn(a, b):
    return lax.dot_general(a, b, (((1,), (0,)), ((), ())), preferred_element_type=F32)


def tn(a, b):
    return lax.dot_general(a, b, (((0,), (0,)), ((), ())), preferred_element_type=F32)


def iota(shape, dim):
    return lax.broadcasted_iota(jnp.int32, shape, dim)


def phase_order(p, inverse=False):
    shape = (p.tokens, p.tokens)
    row, col = (iota(shape, 1), iota(shape, 0)) if inverse else (iota(shape, 0), iota(shape, 1))
    return jnp.where(col == p.r2 * (row % p.n2) + row // p.n2, 1.0, 0.0).astype(BF16)


def first_head(p):
    return lax.axis_index("head") * p.heads


def column_class(p):
    return (first_head(p) + iota((1, p.width), 1) // HD) % p.r2


def lane_class(p):
    return (first_head(p) + iota((1, LANES), 1)) % p.r2


def pick(p, whole, label):
    parts = []
    for t in range(p.turns):
        want = (label + DIL1 * t) % p.r2
        part = jnp.zeros((p.n2, whole.shape[1]), F32)
        for c in range(p.r2):
            part = jnp.where(want == c, whole[c * p.n2 : (c + 1) * p.n2], part)
        parts.append(part)
    return jnp.concatenate(parts, axis=0)


def spread(p, kept, label, base):
    parts = []
    for c in range(p.r2):
        part = base[c * p.n2 : (c + 1) * p.n2]
        for t in range(p.turns):
            hit = (label + DIL1 * t) % p.r2 == c
            part = jnp.where(hit, kept[t * p.n2 : (t + 1) * p.n2], part)
        parts.append(part)
    return jnp.concatenate(parts, axis=0)


def window(h):
    low = h * HD // LANES * LANES
    high = -(-(h + 1) * HD // LANES) * LANES
    return low, high


def window_mask(h, low, high):
    lane = low + iota((1, high - low), 1)
    return (lane >= h * HD) & (lane < (h + 1) * HD)


def head_groups(p):
    groups, h = [], 0
    while h < p.heads:
        low, high = window(h)
        end = h + 1
        while end < p.heads and window(end)[1] - low <= 2 * LANES:
            high = window(end)[1]
            end += 1
        groups.append((h, end, low, high))
        h = end
    return groups


def head_mask(p, h):
    lane = iota((1, p.width), 1)
    return (lane >= h * HD) & (lane < (h + 1) * HD)


def own_bias(p):
    shape = (p.tokens, p.tokens)
    row, col = iota(shape, 0), iota(shape, 1)
    qpos = p.r2 * (row % p.n2) + row // p.n2
    kpos = p.r2 * (col % p.n2) + col // p.n2
    return jnp.where(qpos >= kpos, 0.0, -jnp.inf)


def call(kernel, outs, scratch=(), flops=0, specs=None):
    return pl.pallas_call(
        kernel,
        out_shape=[jax.ShapeDtypeStruct(s, d) for s, d in outs],
        **({} if specs is None else {"in_specs": specs}),
        scratch_shapes=[pltpu.VMEM(*s) if isinstance(s, tuple) else s for s in scratch],
        compiler_params=pltpu.CompilerParams(vmem_limit_bytes=VMEM_BYTES),
        cost_estimate=pl.CostEstimate(flops=flops, bytes_accessed=2**20, transcendentals=0),
    )


def slab(p, g_ref, b):
    start = pl.multiple_of(jnp.bitwise_xor(lax.axis_index("head"), b) * p.width, LANES)
    return g_ref.at[:, pl.ds(start, p.width)]


def pack_kernel(p, q_ref, k_ref, v_ref, g_ref, qp, kp, vp, q1, kv1, kv2, *refs):
    gz, (q_in, k_in, v_in, sems) = refs[: p.zcount], refs[p.zcount :]
    loads = [(k_ref, k_in), (v_ref, v_in), (q_ref, q_in)]
    loads += [(slab(p, g_ref, b), gz[b]) for b in range(p.zcount)]
    copies = [pltpu.make_async_copy(src, dst, sems.at[i]) for i, (src, dst) in enumerate(loads)]
    for copy in copies:
        copy.start()
    order = phase_order(p)
    label = column_class(p)
    copies[0].wait()
    k = nn(order, k_in[...])
    kp[...] = k.astype(BF16)
    k_kept = pick(p, k, label)
    copies[1].wait()
    v = nn(order, v_in[...])
    vp[...] = v.astype(BF16)
    v_kept = pick(p, v, label)
    kv1[...] = jnp.concatenate([k_kept, v_kept], axis=0).astype(BF16)
    kv2[...] = jnp.concatenate([k_kept[: p.n2], v_kept[: p.n2]], axis=0).astype(BF16)
    copies[2].wait()
    q = nn(order, q_in[...])
    qp[...] = q.astype(BF16)
    q1[...] = pick(p, q, label).astype(BF16)
    for copy in copies[3:]:
        copy.wait()


def own_scores_kernel(p, qp, kp, weight, lse0, lse01):
    bias = own_bias(p)
    lane = iota((1, LANES), 1)
    lse_all = jnp.zeros((p.tokens, LANES), F32)
    for h in range(p.heads):
        low, high = window(h)
        mask = jnp.where(window_mask(h, low, high), 1.0, 0.0).astype(BF16)
        s = nt(qp[:, low:high] * mask, kp[:, low:high]) * SCALE2 + bias
        top = jnp.max(s, axis=1, keepdims=True)
        e = jnp.exp2(s - top)
        denom = jnp.sum(e, axis=1, keepdims=True)
        weight[h * p.tokens : (h + 1) * p.tokens, :] = e * (1.0 / denom)
        lse_all = jnp.where(lane == h, top + jnp.log2(denom), lse_all)
    lse0[...] = lse_all
    lse01[...] = pick(p, lse_all, lane_class(p))


def gather_kernel(p, *refs):
    gz, (gp, g1, natural) = refs[: p.zcount], refs[p.zcount :]
    z = lax.axis_index("head")
    share = p.tokens // p.zcount
    for b in range(p.zcount):
        start = pl.multiple_of(jnp.bitwise_xor(z, b) * share, share)
        natural[pl.ds(start, share), :] = gz[b][...]
    g = nn(phase_order(p), natural[...])
    gp[...] = g.astype(BF16)
    g1[...] = pick(p, g, column_class(p)).astype(BF16)


def own_delta_kernel(p, vp, weight, gp, dprob, d0, d01):
    lane = iota((1, LANES), 1)
    d_all = jnp.zeros((p.tokens, LANES), F32)
    for h in range(p.heads):
        low, high = window(h)
        rows = slice(h * p.tokens, (h + 1) * p.tokens)
        mask = jnp.where(window_mask(h, low, high), 1.0, 0.0).astype(BF16)
        dp = nt(gp[:, low:high] * mask, vp[:, low:high])
        dprob[rows, :] = dp
        d = jnp.sum(weight[rows, :] * dp, axis=1, keepdims=True)
        d_all = jnp.where(lane == h, d, d_all)
    d0[...] = d_all
    d01[...] = pick(p, d_all, lane_class(p))


def columns(p, stat):
    return jnp.concatenate([stat[:, h : h + 1] for h in range(p.heads)], axis=0)


def to_lanes(p, column):
    lane = iota((1, LANES), 1)
    count = 2 * p.n1
    out = jnp.zeros((count, LANES), F32)
    for h in range(p.heads):
        out = jnp.where(lane == h, column[h * count : (h + 1) * count], out)
    return out


def wide_rows(p, column):
    starts = range(0, 2 * p.heads * p.n1, p.n1)
    return jnp.concatenate([column[s : s + p.n2] for s in starts], axis=0)


def widen(p, column, fill):
    rest = jnp.full((p.n1 - p.n2, column.shape[1]), fill, F32)
    parts = []
    for s in range(0, 2 * p.heads * p.n2, p.n2):
        parts += [column[s : s + p.n2], rest]
    return jnp.concatenate(parts, axis=0)


def cut(p, block, start, count):
    if start % 16 or count % 16:
        block = block.astype(F32)
    return block[start : start + count]


def both_cores(p, own, other, count):
    return jnp.concatenate([cut(p, own, 0, count), cut(p, other, 0, count)], axis=0)


def by_head(p, rows, group):
    first, end, low, high = group
    parts = []
    for h in range(first, end):
        mask = jnp.where(window_mask(h, low, high), 1.0, 0.0).astype(rows.dtype)
        parts.append(rows[:, low:high] * mask)
    return jnp.concatenate(parts, axis=0).astype(BF16)


def against(p, rows, cols):
    parts = []
    for group in head_groups(p):
        low, high = group[2:]
        parts.append(nt(by_head(p, rows, group), cols[:, low:high]))
    return jnp.concatenate(parts, axis=0)


def collect(p, weights, rows, out):
    count = rows.shape[0]
    for group in head_groups(p):
        first, end, low, high = group
        part = tn(weights[first * count : end * count], by_head(p, rows, group))
        out[:, low:high] += part


def back(p, weights, cols, count, out):
    for first, end, low, high in head_groups(p):
        part = nn(weights[first * count : end * count], cols[:, low:high])
        for h in range(first, end):
            low_h, high_h = window(h)
            at = (h - first) * count
            piece = part[at : at + count, low_h - low : high_h - low]
            hit = window_mask(h, low_h, high_h)
            out[:count, low_h:high_h] = jnp.where(hit, piece, out[:count, low_h:high_h])


def key_blocks(p, half, kv):
    blocks = [ref[...] for ref in kv]
    near = [cut(p, blocks[i], half * p.n1, p.n1) for i in range(p.g1 // 2)]
    wide = [cut(p, blocks[i], half * p.rows[2 * i] // 2, p.n2) for i in range(p.g2 // 2)]
    return jnp.concatenate(near, axis=0).astype(BF16), jnp.concatenate(wide, axis=0).astype(BF16)


def soft(scores):
    top = jnp.maximum(jnp.max(scores, axis=1, keepdims=True), LOWEST)
    e = jnp.exp2(scores - top)
    return top, e, jnp.sum(e, axis=1, keepdims=True)


def scores_kernel(p, q_own, q_other, *refs):
    kv, (p1, p2, lse) = refs[: p.g2 // 2], refs[p.g2 // 2 :]
    d = lax.axis_index("seq")
    n1, n2 = p.n1, p.n2
    k1, k2 = key_blocks(p, 0, kv)
    q1 = both_cores(p, q_own[...], q_other[...], n1)
    q2 = both_cores(p, q_own[...], q_other[...], n2)

    row = iota((2 * p.heads * n1, 1), 0)
    col = iota((1, p.g1 // 2 * n1), 1)
    head = first_head(p) + row // (2 * n1)
    own = row % n1
    device = jnp.bitwise_xor(d, row // n1 % 2)
    qpos = p.tokens * device + p.r2 * (own % n2) + (head + DIL1 * (own // n2)) % p.r2
    other = col % n1
    kbase = p.tokens * jnp.bitwise_xor(d, 2 * (col // n1)) + p.r2 * (other % n2)
    kpos = kbase + jnp.bitwise_and(head + DIL1 * (other // n2), p.r2 - 1)
    s1 = jnp.where(kpos <= qpos, against(p, q1, k1) * SCALE2, -jnp.inf)
    top1, e1, sum1 = soft(s1)

    row2 = iota((2 * p.heads * n2, 1), 0)
    row2 = jnp.bitwise_xor(d, row2 // n2 % 2) * n2 + row2 % n2
    col2 = iota((1, p.g2 // 2 * n2), 1)
    col2 = jnp.bitwise_xor(d, 2 * (col2 // n2)) * n2 + col2 % n2
    s2 = jnp.where(col2 <= row2, against(p, q2, k2) * SCALE2, -jnp.inf)
    top2, e2, sum2 = soft(s2)

    top2_all, sum2_all = widen(p, top2, LOWEST), widen(p, sum2, 0.0)
    peak = jnp.maximum(top1, top2_all)
    both = sum1 * jnp.exp2(top1 - peak) + sum2_all * jnp.exp2(top2_all - peak)
    part = peak + jnp.log2(jnp.maximum(both, TINY))
    p1[...] = e1 * jnp.exp2(top1 - part)
    p2[...] = e2 * jnp.exp2(top2 - wide_rows(p, part))
    lse[...] = to_lanes(p, part)


def delta_kernel(p, g_own, g_other, p1, p2, lse, lse01, d01, *refs):
    kv, (dp1, dp2, stats) = refs[: p.g2 // 2], refs[p.g2 // 2 :]
    n1 = p.n1
    v1, v2 = key_blocks(p, 1, kv)
    dp = against(p, both_cores(p, g_own[...], g_other[...], n1), v1)
    dp1[...] = dp
    d = jnp.sum(p1[...] * dp, axis=1, keepdims=True)
    dp = against(p, both_cores(p, g_own[...], g_other[...], p.n2), v2)
    dp2[...] = dp
    d += widen(p, jnp.sum(p2[...] * dp, axis=1, keepdims=True), 0.0)
    d = to_lanes(p, d)
    part = lse[:n1, :]
    total, delta = join(lse01[...], d01[...], part, d[:n1])
    stats[...] = jnp.concatenate([total, delta, lse[n1:, :], d[n1:]], axis=0)


def join(lse_a, d_a, lse_b, d_b):
    peak = jnp.maximum(lse_a, lse_b)
    total = peak + jnp.log2(jnp.exp2(lse_a - peak) + jnp.exp2(lse_b - peak))
    return total, jnp.exp2(lse_a - total) * d_a + jnp.exp2(lse_b - total) * d_b


def levels_kernel(p, q_own, q_other, g_own, g_other, p1, p2, dp1, dp2, lse, mine, theirs, *refs):
    kv, refs = refs[: p.g2 // 2], refs[p.g2 // 2 :]
    dq_own, dq_other, total1, delta1, own_part = refs[:5]
    outs, (dk1, dv1, dk2, dv2, dq1, dq2) = refs[5:-6], refs[-6:]
    n1, n2 = p.n1, p.n2
    quarter = lambda ref, i: ref[i * n1 : (i + 1) * n1, :]
    first = join(quarter(mine, 0), quarter(mine, 1), quarter(theirs, 2), quarter(theirs, 3))
    second = join(quarter(theirs, 0), quarter(theirs, 1), quarter(mine, 2), quarter(mine, 3))
    total1[...], delta1[...] = first
    total = jnp.concatenate([first[0], second[0]], axis=0)
    share = columns(p, jnp.exp2(lse[...] - total))
    delta = columns(p, jnp.concatenate([first[1], second[1]], axis=0))
    k1, k2 = key_blocks(p, 0, kv)
    for ref in (dk1, dv1, dk2, dv2):
        ref[...] = jnp.zeros_like(ref)

    prob = p1[...] * share
    ds = (prob * (dp1[...] - delta) * SCALE).astype(BF16)
    collect(p, prob.astype(BF16), both_cores(p, g_own[...], g_other[...], n1), dv1)
    collect(p, ds, both_cores(p, q_own[...], q_other[...], n1), dk1)
    prob2 = p2[...] * wide_rows(p, share)
    ds2 = (prob2 * (dp2[...] - wide_rows(p, delta)) * SCALE).astype(BF16)
    collect(p, prob2.astype(BF16), both_cores(p, g_own[...], g_other[...], n2), dv2)
    collect(p, ds2, both_cores(p, q_own[...], q_other[...], n2), dk2)
    for i in range(p.g2 // 2):
        rows = slice(i * n2, (i + 1) * n2)
        if 2 * i < p.g1:
            head = slice(i * n1, i * n1 + n2)
            rest = slice(i * n1 + n2, (i + 1) * n1)
            part = []
            for near, wide in ((dk1, dk2), (dv1, dv2)):
                part += [near[head, :] + wide[rows, :], near[rest, :]]
        else:
            part = [dk2[rows, :], dv2[rows, :]]
        part = jnp.concatenate(part, axis=0)
        ref = outs[i - 1] if i else own_part
        ref[...] = part.astype(ref.dtype)
    back(p, ds, k1, 2 * n1, dq1)
    back(p, ds2, k2, 2 * n2, dq2)
    for core, ref in enumerate((dq_own, dq_other)):
        near = dq1[core * n1 : (core + 1) * n1, :]
        near = jnp.concatenate([near[:n2] + dq2[core * n2 : (core + 1) * n2, :], near[n2:]], axis=0)
        ref[...] = near.astype(ref.dtype)


def own_grad_kernel(
    p, qp, kp, gp, weight, dprob, lse0, d0, total1, delta1, dq1, dq2, grad_q, dk0, dv0, dq
):
    label = lane_class(p)
    lse = lse0[...]
    share = jnp.exp2(lse - spread(p, total1[...], label, lse))
    delta = spread(p, delta1[...], label, d0[...])
    for ref in (dk0, dv0):
        ref[...] = jnp.zeros_like(ref)
    for h in range(p.heads):
        low, high = window(h)
        rows = slice(h * p.tokens, (h + 1) * p.tokens)
        hit = window_mask(h, low, high)
        mask = jnp.where(hit, 1.0, 0.0).astype(BF16)
        prob = weight[rows, :] * share[:, h : h + 1]
        ds = (prob * (dprob[rows, :] - delta[:, h : h + 1]) * SCALE).astype(BF16)
        dq[:, low:high] = jnp.where(hit, nn(ds, kp[:, low:high]), dq[:, low:high])
        dk0[:, low:high] += tn(ds, qp[:, low:high] * mask)
        dv0[:, low:high] += tn(prob.astype(BF16), gp[:, low:high] * mask)
    zero = jnp.zeros((p.tokens, p.width), F32)
    kept = dq1[...] + dq2[...].astype(F32)
    all_q = dq[...] + spread(p, kept, column_class(p), zero)
    grad_q[...] = nn(phase_order(p, True), all_q.astype(BF16)).astype(BF16)


def last_kernel(p, dk0, dv0, own, *refs):
    came, (grad_k, grad_v) = refs[:-2], refs[-2:]
    order = phase_order(p, True)
    label = column_class(p)
    zero = jnp.zeros((p.tokens, p.width), F32)
    sums = own[...]
    wide = []
    for ref, b in zip(came, range(2, p.g2, 2)):
        block = ref[...].astype(F32)
        if b < p.g1:
            sums = sums + block
        else:
            wide.append(block)
    for index, (base, grad) in enumerate(((dk0, grad_k), (dv0, grad_v))):
        kept = sums[index * p.n1 : (index + 1) * p.n1]
        if wide:
            first = kept[: p.n2]
            for block in wide:
                first = first + block[index * p.n2 : (index + 1) * p.n2]
            kept = jnp.concatenate([first, kept[p.n2 :]], axis=0)
        whole = base[...] + spread(p, kept, label, zero)
        grad[...] = nn(order, whole.astype(BF16)).astype(BF16)


def swap(block, axis, bits):
    count = lax.axis_size(axis)
    return lax.ppermute(block, axis, [(i, i ^ bits) for i in range(count)])


def body(queries, keys, values, grad_out):
    tokens, width = queries.shape
    queries, keys, values, grad_out = (
        pltpu.with_memory_space_constraint(field, pltpu.HBM)
        for field in (queries, keys, values, grad_out)
    )
    p = Plan(tokens, width, lax.axis_size("seq"), lax.axis_size("head"))
    n1, n2 = p.n1, p.n2
    run = lambda kernel: functools.partial(kernel, p)
    row, kept = (tokens, width), (n1, width)
    share = (tokens // p.zcount, width)
    stat, stat1 = (tokens, LANES), (n1, LANES)
    flat = lambda count: (count, tokens)
    even = range(0, p.g2, 2)
    half_rows = sum(p.rows[::2])
    hbm = pl.BlockSpec(memory_space=pltpu.HBM)

    outs = call(
        run(pack_kernel),
        [(row, BF16)] * 3
        + [(kept, BF16), ((2 * n1, width), BF16), ((2 * n2, width), BF16)]
        + [(share, BF16)] * p.zcount,
        [(row, BF16)] * 3 + [pltpu.SemaphoreType.DMA((p.zcount + 3,))],
        specs=[hbm] * 4,
    )(queries, keys, values, grad_out)
    qp, kp, vp, q1, kv1, kv2 = outs[:6]
    gz = outs[6:]
    gz = [gz[0]] + [swap(gz[b], "head", b) for b in range(1, p.zcount)]

    kv = [kv1] + [swap(kv1 if b < p.g1 else kv2, "seq", b) for b in even[1:]]

    weight, lse0, lse01 = call(
        run(own_scores_kernel), [(flat(p.heads * tokens), F32), (stat, F32), (stat1, F32)]
    )(qp, kp)
    q_other = swap(q1, "seq", 1)
    near = (2 * p.heads * n1, p.g1 // 2 * n1)
    wide = (2 * p.heads * n2, p.g2 // 2 * n2)
    p1, p2, lse = call(run(scores_kernel), [(near, F32), (wide, F32), ((2 * n1, LANES), F32)])(
        q1, q_other, *kv
    )
    gp, g1 = call(run(gather_kernel), [(row, BF16), (kept, BF16)], [(row, BF16)])(*gz)
    g_other = swap(g1, "seq", 1)
    dprob, d0, d01 = call(
        run(own_delta_kernel), [(flat(p.heads * tokens), F32), (stat, F32), (stat1, F32)]
    )(vp, weight, gp)
    dp1, dp2, mine = call(
        run(delta_kernel), [(near, F32), (wide, F32), ((4 * n1, LANES), F32)]
    )(g1, g_other, p1, p2, lse, lse01, d01, *kv)
    theirs = swap(mine, "seq", 1)
    part = lambda b, dtype: ((p.rows[b], width), dtype)
    outs = call(
        run(levels_kernel),
        [(kept, F32), (kept, BF16), (stat1, F32), (stat1, F32), part(0, F32)]
        + [part(b, BF16) for b in even[1:]],
        [((near[1], width), F32)] * 2
        + [((wide[1], width), F32)] * 2
        + [((2 * n1, width), F32), ((2 * n2, width), F32)],
    )(q1, q_other, g1, g_other, p1, p2, dp1, dp2, lse, mine, theirs, *kv)
    dq_own, dq_other, total1, delta1, own_part = outs[:5]
    parts = [swap(s, "seq", b) for s, b in zip(outs[5:], even[1:])]
    dq_came = swap(dq_other, "seq", 1)
    grad_q, dk0, dv0 = call(
        run(own_grad_kernel), [(row, BF16), (row, F32), (row, F32)], [(row, F32)]
    )(qp, kp, gp, weight, dprob, lse0, d0, total1, delta1, dq_own, dq_came)
    grad_k, grad_v = call(run(last_kernel), [(row, BF16)] * 2)(dk0, dv0, own_part, *parts)
    return grad_q, grad_k, grad_v


def solution(mesh):
    return jax.shard_map(
        body,
        mesh=mesh,
        in_specs=(P("seq", "head"), P("seq", "head"), P("seq", "head"), P(("seq", "head"), None)),
        out_specs=(P("seq", "head"), P("seq", "head"), P("seq", "head")),
        check_vma=False,
    )
```

```python
import functools
import math

import jax
import jax.numpy as jnp
from jax import lax
from jax.experimental import pallas as pl
from jax.experimental.pallas import tpu as pltpu
from jax.sharding import PartitionSpec as P

HD = 80
SPAN1 = 4
DIL1 = 4
WIDEST = 32
LANES = 128
BF16 = jnp.bfloat16
F32 = jnp.float32
SCALE = HD**-0.5
SCALE2 = SCALE * math.log2(math.e)
VMEM_BYTES = 28 * 2**20
LOWEST = -1e30
TINY = 1e-30


class Plan:
    def __init__(self, tokens, width, seq_count, head_count):
        self.tokens = tokens
        self.width = width
        self.heads = width // HD
        self.g1 = SPAN1
        self.g2 = min(WIDEST, seq_count)
        self.r2 = self.g2
        self.n1 = tokens // DIL1
        self.n2 = tokens // self.r2
        self.turns = self.r2 // DIL1
        self.zcount = head_count
        self.rows = [2 * (self.n1 if b < self.g1 else self.n2) for b in range(self.g2)]


def nt(a, b):
    return lax.dot_general(a, b, (((1,), (1,)), ((), ())), preferred_element_type=F32)


def nn(a, b):
    return lax.dot_general(a, b, (((1,), (0,)), ((), ())), preferred_element_type=F32)


def tn(a, b):
    return lax.dot_general(a, b, (((0,), (0,)), ((), ())), preferred_element_type=F32)


def iota(shape, dim):
    return lax.broadcasted_iota(jnp.int32, shape, dim)


def phase_order(p, inverse=False):
    shape = (p.tokens, p.tokens)
    row, col = (iota(shape, 1), iota(shape, 0)) if inverse else (iota(shape, 0), iota(shape, 1))
    return jnp.where(col == p.r2 * (row % p.n2) + row // p.n2, 1.0, 0.0).astype(BF16)


def first_head(p):
    return lax.axis_index("head") * p.heads


def column_class(p):
    return (first_head(p) + iota((1, p.width), 1) // HD) % p.r2


def lane_class(p):
    return (first_head(p) + iota((1, LANES), 1)) % p.r2


def pick(p, whole, label):
    parts = []
    for t in range(p.turns):
        want = (label + DIL1 * t) % p.r2
        part = jnp.zeros((p.n2, whole.shape[1]), F32)
        for c in range(p.r2):
            part = jnp.where(want == c, whole[c * p.n2 : (c + 1) * p.n2], part)
        parts.append(part)
    return jnp.concatenate(parts, axis=0)


def spread(p, kept, label, base):
    parts = []
    for c in range(p.r2):
        part = base[c * p.n2 : (c + 1) * p.n2]
        for t in range(p.turns):
            hit = (label + DIL1 * t) % p.r2 == c
            part = jnp.where(hit, kept[t * p.n2 : (t + 1) * p.n2], part)
        parts.append(part)
    return jnp.concatenate(parts, axis=0)


def window(h):
    low = h * HD // LANES * LANES
    high = -(-(h + 1) * HD // LANES) * LANES
    return low, high


def window_mask(h, low, high):
    lane = low + iota((1, high - low), 1)
    return (lane >= h * HD) & (lane < (h + 1) * HD)


def head_groups(p):
    groups, h = [], 0
    while h < p.heads:
        low, high = window(h)
        end = h + 1
        while end < p.heads and window(end)[1] - low <= 2 * LANES:
            high = window(end)[1]
            end += 1
        groups.append((h, end, low, high))
        h = end
    return groups


def head_mask(p, h):
    lane = iota((1, p.width), 1)
    return (lane >= h * HD) & (lane < (h + 1) * HD)


def own_bias(p):
    shape = (p.tokens, p.tokens)
    row, col = iota(shape, 0), iota(shape, 1)
    qpos = p.r2 * (row % p.n2) + row // p.n2
    kpos = p.r2 * (col % p.n2) + col // p.n2
    return jnp.where(qpos >= kpos, 0.0, -jnp.inf)


def call(kernel, outs, scratch=(), flops=0, **specs):
    return pl.pallas_call(
        kernel,
        out_shape=[jax.ShapeDtypeStruct(s, d) for s, d in outs],
        scratch_shapes=[pltpu.VMEM(*s) if isinstance(s, tuple) else s for s in scratch],
        compiler_params=pltpu.CompilerParams(vmem_limit_bytes=VMEM_BYTES),
        cost_estimate=pl.CostEstimate(flops=flops, bytes_accessed=2**20, transcendentals=0),
        **specs,
    )


def slab(p, g_ref, b):
    start = pl.multiple_of(jnp.bitwise_xor(lax.axis_index("head"), b) * p.width, LANES)
    return g_ref.at[:, pl.ds(start, p.width)]


def pack_kernel(p, q_ref, k_ref, v_ref, g_ref, qp, kp, vp, q1, kv1, kv2, *refs):
    gz, (q_in, k_in, v_in, sems) = refs[: p.zcount], refs[p.zcount :]
    loads = [(k_ref, k_in), (v_ref, v_in), (q_ref, q_in)]
    loads += [(slab(p, g_ref, b), gz[b]) for b in range(p.zcount)]
    copies = [pltpu.make_async_copy(src, dst, sems.at[i]) for i, (src, dst) in enumerate(loads)]
    for copy in copies:
        copy.start()
    order = phase_order(p)
    label = column_class(p)
    copies[0].wait()
    k = nn(order, k_in[...])
    kp[...] = k.astype(BF16)
    k_kept = pick(p, k, label)
    copies[1].wait()
    v = nn(order, v_in[...])
    vp[...] = v.astype(BF16)
    v_kept = pick(p, v, label)
    kv1[...] = jnp.concatenate([k_kept, v_kept], axis=0).astype(BF16)
    kv2[...] = jnp.concatenate([k_kept[: p.n2], v_kept[: p.n2]], axis=0).astype(BF16)
    copies[2].wait()
    q = nn(order, q_in[...])
    qp[...] = q.astype(BF16)
    q1[...] = pick(p, q, label).astype(BF16)
    for copy in copies[3:]:
        copy.wait()


def own_scores_kernel(p, qp, kp, after, weight, lse0, lse01):
    bias = own_bias(p)
    lane = iota((1, LANES), 1)
    lse_all = jnp.zeros((p.tokens, LANES), F32)
    for h in range(p.heads):
        low, high = window(h)
        mask = jnp.where(window_mask(h, low, high), 1.0, 0.0).astype(BF16)
        s = nt(qp[:, low:high] * mask, kp[:, low:high]) * SCALE2 + bias
        top = jnp.max(s, axis=1, keepdims=True)
        e = jnp.exp2(s - top)
        denom = jnp.sum(e, axis=1, keepdims=True)
        weight[h * p.tokens : (h + 1) * p.tokens, :] = e * (1.0 / denom)
        lse_all = jnp.where(lane == h, top + jnp.log2(denom), lse_all)
    lse0[...] = lse_all
    lse01[...] = pick(p, lse_all, lane_class(p))


def gather_kernel(p, after, *refs):
    gz, (gp, g1, natural) = refs[: p.zcount], refs[p.zcount :]
    z = lax.axis_index("head")
    share = p.tokens // p.zcount
    for b in range(p.zcount):
        start = pl.multiple_of(jnp.bitwise_xor(z, b) * share, share)
        natural[pl.ds(start, share), :] = gz[p.zcount - 1 - b][...]
    g = nn(phase_order(p), natural[...])
    gp[...] = g.astype(BF16)
    g1[...] = pick(p, g, column_class(p)).astype(BF16)


def own_delta_kernel(p, vp, weight, gp, dprob, d0, d01):
    lane = iota((1, LANES), 1)
    d_all = jnp.zeros((p.tokens, LANES), F32)
    for h in range(p.heads):
        low, high = window(h)
        rows = slice(h * p.tokens, (h + 1) * p.tokens)
        mask = jnp.where(window_mask(h, low, high), 1.0, 0.0).astype(BF16)
        dp = nt(gp[:, low:high] * mask, vp[:, low:high])
        dprob[rows, :] = dp
        d = jnp.sum(weight[rows, :] * dp, axis=1, keepdims=True)
        d_all = jnp.where(lane == h, d, d_all)
    d0[...] = d_all
    d01[...] = pick(p, d_all, lane_class(p))


def columns(p, stat):
    return jnp.concatenate([stat[:, h : h + 1] for h in range(p.heads)], axis=0)


def to_lanes(p, column, count):
    lane = iota((1, LANES), 1)
    out = jnp.zeros((2 * count, LANES), F32)
    for h in range(p.heads):
        out = jnp.where(lane == h, column[2 * h * count : 2 * (h + 1) * count], out)
    return out


def wide_rows(p, stat):
    return jnp.concatenate([stat[: p.n2], stat[p.n1 : p.n1 + p.n2]], axis=0)


def widen(p, stat, fill):
    rest = jnp.full((p.n1 - p.n2, LANES), fill, F32)
    return jnp.concatenate([stat[: p.n2], rest, stat[p.n2 :], rest], axis=0)


def cut(p, block, start, count):
    if start % 16 or count % 16:
        block = block.astype(F32)
    return block[start : start + count]


def both_cores(p, own, other, count):
    return jnp.concatenate([cut(p, own, 0, count), cut(p, other, 0, count)], axis=0)


def by_head(p, rows, group):
    first, end, low, high = group
    parts = []
    for h in range(first, end):
        mask = jnp.where(window_mask(h, low, high), 1.0, 0.0).astype(rows.dtype)
        parts.append(rows[:, low:high] * mask)
    return jnp.concatenate(parts, axis=0).astype(BF16)


def against(p, rows, cols):
    parts = []
    for group in head_groups(p):
        low, high = group[2:]
        parts.append(nt(by_head(p, rows, group), cols[:, low:high]))
    return jnp.concatenate(parts, axis=0)


def collect(p, weights, rows, out):
    count = rows.shape[0]
    for group in head_groups(p):
        first, end, low, high = group
        part = tn(weights[first * count : end * count], by_head(p, rows, group))
        out[:, low:high] += part


def back(p, weights, cols, count, out):
    for first, end, low, high in head_groups(p):
        part = nn(weights[first * count : end * count], cols[:, low:high])
        for h in range(first, end):
            low_h, high_h = window(h)
            at = (h - first) * count
            piece = part[at : at + count, low_h - low : high_h - low]
            hit = window_mask(h, low_h, high_h)
            out[:count, low_h:high_h] = jnp.where(hit, piece, out[:count, low_h:high_h])


def near_blocks(p, half, kv):
    blocks = [cut(p, ref[...], half * p.n1, p.n1) for ref in kv[: p.g1 // 2]]
    return jnp.concatenate(blocks, axis=0).astype(BF16)


def wide_blocks(p, half, kv):
    blocks = [cut(p, ref[...], half * ref.shape[0] // 2, p.n2) for ref in kv]
    return jnp.concatenate(blocks, axis=0).astype(BF16)


def soft(p, scores, count, e, tops, sums):
    top = jnp.maximum(jnp.max(scores, axis=1, keepdims=True), LOWEST)
    weight = jnp.exp2(scores - top)
    e[...] = weight
    tops[...] = to_lanes(p, top, count)
    sums[...] = to_lanes(p, jnp.sum(weight, axis=1, keepdims=True), count)


def near_kernel(p, q_own, q_other, *refs):
    kv, outs = refs[: p.g1 // 2], refs[p.g1 // 2 :]
    d = lax.axis_index("seq")
    n1, n2 = p.n1, p.n2
    q = both_cores(p, q_own[...], q_other[...], n1)
    row = iota((2 * p.heads * n1, 1), 0)
    col = iota((1, p.g1 // 2 * n1), 1)
    head = first_head(p) + row // (2 * n1)
    own = row % n1
    device = jnp.bitwise_xor(d, row // n1 % 2)
    qpos = p.tokens * device + p.r2 * (own % n2) + (head + DIL1 * (own // n2)) % p.r2
    other = col % n1
    kbase = p.tokens * jnp.bitwise_xor(d, 2 * (col // n1)) + p.r2 * (other % n2)
    kpos = kbase + jnp.bitwise_and(head + DIL1 * (other // n2), p.r2 - 1)
    s = jnp.where(kpos <= qpos, against(p, q, near_blocks(p, 0, kv)) * SCALE2, -jnp.inf)
    soft(p, s, n1, *outs)


def wide_kernel(p, q_own, q_other, *refs):
    kv, outs = refs[: p.g2 // 2], refs[p.g2 // 2 :]
    d = lax.axis_index("seq")
    n2 = p.n2
    q = both_cores(p, q_own[...], q_other[...], n2)
    row = iota((2 * p.heads * n2, 1), 0)
    row = jnp.bitwise_xor(d, row // n2 % 2) * n2 + row % n2
    col = iota((1, p.g2 // 2 * n2), 1)
    col = jnp.bitwise_xor(d, 2 * (col // n2)) * n2 + col % n2
    s = jnp.where(col <= row, against(p, q, wide_blocks(p, 0, kv)) * SCALE2, -jnp.inf)
    soft(p, s, n2, *outs)


def delta_kernel(p, g_own, g_other, e1, e2, top1, sum1, top2, sum2, lse01, d01, *refs):
    kv, (dp1, dp2, stats) = refs[: p.g2 // 2], refs[p.g2 // 2 :]
    n1, n2 = p.n1, p.n2
    dp = against(p, both_cores(p, g_own[...], g_other[...], n1), near_blocks(p, 1, kv))
    dp1[...] = dp
    near = to_lanes(p, jnp.sum(e1[...] * dp, axis=1, keepdims=True), n1)
    dp = against(p, both_cores(p, g_own[...], g_other[...], n2), wide_blocks(p, 1, kv))
    dp2[...] = dp
    wide = to_lanes(p, jnp.sum(e2[...] * dp, axis=1, keepdims=True), n2)

    top1, top2 = top1[...], widen(p, top2[...], LOWEST)
    peak = jnp.maximum(top1, top2)
    up1, up2 = jnp.exp2(top1 - peak), jnp.exp2(top2 - peak)
    both = jnp.maximum(sum1[...] * up1 + widen(p, sum2[...], 0.0) * up2, TINY)
    lse = peak + jnp.log2(both)
    d = (near * up1 + widen(p, wide, 0.0) * up2) / both
    total, delta = join(lse01[...], d01[...], lse[:n1], d[:n1])
    stats[...] = jnp.concatenate([total, delta, lse[n1:], d[n1:]], axis=0)


def join(lse_a, d_a, lse_b, d_b):
    peak = jnp.maximum(lse_a, lse_b)
    total = peak + jnp.log2(jnp.exp2(lse_a - peak) + jnp.exp2(lse_b - peak))
    return total, jnp.exp2(lse_a - total) * d_a + jnp.exp2(lse_b - total) * d_b


def levels_kernel(
    p, q_own, q_other, g_own, g_other, e1, e2, top1, top2, dp1, dp2, mine, theirs, *refs
):
    kv, refs = refs[: p.g2 // 2], refs[p.g2 // 2 :]
    dq_own, dq_other, total1, delta1, own_part = refs[:5]
    outs, (dk1, dv1, dk2, dv2, dq1, dq2) = refs[5:-6], refs[-6:]
    n1, n2 = p.n1, p.n2
    quarter = lambda ref, i: ref[i * n1 : (i + 1) * n1, :]
    first = join(quarter(mine, 0), quarter(mine, 1), quarter(theirs, 2), quarter(theirs, 3))
    second = join(quarter(theirs, 0), quarter(theirs, 1), quarter(mine, 2), quarter(mine, 3))
    total1[...], delta1[...] = first
    total = jnp.concatenate([first[0], second[0]], axis=0)
    delta = jnp.concatenate([first[1], second[1]], axis=0)
    k1, k2 = near_blocks(p, 0, kv), wide_blocks(p, 0, kv)
    for ref in (dk1, dv1, dk2, dv2):
        ref[...] = jnp.zeros_like(ref)

    prob = e1[...] * columns(p, jnp.exp2(top1[...] - total))
    ds = (prob * (dp1[...] - columns(p, delta)) * SCALE).astype(BF16)
    collect(p, prob.astype(BF16), both_cores(p, g_own[...], g_other[...], n1), dv1)
    collect(p, ds, both_cores(p, q_own[...], q_other[...], n1), dk1)
    prob2 = e2[...] * columns(p, jnp.exp2(top2[...] - wide_rows(p, total)))
    ds2 = (prob2 * (dp2[...] - columns(p, wide_rows(p, delta))) * SCALE).astype(BF16)
    collect(p, prob2.astype(BF16), both_cores(p, g_own[...], g_other[...], n2), dv2)
    collect(p, ds2, both_cores(p, q_own[...], q_other[...], n2), dk2)
    for i in range(p.g2 // 2):
        rows = slice(i * n2, (i + 1) * n2)
        if 2 * i < p.g1:
            head = slice(i * n1, i * n1 + n2)
            rest = slice(i * n1 + n2, (i + 1) * n1)
            part = []
            for near, wide in ((dk1, dk2), (dv1, dv2)):
                part += [near[head, :] + wide[rows, :], near[rest, :]]
        else:
            part = [dk2[rows, :], dv2[rows, :]]
        part = jnp.concatenate(part, axis=0)
        ref = outs[i - 1] if i else own_part
        ref[...] = part.astype(ref.dtype)
    back(p, ds, k1, 2 * n1, dq1)
    back(p, ds2, k2, 2 * n2, dq2)
    for core, ref in enumerate((dq_own, dq_other)):
        near = dq1[core * n1 : (core + 1) * n1, :]
        near = jnp.concatenate([near[:n2] + dq2[core * n2 : (core + 1) * n2, :], near[n2:]], axis=0)
        ref[...] = near.astype(ref.dtype)


def own_grad_kernel(
    p, qp, kp, gp, weight, dprob, lse0, d0, total1, delta1, dq1, dq2, grad_q, dk0, dv0, dq
):
    label = lane_class(p)
    lse = lse0[...]
    share = jnp.exp2(lse - spread(p, total1[...], label, lse))
    delta = spread(p, delta1[...], label, d0[...])
    for ref in (dk0, dv0):
        ref[...] = jnp.zeros_like(ref)
    for h in range(p.heads):
        low, high = window(h)
        rows = slice(h * p.tokens, (h + 1) * p.tokens)
        hit = window_mask(h, low, high)
        mask = jnp.where(hit, 1.0, 0.0).astype(BF16)
        prob = weight[rows, :] * share[:, h : h + 1]
        ds = (prob * (dprob[rows, :] - delta[:, h : h + 1]) * SCALE).astype(BF16)
        dq[:, low:high] = jnp.where(hit, nn(ds, kp[:, low:high]), dq[:, low:high])
        dk0[:, low:high] += tn(ds, qp[:, low:high] * mask)
        dv0[:, low:high] += tn(prob.astype(BF16), gp[:, low:high] * mask)
    zero = jnp.zeros((p.tokens, p.width), F32)
    kept = dq1[...] + dq2[...].astype(F32)
    all_q = dq[...] + spread(p, kept, column_class(p), zero)
    grad_q[...] = nn(phase_order(p, True), all_q.astype(BF16)).astype(BF16)


def last_kernel(p, dk0, dv0, own, *refs):
    came, (grad_k, grad_v, out_k, out_v, sems) = refs[:-5], refs[-5:]
    order = phase_order(p, True)
    label = column_class(p)
    zero = jnp.zeros((p.tokens, p.width), F32)
    copies = []
    for index, (base, out, grad) in enumerate(((dk0, out_k, grad_k), (dv0, out_v, grad_v))):
        first = own[index * p.n1 : index * p.n1 + p.n2, :]
        rest = own[index * p.n1 + p.n2 : (index + 1) * p.n1, :]
        for ref in came:
            half = ref.shape[0] // 2
            block = ref[...].astype(F32)
            first = first + block[index * half : index * half + p.n2]
            if half == p.n1:
                rest = rest + block[index * half + p.n2 : (index + 1) * half]
        kept = jnp.concatenate([first, rest], axis=0)
        whole = base[...] + spread(p, kept, label, zero)
        out[...] = nn(order, whole.astype(BF16)).astype(BF16)
        copies.append(pltpu.make_async_copy(out, grad, sems.at[index]))
        copies[-1].start()
    for copy in copies:
        copy.wait()


def swap(block, axis, bits):
    count = lax.axis_size(axis)
    return lax.ppermute(block, axis, [(i, i ^ bits) for i in range(count)])


def body(queries, keys, values, grad_out):
    tokens, width = queries.shape
    queries, keys, values, grad_out = (
        pltpu.with_memory_space_constraint(field, pltpu.HBM)
        for field in (queries, keys, values, grad_out)
    )
    p = Plan(tokens, width, lax.axis_size("seq"), lax.axis_size("head"))
    n1, n2 = p.n1, p.n2
    run = lambda kernel: functools.partial(kernel, p)
    row, kept = (tokens, width), (n1, width)
    share = (tokens // p.zcount, width)
    stat, stat1 = (tokens, LANES), (n1, LANES)
    flat = lambda count: (count, tokens)
    even = range(0, p.g2, 2)
    half_rows = sum(p.rows[::2])
    hbm = pl.BlockSpec(memory_space=pltpu.HBM)

    outs = call(
        run(pack_kernel),
        [(row, BF16)] * 3
        + [(kept, BF16), ((2 * n1, width), BF16), ((2 * n2, width), BF16)]
        + [(share, BF16)] * p.zcount,
        [(row, BF16)] * 3 + [pltpu.SemaphoreType.DMA((p.zcount + 3,))],
        in_specs=[hbm] * 4,
    )(queries, keys, values, grad_out)
    qp, kp, vp, q1, kv1, kv2 = outs[:6]
    gz = outs[6:]
    gz = [gz[0]] + [swap(gz[b], "head", b) for b in range(1, p.zcount)]

    kv = [kv1] + [swap(kv1 if b < p.g1 else kv2, "seq", b) for b in even[1:]]

    q_other = swap(q1, "seq", 1)
    weight, lse0, lse01 = call(
        run(own_scores_kernel), [(flat(p.heads * tokens), F32), (stat, F32), (stat1, F32)]
    )(qp, kp, q_other)
    near = (2 * p.heads * n1, p.g1 // 2 * n1)
    wide = (2 * p.heads * n2, p.g2 // 2 * n2)
    e1, top1, sum1 = call(run(near_kernel), [(near, F32)] + [((2 * n1, LANES), F32)] * 2)(
        q1, q_other, *kv[: p.g1 // 2]
    )
    e2, top2, sum2 = call(run(wide_kernel), [(wide, F32)] + [((2 * n2, LANES), F32)] * 2)(
        q1, q_other, *kv
    )
    gp, g1 = call(run(gather_kernel), [(row, BF16), (kept, BF16)], [(row, BF16)])(
        lse01, *gz[::-1]
    )
    g_other = swap(g1, "seq", 1)
    dprob, d0, d01 = call(
        run(own_delta_kernel), [(flat(p.heads * tokens), F32), (stat, F32), (stat1, F32)]
    )(vp, weight, gp)
    dp1, dp2, mine = call(
        run(delta_kernel), [(near, F32), (wide, F32), ((4 * n1, LANES), F32)]
    )(g1, g_other, e1, e2, top1, sum1, top2, sum2, lse01, d01, *kv)
    theirs = swap(mine, "seq", 1)
    part = lambda b, dtype: ((p.rows[b], width), dtype)
    outs = call(
        run(levels_kernel),
        [(kept, F32), (kept, BF16), (stat1, F32), (stat1, F32), part(0, F32)]
        + [part(b, BF16) for b in even[1:]],
        [((near[1], width), F32)] * 2
        + [((wide[1], width), F32)] * 2
        + [((2 * n1, width), F32), ((2 * n2, width), F32)],
    )(q1, q_other, g1, g_other, e1, e2, top1, top2, dp1, dp2, mine, theirs, *kv)
    dq_own, dq_other, total1, delta1, own_part = outs[:5]
    parts = [swap(s, "seq", b) for s, b in zip(outs[5:], even[1:])]
    dq_came = swap(dq_other, "seq", 1)
    grad_q, dk0, dv0 = call(
        run(own_grad_kernel), [(row, BF16), (row, F32), (row, F32)], [(row, F32)]
    )(qp, kp, gp, weight, dprob, lse0, d0, total1, delta1, dq_own, dq_came)
    grad_k, grad_v = call(
        run(last_kernel),
        [(row, BF16)] * 2,
        [(row, BF16)] * 2 + [pltpu.SemaphoreType.DMA((2,))],
        out_specs=[hbm] * 2,
    )(dk0, dv0, own_part, *parts)
    return grad_q, grad_k, grad_v


def solution(mesh):
    return jax.shard_map(
        body,
        mesh=mesh,
        in_specs=(P("seq", "head"), P("seq", "head"), P("seq", "head"), P(("seq", "head"), None)),
        out_specs=(P("seq", "head"), P("seq", "head"), P("seq", "head")),
        check_vma=False,
    )
```

```python
import functools
import math

import jax
import jax.numpy as jnp
from jax import lax
from jax.experimental import pallas as pl
from jax.experimental.pallas import tpu as pltpu
from jax.sharding import PartitionSpec as P

HD = 80
SPAN1 = 4
DIL1 = 4
WIDEST = 32
LANES = 128
BF16 = jnp.bfloat16
F32 = jnp.float32
SCALE = HD**-0.5
SCALE2 = SCALE * math.log2(math.e)
VMEM_BYTES = 28 * 2**20
LOWEST = -1e30
TINY = 1e-30


class Plan:
    def __init__(self, tokens, width, seq_count, head_count):
        self.tokens = tokens
        self.width = width
        self.heads = width // HD
        self.g1 = SPAN1
        self.g2 = min(WIDEST, seq_count)
        self.r2 = self.g2
        self.n1 = tokens // DIL1
        self.n2 = tokens // self.r2
        self.turns = self.r2 // DIL1
        self.zcount = head_count
        self.rows = [2 * (self.n1 if b < self.g1 else self.n2) for b in range(self.g2)]


def nt(a, b):
    return lax.dot_general(a, b, (((1,), (1,)), ((), ())), preferred_element_type=F32)


def nn(a, b):
    return lax.dot_general(a, b, (((1,), (0,)), ((), ())), preferred_element_type=F32)


def tn(a, b):
    return lax.dot_general(a, b, (((0,), (0,)), ((), ())), preferred_element_type=F32)


def iota(shape, dim):
    return lax.broadcasted_iota(jnp.int32, shape, dim)


def phase_order(p, inverse=False):
    shape = (p.tokens, p.tokens)
    row, col = (iota(shape, 1), iota(shape, 0)) if inverse else (iota(shape, 0), iota(shape, 1))
    return jnp.where(col == p.r2 * (row % p.n2) + row // p.n2, 1.0, 0.0).astype(BF16)


def first_head(p):
    return lax.axis_index("head") * p.heads


def column_class(p):
    return (first_head(p) + iota((1, p.width), 1) // HD) % p.r2


def row_class(p):
    return (first_head(p) + iota((p.heads, 1), 0)) % p.r2


def pick(p, whole, label):
    parts = []
    for t in range(p.turns):
        want = (label + DIL1 * t) % p.r2
        part = jnp.zeros((p.n2, whole.shape[1]), F32)
        for c in range(p.r2):
            part = jnp.where(want == c, whole[c * p.n2 : (c + 1) * p.n2], part)
        parts.append(part)
    return jnp.concatenate(parts, axis=0)


def spread(p, kept, label, base):
    parts = []
    for c in range(p.r2):
        part = base[c * p.n2 : (c + 1) * p.n2]
        for t in range(p.turns):
            hit = (label + DIL1 * t) % p.r2 == c
            part = jnp.where(hit, kept[t * p.n2 : (t + 1) * p.n2], part)
        parts.append(part)
    return jnp.concatenate(parts, axis=0)


def window(h):
    low = h * HD // LANES * LANES
    high = -(-(h + 1) * HD // LANES) * LANES
    return low, high


def window_mask(h, low, high):
    lane = low + iota((1, high - low), 1)
    return (lane >= h * HD) & (lane < (h + 1) * HD)


def head_groups(p):
    groups, h = [], 0
    while h < p.heads:
        low, high = window(h)
        end = h + 1
        while end < p.heads and window(end)[1] - low <= 2 * LANES:
            high = window(end)[1]
            end += 1
        groups.append((h, end, low, high))
        h = end
    return groups


def head_mask(p, h):
    lane = iota((1, p.width), 1)
    return (lane >= h * HD) & (lane < (h + 1) * HD)


def own_bias(p):
    shape = (p.tokens, p.tokens)
    key, query = iota(shape, 0), iota(shape, 1)
    qpos = p.r2 * (query % p.n2) + query // p.n2
    kpos = p.r2 * (key % p.n2) + key // p.n2
    return jnp.where(qpos >= kpos, 0.0, -jnp.inf)


def pick_stat(p, stat, fill):
    lane = iota((1, 2 * p.n1), 1)
    label = row_class(p)
    out = jnp.full((p.heads, 2 * p.n1), fill, F32)
    for t in range(p.turns):
        here = (lane >= t * p.n2) & (lane < (t + 1) * p.n2)
        for c in range(p.r2):
            moved = pltpu.roll(stat, (t - c) * p.n2 % p.tokens, 1)[:, : 2 * p.n1]
            out = jnp.where(here & ((label + DIL1 * t) % p.r2 == c), moved, out)
    return out


def spread_stat(p, kept, base):
    lane = iota((1, p.tokens), 1)
    label = row_class(p)
    padded = jnp.concatenate([kept] * (p.tokens // kept.shape[1]), axis=1)
    out = base
    for t in range(p.turns):
        for c in range(p.r2):
            moved = pltpu.roll(padded, (c - t) * p.n2 % p.tokens, 1)
            here = (lane >= c * p.n2) & (lane < (c + 1) * p.n2)
            out = jnp.where(here & ((label + DIL1 * t) % p.r2 == c), moved, out)
    return out


def by_rows(p, flat):
    count = flat.shape[1] // p.heads
    return jnp.concatenate([flat[:, h * count : (h + 1) * count] for h in range(p.heads)], axis=0)


def along(p, stat):
    return jnp.concatenate([stat[h : h + 1, :] for h in range(p.heads)], axis=1)


def call(kernel, outs, scratch=(), flops=0, **specs):
    return pl.pallas_call(
        kernel,
        out_shape=[jax.ShapeDtypeStruct(s, d) for s, d in outs],
        scratch_shapes=[pltpu.VMEM(*s) if isinstance(s, tuple) else s for s in scratch],
        compiler_params=pltpu.CompilerParams(vmem_limit_bytes=VMEM_BYTES),
        cost_estimate=pl.CostEstimate(flops=flops, bytes_accessed=2**20, transcendentals=0),
        **specs,
    )


def slab(p, g_ref, b):
    start = pl.multiple_of(jnp.bitwise_xor(lax.axis_index("head"), b) * p.width, LANES)
    return g_ref.at[:, pl.ds(start, p.width)]


def pack_kernel(p, q_ref, k_ref, v_ref, g_ref, qp, kp, vp, q1, kv1, kv2, *refs):
    gz, (q_in, k_in, v_in, sems) = refs[: p.zcount], refs[p.zcount :]
    loads = [(k_ref, k_in), (v_ref, v_in), (q_ref, q_in)]
    loads += [(slab(p, g_ref, b), gz[b]) for b in range(p.zcount)]
    copies = [pltpu.make_async_copy(src, dst, sems.at[i]) for i, (src, dst) in enumerate(loads)]
    for copy in copies:
        copy.start()
    order = phase_order(p)
    label = column_class(p)
    copies[0].wait()
    k = nn(order, k_in[...])
    kp[...] = k.astype(BF16)
    k_kept = pick(p, k, label)
    copies[1].wait()
    v = nn(order, v_in[...])
    vp[...] = v.astype(BF16)
    v_kept = pick(p, v, label)
    kv1[...] = jnp.concatenate([k_kept, v_kept], axis=0).astype(BF16)
    kv2[...] = jnp.concatenate([k_kept[: p.n2], v_kept[: p.n2]], axis=0).astype(BF16)
    copies[2].wait()
    q = nn(order, q_in[...])
    qp[...] = q.astype(BF16)
    q1[...] = pick(p, q, label).astype(BF16)
    for copy in copies[3:]:
        copy.wait()


def own_scores_kernel(p, qp, kp, after, weight, lse0, lse01):
    bias = own_bias(p)
    rows = []
    for h in range(p.heads):
        low, high = window(h)
        mask = jnp.where(window_mask(h, low, high), 1.0, 0.0).astype(BF16)
        s = nt(kp[:, low:high], qp[:, low:high] * mask) * SCALE2 + bias
        top = jnp.max(s, axis=0, keepdims=True)
        e = jnp.exp2(s - top)
        denom = jnp.sum(e, axis=0, keepdims=True)
        weight[h * p.tokens : (h + 1) * p.tokens, :] = e * (1.0 / denom)
        rows.append(top + jnp.log2(denom))
    lse = jnp.concatenate(rows, axis=0)
    lse0[...] = lse
    lse01[...] = pick_stat(p, lse, LOWEST)


def gather_kernel(p, after, *refs):
    gz, (gp, g1, natural) = refs[: p.zcount], refs[p.zcount :]
    z = lax.axis_index("head")
    share = p.tokens // p.zcount
    for b in range(p.zcount):
        start = pl.multiple_of(jnp.bitwise_xor(z, b) * share, share)
        natural[pl.ds(start, share), :] = gz[p.zcount - 1 - b][...]
    g = nn(phase_order(p), natural[...])
    gp[...] = g.astype(BF16)
    g1[...] = pick(p, g, column_class(p)).astype(BF16)


def own_delta_kernel(p, vp, weight, gp, dprob, d0, d01):
    sums = []
    for h in range(p.heads):
        low, high = window(h)
        rows = slice(h * p.tokens, (h + 1) * p.tokens)
        mask = jnp.where(window_mask(h, low, high), 1.0, 0.0).astype(BF16)
        dp = nt(vp[:, low:high], gp[:, low:high] * mask)
        dprob[rows, :] = dp
        sums.append(jnp.sum(weight[rows, :] * dp, axis=0, keepdims=True))
    d = jnp.concatenate(sums, axis=0)
    d0[...] = d
    d01[...] = pick_stat(p, d, 0.0)


def cut(p, block, start, count):
    if start % 16 or count % 16:
        block = block.astype(F32)
    return block[start : start + count]


def both_cores(own, other):
    return jnp.concatenate([own[...], other[...]], axis=0)


def by_head(rows, group):
    first, end, low, high = group
    parts = []
    for h in range(first, end):
        mask = jnp.where(window_mask(h, low, high), 1.0, 0.0).astype(BF16)
        parts.append(rows[:, low:high] * mask)
    return jnp.concatenate(parts, axis=0)


def against(p, cols, rows):
    parts = []
    for group in head_groups(p):
        low, high = group[2:]
        parts.append(nt(cols[:, low:high], by_head(rows, group)))
    return jnp.concatenate(parts, axis=1)


def collect(p, weights, rows, out):
    count = rows.shape[0]
    for group in head_groups(p):
        first, end, low, high = group
        part = nn(weights[:, first * count : end * count], by_head(rows, group))
        out[:, low:high] += part


def near_blocks(p, half, kv):
    blocks = [cut(p, ref[...], half * p.n1, p.n1) for ref in kv[: p.g1 // 2]]
    return jnp.concatenate(blocks, axis=0).astype(BF16)


def wide_blocks(p, half, kv):
    blocks = [cut(p, ref[...], half * ref.shape[0] // 2, p.n2) for ref in kv]
    return jnp.concatenate(blocks, axis=0).astype(BF16)


def soft(p, scores, e, tops, sums):
    top = jnp.maximum(jnp.max(scores, axis=0, keepdims=True), LOWEST)
    weight = jnp.exp2(scores - top)
    e[...] = weight
    tops[...] = by_rows(p, top)
    sums[...] = by_rows(p, jnp.sum(weight, axis=0, keepdims=True))


def near_kernel(p, q_own, q_other, *refs):
    kv, outs = refs[: p.g1 // 2], refs[p.g1 // 2 :]
    d = lax.axis_index("seq")
    n1, n2 = p.n1, p.n2
    row = iota((p.g1 // 2 * n1, 1), 0)
    col = iota((1, 2 * p.heads * n1), 1)
    head = first_head(p) + col // (2 * n1)
    own = col % n1
    device = jnp.bitwise_xor(d, col // n1 % 2)
    qpos = p.tokens * device + p.r2 * (own % n2) + (head + DIL1 * (own // n2)) % p.r2
    other = row % n1
    kbase = p.tokens * jnp.bitwise_xor(d, 2 * (row // n1)) + p.r2 * (other % n2)
    kpos = kbase + jnp.bitwise_and(head + DIL1 * (other // n2), p.r2 - 1)
    s = against(p, near_blocks(p, 0, kv), both_cores(q_own, q_other)) * SCALE2
    soft(p, jnp.where(kpos <= qpos, s, -jnp.inf), *outs)


def wide_kernel(p, q_own, q_other, *refs):
    kv, outs = refs[: p.g2 // 2], refs[p.g2 // 2 :]
    d = lax.axis_index("seq")
    n1, n2 = p.n1, p.n2
    row = iota((p.g2 // 2 * n2, 1), 0)
    row = jnp.bitwise_xor(d, 2 * (row // n2)) * n2 + row % n2
    col = iota((1, 2 * p.heads * n1), 1)
    last = jnp.bitwise_xor(d, col // n1 % 2) * n2 + col % n1
    last = jnp.where(col % n1 < n2, last, -1)
    s = against(p, wide_blocks(p, 0, kv), both_cores(q_own, q_other)) * SCALE2
    soft(p, jnp.where(row <= last, s, -jnp.inf), *outs)


def delta_kernel(p, g_own, g_other, e1, e2, top1, sum1, top2, sum2, lse01, d01, *refs):
    kv, (dp1, dp2, stats) = refs[: p.g2 // 2], refs[p.g2 // 2 :]
    g = both_cores(g_own, g_other)
    dp = against(p, near_blocks(p, 1, kv), g)
    dp1[...] = dp
    near = by_rows(p, jnp.sum(e1[...] * dp, axis=0, keepdims=True))
    dp = against(p, wide_blocks(p, 1, kv), g)
    dp2[...] = dp
    wide = by_rows(p, jnp.sum(e2[...] * dp, axis=0, keepdims=True))

    peak = jnp.maximum(top1[...], top2[...])
    up1, up2 = jnp.exp2(top1[...] - peak), jnp.exp2(top2[...] - peak)
    both = jnp.maximum(sum1[...] * up1 + sum2[...] * up2, TINY)
    d = (near * up1 + wide * up2) / both
    total, delta = join(lse01[...], d01[...], peak + jnp.log2(both), d)
    stats[...] = jnp.concatenate([total, delta], axis=0)


def join(lse_a, d_a, lse_b, d_b):
    peak = jnp.maximum(lse_a, lse_b)
    total = peak + jnp.log2(jnp.exp2(lse_a - peak) + jnp.exp2(lse_b - peak))
    return total, jnp.exp2(lse_a - total) * d_a + jnp.exp2(lse_b - total) * d_b


def levels_kernel(
    p, q_own, q_other, g_own, g_other, e1, e2, top1, top2, dp1, dp2, mine, theirs, *refs
):
    ds1, ds2, total1, delta1, own_part = refs[:5]
    outs, (dk1, dv1, dk2, dv2) = refs[5:-4], refs[-4:]
    n1, n2 = p.n1, p.n2
    came = pltpu.roll(theirs[...], n1, 1)
    total, delta = join(mine[: p.heads, :], mine[p.heads :, :], came[: p.heads], came[p.heads :])
    total1[...] = total
    delta1[...] = delta
    delta = along(p, delta)
    q, g = both_cores(q_own, q_other), both_cores(g_own, g_other)
    for ref in (dk1, dv1, dk2, dv2):
        ref[...] = jnp.zeros_like(ref)
    for e, top, dp, kept, dk, dv in ((e1, top1, dp1, ds1, dk1, dv1), (e2, top2, dp2, ds2, dk2, dv2)):
        prob = e[...] * along(p, jnp.exp2(top[...] - total))
        ds = (prob * (dp[...] - delta) * SCALE).astype(BF16)
        kept[...] = ds
        collect(p, prob.astype(BF16), g, dv)
        collect(p, ds, q, dk)
    for i in range(p.g2 // 2):
        rows = slice(i * n2, (i + 1) * n2)
        if 2 * i < p.g1:
            head = slice(i * n1, i * n1 + n2)
            rest = slice(i * n1 + n2, (i + 1) * n1)
            part = []
            for near, wide in ((dk1, dk2), (dv1, dv2)):
                part += [near[head, :] + wide[rows, :], near[rest, :]]
        else:
            part = [dk2[rows, :], dv2[rows, :]]
        part = jnp.concatenate(part, axis=0)
        ref = outs[i - 1] if i else own_part
        ref[...] = part.astype(ref.dtype)


def queries_kernel(p, ds1, ds2, *refs):
    kv, (dq_own, dq_other, dq) = refs[: p.g2 // 2], refs[p.g2 // 2 :]
    k1, k2 = near_blocks(p, 0, kv), wide_blocks(p, 0, kv)
    count = 2 * p.n1
    for first, end, low, high in head_groups(p):
        columns = slice(first * count, end * count)
        part = tn(ds1[:, columns], k1[:, low:high]) + tn(ds2[:, columns], k2[:, low:high])
        for h in range(first, end):
            low_h, high_h = window(h)
            at = (h - first) * count
            piece = part[at : at + count, low_h - low : high_h - low]
            hit = window_mask(h, low_h, high_h)
            dq[:, low_h:high_h] = jnp.where(hit, piece, dq[:, low_h:high_h])
    dq_own[...] = dq[: p.n1, :]
    dq_other[...] = dq[p.n1 :, :].astype(BF16)


def own_grad_kernel(
    p, qp, kp, gp, weight, dprob, lse0, d0, total1, delta1, own_part, dq, dk0, dv0
):
    lse = lse0[...]
    share = jnp.exp2(lse - spread_stat(p, total1[...], lse))
    delta = spread_stat(p, delta1[...], d0[...])
    zero = jnp.zeros((p.tokens, p.width), F32)
    dk0[...] = spread(p, own_part[: p.n1, :], column_class(p), zero)
    dv0[...] = spread(p, own_part[p.n1 :, :], column_class(p), zero)
    for h in range(p.heads):
        low, high = window(h)
        rows = slice(h * p.tokens, (h + 1) * p.tokens)
        hit = window_mask(h, low, high)
        mask = jnp.where(hit, 1.0, 0.0).astype(BF16)
        prob = weight[rows, :] * share[h : h + 1, :]
        ds = (prob * (dprob[rows, :] - delta[h : h + 1, :]) * SCALE).astype(BF16)
        dq[:, low:high] = jnp.where(hit, tn(ds, kp[:, low:high]), dq[:, low:high])
        dk0[:, low:high] += nn(ds, qp[:, low:high] * mask)
        dv0[:, low:high] += nn(prob.astype(BF16), gp[:, low:high] * mask)


def finish_kernel(p, dq, dq_own, dq_came, grad_q):
    kept = dq_own[...] + dq_came[...].astype(F32)
    zero = jnp.zeros((p.tokens, p.width), F32)
    whole = dq[...] + spread(p, kept, column_class(p), zero)
    grad_q[...] = nn(phase_order(p, True), whole.astype(BF16)).astype(BF16)


def last_kernel(p, dk0, dv0, *refs):
    came, (grad_k, grad_v, out_k, out_v, sems) = refs[:-5], refs[-5:]
    order = phase_order(p, True)
    label = column_class(p)
    zero = jnp.zeros((p.tokens, p.width), F32)
    copies = []
    for index, (base, out, grad) in enumerate(((dk0, out_k, grad_k), (dv0, out_v, grad_v))):
        first = jnp.zeros((p.n2, p.width), F32)
        rest = jnp.zeros((p.n1 - p.n2, p.width), F32)
        for ref in came:
            half = ref.shape[0] // 2
            block = ref[...].astype(F32)
            first = first + block[index * half : index * half + p.n2]
            if half == p.n1:
                rest = rest + block[index * half + p.n2 : (index + 1) * half]
        kept = jnp.concatenate([first, rest], axis=0)
        whole = base[...] + spread(p, kept, label, zero)
        out[...] = nn(order, whole.astype(BF16)).astype(BF16)
        copies.append(pltpu.make_async_copy(out, grad, sems.at[index]))
        copies[-1].start()
    for copy in copies:
        copy.wait()


def swap(block, axis, bits):
    count = lax.axis_size(axis)
    return lax.ppermute(block, axis, [(i, i ^ bits) for i in range(count)])


def body(queries, keys, values, grad_out):
    tokens, width = queries.shape
    queries, keys, values, grad_out = (
        pltpu.with_memory_space_constraint(field, pltpu.HBM)
        for field in (queries, keys, values, grad_out)
    )
    p = Plan(tokens, width, lax.axis_size("seq"), lax.axis_size("head"))
    n1, n2 = p.n1, p.n2
    run = lambda kernel: functools.partial(kernel, p)
    row, kept = (tokens, width), (n1, width)
    share = (tokens // p.zcount, width)
    stat, stat1 = (p.heads, tokens), (p.heads, 2 * n1)
    flat = lambda count: (count, tokens)
    even = range(0, p.g2, 2)
    half_rows = sum(p.rows[::2])
    hbm = pl.BlockSpec(memory_space=pltpu.HBM)

    outs = call(
        run(pack_kernel),
        [(row, BF16)] * 3
        + [(kept, BF16), ((2 * n1, width), BF16), ((2 * n2, width), BF16)]
        + [(share, BF16)] * p.zcount,
        [(row, BF16)] * 3 + [pltpu.SemaphoreType.DMA((p.zcount + 3,))],
        in_specs=[hbm] * 4,
    )(queries, keys, values, grad_out)
    qp, kp, vp, q1, kv1, kv2 = outs[:6]
    gz = outs[6:]
    gz = [gz[0]] + [swap(gz[b], "head", b) for b in range(1, p.zcount)]

    kv = [kv1] + [swap(kv1 if b < p.g1 else kv2, "seq", b) for b in even[1:]]

    q_other = swap(q1, "seq", 1)
    weight, lse0, lse01 = call(
        run(own_scores_kernel), [(flat(p.heads * tokens), F32), (stat, F32), (stat1, F32)]
    )(qp, kp, q_other)
    near = (p.g1 // 2 * n1, 2 * p.heads * n1)
    wide = (p.g2 // 2 * n2, 2 * p.heads * n1)
    e1, top1, sum1 = call(run(near_kernel), [(near, F32)] + [(stat1, F32)] * 2)(
        q1, q_other, *kv[: p.g1 // 2]
    )
    e2, top2, sum2 = call(run(wide_kernel), [(wide, F32)] + [(stat1, F32)] * 2)(
        q1, q_other, *kv
    )
    gp, g1 = call(run(gather_kernel), [(row, BF16), (kept, BF16)], [(row, BF16)])(
        lse01, *gz[::-1]
    )
    g_other = swap(g1, "seq", 1)
    dprob, d0, d01 = call(
        run(own_delta_kernel), [(flat(p.heads * tokens), F32), (stat, F32), (stat1, F32)]
    )(vp, weight, gp)
    dp1, dp2, mine = call(
        run(delta_kernel), [(near, F32), (wide, F32), ((2 * p.heads, 2 * n1), F32)]
    )(g1, g_other, e1, e2, top1, sum1, top2, sum2, lse01, d01, *kv)
    theirs = swap(mine, "seq", 1)
    part = lambda b, dtype: ((p.rows[b], width), dtype)
    outs = call(
        run(levels_kernel),
        [(near, BF16), (wide, BF16), (stat1, F32), (stat1, F32), part(0, F32)]
        + [part(b, BF16) for b in even[1:]],
        [((near[0], width), F32)] * 2 + [((wide[0], width), F32)] * 2,
    )(q1, q_other, g1, g_other, e1, e2, top1, top2, dp1, dp2, mine, theirs)
    ds1, ds2, total1, delta1, own_part = outs[:5]
    parts = [swap(s, "seq", b) for s, b in zip(outs[5:], even[1:])]
    dq_own, dq_other = call(
        run(queries_kernel),
        [(kept, F32), (kept, BF16)],
        [((2 * n1, width), F32)],
    )(ds1, ds2, *kv)
    dq_came = swap(dq_other, "seq", 1)
    dq, dk0, dv0 = call(run(own_grad_kernel), [(row, F32)] * 3)(
        qp, kp, gp, weight, dprob, lse0, d0, total1, delta1, own_part
    )
    (grad_q,) = call(run(finish_kernel), [(row, BF16)])(dq, dq_own, dq_came)
    grad_k, grad_v = call(
        run(last_kernel),
        [(row, BF16)] * 2,
        [(row, BF16)] * 2 + [pltpu.SemaphoreType.DMA((2,))],
        out_specs=[hbm] * 2,
    )(dk0, dv0, *parts)
    return grad_q, grad_k, grad_v


def solution(mesh):
    return jax.shard_map(
        body,
        mesh=mesh,
        in_specs=(P("seq", "head"), P("seq", "head"), P("seq", "head"), P(("seq", "head"), None)),
        out_specs=(P("seq", "head"), P("seq", "head"), P("seq", "head")),
        check_vma=False,
    )
```

```python
import functools
import math

import jax
import jax.numpy as jnp
from jax import lax
from jax.experimental import pallas as pl
from jax.experimental.pallas import tpu as pltpu
from jax.sharding import PartitionSpec as P

HD = 80
SPAN1 = 4
DIL1 = 4
WIDEST = 32
LANES = 128
BF16 = jnp.bfloat16
F32 = jnp.float32
SCALE = HD**-0.5
SCALE2 = SCALE * math.log2(math.e)
VMEM_BYTES = 28 * 2**20
LOWEST = -1e30
TINY = 1e-30


class Plan:
    def __init__(self, tokens, width, seq_count, head_count):
        self.tokens = tokens
        self.width = width
        self.heads = width // HD
        self.g1 = SPAN1
        self.g2 = min(WIDEST, seq_count)
        self.r2 = self.g2
        self.n1 = tokens // DIL1
        self.n2 = tokens // self.r2
        self.turns = self.r2 // DIL1
        self.zcount = head_count
        self.rows = [2 * (self.n1 if b < self.g1 else self.n2) for b in range(self.g2)]


def nt(a, b):
    return lax.dot_general(a, b, (((1,), (1,)), ((), ())), preferred_element_type=F32)


def nn(a, b):
    return lax.dot_general(a, b, (((1,), (0,)), ((), ())), preferred_element_type=F32)


def tn(a, b):
    return lax.dot_general(a, b, (((0,), (0,)), ((), ())), preferred_element_type=F32)


def iota(shape, dim):
    return lax.broadcasted_iota(jnp.int32, shape, dim)


def phase_order(p, inverse=False):
    shape = (p.tokens, p.tokens)
    row, col = (iota(shape, 1), iota(shape, 0)) if inverse else (iota(shape, 0), iota(shape, 1))
    return jnp.where(col == p.r2 * (row % p.n2) + row // p.n2, 1.0, 0.0).astype(BF16)


def first_head(p):
    return lax.axis_index("head") * p.heads


def column_class(p):
    return (first_head(p) + iota((1, p.width), 1) // HD) % p.r2


def row_class(p):
    return (first_head(p) + iota((p.heads, 1), 0)) % p.r2


def pick(p, whole, label):
    parts = []
    for t in range(p.turns):
        want = (label + DIL1 * t) % p.r2
        part = jnp.zeros((p.n2, whole.shape[1]), F32)
        for c in range(p.r2):
            part = jnp.where(want == c, whole[c * p.n2 : (c + 1) * p.n2], part)
        parts.append(part)
    return jnp.concatenate(parts, axis=0)


def spread(p, kept, label, base):
    parts = []
    for c in range(p.r2):
        part = base[c * p.n2 : (c + 1) * p.n2]
        for t in range(p.turns):
            hit = (label + DIL1 * t) % p.r2 == c
            part = jnp.where(hit, kept[t * p.n2 : (t + 1) * p.n2], part)
        parts.append(part)
    return jnp.concatenate(parts, axis=0)


def window(h):
    low = h * HD // LANES * LANES
    high = -(-(h + 1) * HD // LANES) * LANES
    return low, high


def window_mask(h, low, high):
    lane = low + iota((1, high - low), 1)
    return (lane >= h * HD) & (lane < (h + 1) * HD)


def head_groups(p):
    groups, h = [], 0
    while h < p.heads:
        low, high = window(h)
        end = h + 1
        while end < p.heads and window(end)[1] - low <= 2 * LANES:
            high = window(end)[1]
            end += 1
        groups.append((h, end, low, high))
        h = end
    return groups


def head_mask(p, h):
    lane = iota((1, p.width), 1)
    return (lane >= h * HD) & (lane < (h + 1) * HD)


def own_bias(p):
    shape = (p.tokens, p.tokens)
    key, query = iota(shape, 0), iota(shape, 1)
    qpos = p.r2 * (query % p.n2) + query // p.n2
    kpos = p.r2 * (key % p.n2) + key // p.n2
    return jnp.where(qpos >= kpos, 0.0, -jnp.inf)


def pick_stat(p, stat, fill):
    lane = iota((1, 2 * p.n1), 1)
    label = row_class(p)
    out = jnp.full((p.heads, 2 * p.n1), fill, F32)
    for t in range(p.turns):
        here = (lane >= t * p.n2) & (lane < (t + 1) * p.n2)
        for c in range(p.r2):
            moved = pltpu.roll(stat, (t - c) * p.n2 % p.tokens, 1)[:, : 2 * p.n1]
            out = jnp.where(here & ((label + DIL1 * t) % p.r2 == c), moved, out)
    return out


def spread_stat(p, kept, base):
    lane = iota((1, p.tokens), 1)
    label = row_class(p)
    padded = jnp.concatenate([kept] * (p.tokens // kept.shape[1]), axis=1)
    out = base
    for t in range(p.turns):
        for c in range(p.r2):
            moved = pltpu.roll(padded, (c - t) * p.n2 % p.tokens, 1)
            here = (lane >= c * p.n2) & (lane < (c + 1) * p.n2)
            out = jnp.where(here & ((label + DIL1 * t) % p.r2 == c), moved, out)
    return out


def by_rows(p, flat):
    count = flat.shape[1] // p.heads
    return jnp.concatenate([flat[:, h * count : (h + 1) * count] for h in range(p.heads)], axis=0)


def along(p, stat):
    return jnp.concatenate([stat[h : h + 1, :] for h in range(p.heads)], axis=1)


def call(kernel, outs, scratch=(), flops=0, **specs):
    return pl.pallas_call(
        kernel,
        out_shape=[jax.ShapeDtypeStruct(s, d) for s, d in outs],
        scratch_shapes=[pltpu.VMEM(*s) if isinstance(s, tuple) else s for s in scratch],
        compiler_params=pltpu.CompilerParams(vmem_limit_bytes=VMEM_BYTES),
        cost_estimate=pl.CostEstimate(flops=flops, bytes_accessed=2**20, transcendentals=0),
        **specs,
    )


def slab(p, g_ref, b):
    start = pl.multiple_of(jnp.bitwise_xor(lax.axis_index("head"), b) * p.width, LANES)
    return g_ref.at[:, pl.ds(start, p.width)]


def pack_kernel(p, q_ref, k_ref, v_ref, g_ref, qp, kp, vp, q1, kv1, kv2, *refs):
    gz, (q_in, k_in, v_in, sems) = refs[: p.zcount], refs[p.zcount :]
    loads = [(k_ref, k_in), (v_ref, v_in), (q_ref, q_in)]
    loads += [(slab(p, g_ref, b), gz[b]) for b in range(p.zcount)]
    copies = [pltpu.make_async_copy(src, dst, sems.at[i]) for i, (src, dst) in enumerate(loads)]
    for copy in copies:
        copy.start()
    order = phase_order(p)
    label = column_class(p)
    copies[0].wait()
    k = nn(order, k_in[...])
    kp[...] = k.astype(BF16)
    k_kept = pick(p, k, label)
    copies[1].wait()
    v = nn(order, v_in[...])
    vp[...] = v.astype(BF16)
    v_kept = pick(p, v, label)
    kv1[...] = jnp.concatenate([k_kept, v_kept], axis=0).astype(BF16)
    kv2[...] = jnp.concatenate([k_kept[: p.n2], v_kept[: p.n2]], axis=0).astype(BF16)
    copies[2].wait()
    q = nn(order, q_in[...])
    qp[...] = q.astype(BF16)
    q1[...] = pick(p, q, label).astype(BF16)
    for copy in copies[3:]:
        copy.wait()


def own_scores_kernel(p, qp, kp, after, weight, lse0, lse01):
    bias = own_bias(p)
    rows = []
    for h in range(p.heads):
        low, high = window(h)
        mask = jnp.where(window_mask(h, low, high), 1.0, 0.0).astype(BF16)
        s = nt(kp[:, low:high], qp[:, low:high] * mask) * SCALE2 + bias
        top = jnp.max(s, axis=0, keepdims=True)
        e = jnp.exp2(s - top)
        denom = jnp.sum(e, axis=0, keepdims=True)
        weight[h * p.tokens : (h + 1) * p.tokens, :] = e * (1.0 / denom)
        rows.append(top + jnp.log2(denom))
    lse = jnp.concatenate(rows, axis=0)
    lse0[...] = lse
    lse01[...] = pick_stat(p, lse, LOWEST)


def gather_kernel(p, after, *refs):
    gz, (gp, g1, natural) = refs[: p.zcount], refs[p.zcount :]
    z = lax.axis_index("head")
    share = p.tokens // p.zcount
    for b in range(p.zcount):
        start = pl.multiple_of(jnp.bitwise_xor(z, b) * share, share)
        natural[pl.ds(start, share), :] = gz[p.zcount - 1 - b][...]
    g = nn(phase_order(p), natural[...])
    gp[...] = g.astype(BF16)
    g1[...] = pick(p, g, column_class(p)).astype(BF16)


def own_delta_kernel(p, vp, weight, gp, dprob, d0, d01):
    sums = []
    for h in range(p.heads):
        low, high = window(h)
        rows = slice(h * p.tokens, (h + 1) * p.tokens)
        mask = jnp.where(window_mask(h, low, high), 1.0, 0.0).astype(BF16)
        dp = nt(vp[:, low:high], gp[:, low:high] * mask)
        dprob[rows, :] = dp
        sums.append(jnp.sum(weight[rows, :] * dp, axis=0, keepdims=True))
    d = jnp.concatenate(sums, axis=0)
    d0[...] = d
    d01[...] = pick_stat(p, d, 0.0)


def cut(p, block, start, count):
    if start % 16 or count % 16:
        block = block.astype(F32)
    return block[start : start + count]


def both_cores(own, other):
    return jnp.concatenate([own[...], other[...]], axis=0)


def by_head(rows, group):
    first, end, low, high = group
    parts = []
    for h in range(first, end):
        mask = jnp.where(window_mask(h, low, high), 1.0, 0.0).astype(BF16)
        parts.append(rows[:, low:high] * mask)
    return jnp.concatenate(parts, axis=0)


def against(p, cols, rows):
    parts = []
    for group in head_groups(p):
        low, high = group[2:]
        parts.append(nt(cols[:, low:high], by_head(rows, group)))
    return jnp.concatenate(parts, axis=1)


def collect(p, weights, rows, out):
    count = rows.shape[0]
    for group in head_groups(p):
        first, end, low, high = group
        part = nn(weights[:, first * count : end * count], by_head(rows, group))
        out[:, low:high] += part


def near_blocks(p, half, kv):
    blocks = [cut(p, ref[...], half * p.n1, p.n1) for ref in kv[: p.g1 // 2]]
    return jnp.concatenate(blocks, axis=0).astype(BF16)


def wide_blocks(p, half, kv):
    blocks = [cut(p, ref[...], half * ref.shape[0] // 2, p.n2) for ref in kv]
    return jnp.concatenate(blocks, axis=0).astype(BF16)


def soft(p, scores, e, tops, sums):
    top = jnp.maximum(jnp.max(scores, axis=0, keepdims=True), LOWEST)
    weight = jnp.exp2(scores - top)
    e[...] = weight
    tops[...] = by_rows(p, top)
    sums[...] = by_rows(p, jnp.sum(weight, axis=0, keepdims=True))


def near_kernel(p, q_own, q_other, *refs):
    kv, outs = refs[: p.g1 // 2], refs[p.g1 // 2 :]
    d = lax.axis_index("seq")
    n1, n2 = p.n1, p.n2
    row = iota((p.g1 // 2 * n1, 1), 0)
    col = iota((1, 2 * p.heads * n1), 1)
    head = first_head(p) + col // (2 * n1)
    own = col % n1
    device = jnp.bitwise_xor(d, col // n1 % 2)
    qpos = p.tokens * device + p.r2 * (own % n2) + (head + DIL1 * (own // n2)) % p.r2
    other = row % n1
    kbase = p.tokens * jnp.bitwise_xor(d, 2 * (row // n1)) + p.r2 * (other % n2)
    kpos = kbase + jnp.bitwise_and(head + DIL1 * (other // n2), p.r2 - 1)
    s = against(p, near_blocks(p, 0, kv), both_cores(q_own, q_other)) * SCALE2
    soft(p, jnp.where(kpos <= qpos, s, -jnp.inf), *outs)


def wide_kernel(p, q_own, q_other, *refs):
    kv, outs = refs[: p.g2 // 2], refs[p.g2 // 2 :]
    d = lax.axis_index("seq")
    n1, n2 = p.n1, p.n2
    row = iota((p.g2 // 2 * n2, 1), 0)
    row = jnp.bitwise_xor(d, 2 * (row // n2)) * n2 + row % n2
    col = iota((1, 2 * p.heads * n1), 1)
    last = jnp.bitwise_xor(d, col // n1 % 2) * n2 + col % n1
    last = jnp.where(col % n1 < n2, last, -1)
    s = against(p, wide_blocks(p, 0, kv), both_cores(q_own, q_other)) * SCALE2
    soft(p, jnp.where(row <= last, s, -jnp.inf), *outs)


def delta_kernel(p, g_own, g_other, e1, e2, top1, sum1, top2, sum2, lse01, d01, *refs):
    kv, (dp1, dp2, stats) = refs[: p.g2 // 2], refs[p.g2 // 2 :]
    g = both_cores(g_own, g_other)
    dp = against(p, near_blocks(p, 1, kv), g)
    dp1[...] = dp
    near = by_rows(p, jnp.sum(e1[...] * dp, axis=0, keepdims=True))
    dp = against(p, wide_blocks(p, 1, kv), g)
    dp2[...] = dp
    wide = by_rows(p, jnp.sum(e2[...] * dp, axis=0, keepdims=True))

    peak = jnp.maximum(top1[...], top2[...])
    up1, up2 = jnp.exp2(top1[...] - peak), jnp.exp2(top2[...] - peak)
    both = jnp.maximum(sum1[...] * up1 + sum2[...] * up2, TINY)
    d = (near * up1 + wide * up2) / both
    total, delta = join(lse01[...], d01[...], peak + jnp.log2(both), d)
    stats[...] = jnp.concatenate([total, delta], axis=0)


def join(lse_a, d_a, lse_b, d_b):
    peak = jnp.maximum(lse_a, lse_b)
    total = peak + jnp.log2(jnp.exp2(lse_a - peak) + jnp.exp2(lse_b - peak))
    return total, jnp.exp2(lse_a - total) * d_a + jnp.exp2(lse_b - total) * d_b


def levels_kernel(
    p, q_own, q_other, g_own, g_other, e1, e2, top1, top2, dp1, dp2, mine, theirs, *refs
):
    ds1, ds2, total1, delta1, own_part = refs[:5]
    outs, (dk1, dv1, dk2, dv2) = refs[5:-4], refs[-4:]
    n1, n2 = p.n1, p.n2
    came = pltpu.roll(theirs[...], n1, 1)
    total, delta = join(mine[: p.heads, :], mine[p.heads :, :], came[: p.heads], came[p.heads :])
    total1[...] = total
    delta1[...] = delta
    delta = along(p, delta)
    q, g = both_cores(q_own, q_other), both_cores(g_own, g_other)
    for ref in (dk1, dv1, dk2, dv2):
        ref[...] = jnp.zeros_like(ref)
    for e, top, dp, kept, dk, dv in ((e1, top1, dp1, ds1, dk1, dv1), (e2, top2, dp2, ds2, dk2, dv2)):
        prob = e[...] * along(p, jnp.exp2(top[...] - total))
        ds = (prob * (dp[...] - delta) * SCALE).astype(BF16)
        kept[...] = ds
        collect(p, prob.astype(BF16), g, dv)
        collect(p, ds, q, dk)
    for i in range(p.g2 // 2):
        rows = slice(i * n2, (i + 1) * n2)
        if 2 * i < p.g1:
            head = slice(i * n1, i * n1 + n2)
            rest = slice(i * n1 + n2, (i + 1) * n1)
            part = []
            for near, wide in ((dk1, dk2), (dv1, dv2)):
                part += [near[head, :] + wide[rows, :], near[rest, :]]
        else:
            part = [dk2[rows, :], dv2[rows, :]]
        part = jnp.concatenate(part, axis=0)
        ref = outs[i - 1] if i else own_part
        ref[...] = part.astype(ref.dtype)


def queries_kernel(p, ds1, ds2, *refs):
    kv, (dq_own, dq_low, dq_high, dq) = refs[: p.g2 // 2], refs[p.g2 // 2 :]
    k1, k2 = near_blocks(p, 0, kv), wide_blocks(p, 0, kv)
    count = 2 * p.n1
    for first, end, low, high in head_groups(p):
        columns = slice(first * count, end * count)
        part = tn(ds1[:, columns], k1[:, low:high]) + tn(ds2[:, columns], k2[:, low:high])
        for h in range(first, end):
            low_h, high_h = window(h)
            at = (h - first) * count
            piece = part[at : at + count, low_h - low : high_h - low]
            hit = window_mask(h, low_h, high_h)
            dq[:, low_h:high_h] = jnp.where(hit, piece, dq[:, low_h:high_h])
    dq_own[...] = dq[: p.n1, :]
    half = p.n1 // 2
    dq_low[...] = dq[p.n1 : p.n1 + half, :].astype(BF16)
    dq_high[...] = dq[p.n1 + half :, :].astype(BF16)


def own_grad_kernel(
    p, qp, kp, gp, weight, dprob, lse0, d0, total1, delta1, own_part, dq, dk0, dv0
):
    lse = lse0[...]
    share = jnp.exp2(lse - spread_stat(p, total1[...], lse))
    delta = spread_stat(p, delta1[...], d0[...])
    zero = jnp.zeros((p.tokens, p.width), F32)
    dk0[...] = spread(p, own_part[: p.n1, :], column_class(p), zero)
    dv0[...] = spread(p, own_part[p.n1 :, :], column_class(p), zero)
    for h in range(p.heads):
        low, high = window(h)
        rows = slice(h * p.tokens, (h + 1) * p.tokens)
        hit = window_mask(h, low, high)
        mask = jnp.where(hit, 1.0, 0.0).astype(BF16)
        prob = weight[rows, :] * share[h : h + 1, :]
        ds = (prob * (dprob[rows, :] - delta[h : h + 1, :]) * SCALE).astype(BF16)
        dq[:, low:high] = jnp.where(hit, tn(ds, kp[:, low:high]), dq[:, low:high])
        dk0[:, low:high] += nn(ds, qp[:, low:high] * mask)
        dv0[:, low:high] += nn(prob.astype(BF16), gp[:, low:high] * mask)


def finish_kernel(p, dq, dq_own, dq_low, dq_high, grad_q):
    kept = dq_own[...] + both_cores(dq_low, dq_high).astype(F32)
    zero = jnp.zeros((p.tokens, p.width), F32)
    whole = dq[...] + spread(p, kept, column_class(p), zero)
    grad_q[...] = nn(phase_order(p, True), whole.astype(BF16)).astype(BF16)


def last_kernel(p, dk0, dv0, *refs):
    came, (grad_k, grad_v, out_k, out_v, sems) = refs[:-5], refs[-5:]
    order = phase_order(p, True)
    label = column_class(p)
    zero = jnp.zeros((p.tokens, p.width), F32)
    copies = []
    for index, (base, out, grad) in enumerate(((dk0, out_k, grad_k), (dv0, out_v, grad_v))):
        first = jnp.zeros((p.n2, p.width), F32)
        rest = jnp.zeros((p.n1 - p.n2, p.width), F32)
        for ref in came:
            half = ref.shape[0] // 2
            block = ref[...].astype(F32)
            first = first + block[index * half : index * half + p.n2]
            if half == p.n1:
                rest = rest + block[index * half + p.n2 : (index + 1) * half]
        kept = jnp.concatenate([first, rest], axis=0)
        whole = base[...] + spread(p, kept, label, zero)
        out[...] = nn(order, whole.astype(BF16)).astype(BF16)
        copies.append(pltpu.make_async_copy(out, grad, sems.at[index]))
        copies[-1].start()
    for copy in copies:
        copy.wait()


def swap(block, axis, bits):
    count = lax.axis_size(axis)
    return lax.ppermute(block, axis, [(i, i ^ bits) for i in range(count)])


def body(queries, keys, values, grad_out):
    tokens, width = queries.shape
    queries, keys, values, grad_out = (
        pltpu.with_memory_space_constraint(field, pltpu.HBM)
        for field in (queries, keys, values, grad_out)
    )
    p = Plan(tokens, width, lax.axis_size("seq"), lax.axis_size("head"))
    n1, n2 = p.n1, p.n2
    run = lambda kernel: functools.partial(kernel, p)
    row, kept = (tokens, width), (n1, width)
    share = (tokens // p.zcount, width)
    stat, stat1 = (p.heads, tokens), (p.heads, 2 * n1)
    flat = lambda count: (count, tokens)
    even = range(0, p.g2, 2)
    half_rows = sum(p.rows[::2])
    hbm = pl.BlockSpec(memory_space=pltpu.HBM)

    outs = call(
        run(pack_kernel),
        [(row, BF16)] * 3
        + [(kept, BF16), ((2 * n1, width), BF16), ((2 * n2, width), BF16)]
        + [(share, BF16)] * p.zcount,
        [(row, BF16)] * 3 + [pltpu.SemaphoreType.DMA((p.zcount + 3,))],
        in_specs=[hbm] * 4,
    )(queries, keys, values, grad_out)
    qp, kp, vp, q1, kv1, kv2 = outs[:6]
    gz = outs[6:]
    gz = [gz[0]] + [swap(gz[b], "head", b) for b in range(1, p.zcount)]

    kv = [kv1] + [swap(kv1 if b < p.g1 else kv2, "seq", b) for b in even[1:]]

    q_other = swap(q1, "seq", 1)
    weight, lse0, lse01 = call(
        run(own_scores_kernel), [(flat(p.heads * tokens), F32), (stat, F32), (stat1, F32)]
    )(qp, kp, q_other)
    near = (p.g1 // 2 * n1, 2 * p.heads * n1)
    wide = (p.g2 // 2 * n2, 2 * p.heads * n1)
    e1, top1, sum1 = call(run(near_kernel), [(near, F32)] + [(stat1, F32)] * 2)(
        q1, q_other, *kv[: p.g1 // 2]
    )
    e2, top2, sum2 = call(run(wide_kernel), [(wide, F32)] + [(stat1, F32)] * 2)(
        q1, q_other, *kv
    )
    gp, g1 = call(run(gather_kernel), [(row, BF16), (kept, BF16)], [(row, BF16)])(
        lse01, *gz[::-1]
    )
    g_other = swap(g1, "seq", 1)
    dprob, d0, d01 = call(
        run(own_delta_kernel), [(flat(p.heads * tokens), F32), (stat, F32), (stat1, F32)]
    )(vp, weight, gp)
    dp1, dp2, mine = call(
        run(delta_kernel), [(near, F32), (wide, F32), ((2 * p.heads, 2 * n1), F32)]
    )(g1, g_other, e1, e2, top1, sum1, top2, sum2, lse01, d01, *kv)
    theirs = swap(mine, "seq", 1)
    part = lambda b, dtype: ((p.rows[b], width), dtype)
    outs = call(
        run(levels_kernel),
        [(near, BF16), (wide, BF16), (stat1, F32), (stat1, F32), part(0, F32)]
        + [part(b, BF16) for b in even[1:]],
        [((near[0], width), F32)] * 2 + [((wide[0], width), F32)] * 2,
    )(q1, q_other, g1, g_other, e1, e2, top1, top2, dp1, dp2, mine, theirs)
    ds1, ds2, total1, delta1, own_part = outs[:5]
    parts = [swap(s, "seq", b) for s, b in zip(outs[5:], even[1:])]
    dq_own, *dq_other = call(
        run(queries_kernel),
        [(kept, F32)] + [((n1 // 2, width), BF16)] * 2,
        [((2 * n1, width), F32)],
    )(ds1, ds2, *kv)
    dq_came = [swap(half, "seq", 1) for half in dq_other]
    dq, dk0, dv0 = call(run(own_grad_kernel), [(row, F32)] * 3)(
        qp, kp, gp, weight, dprob, lse0, d0, total1, delta1, own_part
    )
    (grad_q,) = call(run(finish_kernel), [(row, BF16)])(dq, dq_own, *dq_came)
    grad_k, grad_v = call(
        run(last_kernel),
        [(row, BF16)] * 2,
        [(row, BF16)] * 2 + [pltpu.SemaphoreType.DMA((2,))],
        out_specs=[hbm] * 2,
    )(dk0, dv0, *parts)
    return grad_q, grad_k, grad_v


def solution(mesh):
    return jax.shard_map(
        body,
        mesh=mesh,
        in_specs=(P("seq", "head"), P("seq", "head"), P("seq", "head"), P(("seq", "head"), None)),
        out_specs=(P("seq", "head"), P("seq", "head"), P("seq", "head")),
        check_vma=False,
    )
```

```python
import functools
import math

import jax
import jax.numpy as jnp
from jax import lax
from jax.experimental import pallas as pl
from jax.experimental.pallas import tpu as pltpu
from jax.sharding import PartitionSpec as P

HD = 80
SPAN1 = 4
DIL1 = 4
WIDEST = 32
LANES = 128
BF16 = jnp.bfloat16
F32 = jnp.float32
SCALE = HD**-0.5
SCALE2 = SCALE * math.log2(math.e)
VMEM_BYTES = 28 * 2**20
LOWEST = -1e30
TINY = 1e-30


class Plan:
    def __init__(self, tokens, width, seq_count, head_count):
        self.tokens = tokens
        self.width = width
        self.heads = width // HD
        self.g1 = SPAN1
        self.g2 = min(WIDEST, seq_count)
        self.r2 = self.g2
        self.n1 = tokens // DIL1
        self.n2 = tokens // self.r2
        self.turns = self.r2 // DIL1
        self.zcount = head_count
        self.rows = [2 * (self.n1 if b < self.g1 else self.n2) for b in range(self.g2)]


def nt(a, b):
    return lax.dot_general(a, b, (((1,), (1,)), ((), ())), preferred_element_type=F32)


def nn(a, b):
    return lax.dot_general(a, b, (((1,), (0,)), ((), ())), preferred_element_type=F32)


def tn(a, b):
    return lax.dot_general(a, b, (((0,), (0,)), ((), ())), preferred_element_type=F32)


def iota(shape, dim):
    return lax.broadcasted_iota(jnp.int32, shape, dim)


def phase_order(p, inverse=False):
    shape = (p.tokens, p.tokens)
    row, col = (iota(shape, 1), iota(shape, 0)) if inverse else (iota(shape, 0), iota(shape, 1))
    return jnp.where(col == p.r2 * (row % p.n2) + row // p.n2, 1.0, 0.0).astype(BF16)


def first_head(p):
    return lax.axis_index("head") * p.heads


def column_class(p):
    return (first_head(p) + iota((1, p.width), 1) // HD) % p.r2


def row_class(p):
    return (first_head(p) + iota((p.heads, 1), 0)) % p.r2


def tiles(p):
    out = []
    for low in range(0, p.width, LANES):
        high = min(low + LANES, p.width)
        out.append((low, high, range(low // HD, -(-high // HD))))
    return out


def pick(p, whole, label):
    parts = []
    for t in range(p.turns):
        if p.heads % p.r2 == 0:
            lanes = []
            for low, high, heads in tiles(p):
                lane = low + iota((1, high - low), 1)
                part = None
                for h in heads:
                    c = (h + DIL1 * t) % p.r2
                    rows = whole[c * p.n2 : (c + 1) * p.n2, low:high]
                    part = rows if part is None else jnp.where(lane >= h * HD, rows, part)
                lanes.append(part)
            parts.append(jnp.concatenate(lanes, axis=1))
            continue
        want = (label + DIL1 * t) % p.r2
        part = jnp.zeros((p.n2, whole.shape[1]), F32)
        for c in range(p.r2):
            part = jnp.where(want == c, whole[c * p.n2 : (c + 1) * p.n2], part)
        parts.append(part)
    return jnp.concatenate(parts, axis=0)


def spread(p, kept, label, base):
    parts = []
    for c in range(p.r2):
        rows = slice(c * p.n2, (c + 1) * p.n2)
        if p.heads % p.r2 == 0:
            lanes = []
            for low, high, heads in tiles(p):
                lane = low + iota((1, high - low), 1)
                part = base[rows, low:high]
                for t in range(p.turns):
                    for h in heads:
                        if (h + DIL1 * t) % p.r2 == c:
                            hit = (lane >= h * HD) & (lane < (h + 1) * HD)
                            moved = kept[t * p.n2 : (t + 1) * p.n2, low:high]
                            part = jnp.where(hit, moved, part)
                lanes.append(part)
            parts.append(jnp.concatenate(lanes, axis=1))
            continue
        part = base[rows]
        for t in range(p.turns):
            hit = (label + DIL1 * t) % p.r2 == c
            part = jnp.where(hit, kept[t * p.n2 : (t + 1) * p.n2], part)
        parts.append(part)
    return jnp.concatenate(parts, axis=0)


def window(h):
    low = h * HD // LANES * LANES
    high = -(-(h + 1) * HD // LANES) * LANES
    return low, high


def window_mask(h, low, high):
    lane = low + iota((1, high - low), 1)
    return (lane >= h * HD) & (lane < (h + 1) * HD)


def head_groups(p):
    groups, h = [], 0
    while h < p.heads:
        low, high = window(h)
        end = h + 1
        while end < p.heads and window(end)[1] - low <= 2 * LANES:
            high = window(end)[1]
            end += 1
        groups.append((h, end, low, high))
        h = end
    return groups


def head_mask(p, h):
    lane = iota((1, p.width), 1)
    return (lane >= h * HD) & (lane < (h + 1) * HD)


def own_bias(p):
    shape = (p.tokens, p.tokens)
    key, query = iota(shape, 0), iota(shape, 1)
    qpos = p.r2 * (query % p.n2) + query // p.n2
    kpos = p.r2 * (key % p.n2) + key // p.n2
    return jnp.where(qpos >= kpos, 0.0, -jnp.inf)


def pick_stat(p, stat, fill):
    lane = iota((1, 2 * p.n1), 1)
    label = row_class(p)
    out = jnp.full((p.heads, 2 * p.n1), fill, F32)
    for t in range(p.turns):
        here = (lane >= t * p.n2) & (lane < (t + 1) * p.n2)
        for c in range(p.r2):
            moved = pltpu.roll(stat, (t - c) * p.n2 % p.tokens, 1)[:, : 2 * p.n1]
            out = jnp.where(here & ((label + DIL1 * t) % p.r2 == c), moved, out)
    return out


def spread_stat(p, kept, base):
    lane = iota((1, p.tokens), 1)
    label = row_class(p)
    padded = jnp.concatenate([kept] * (p.tokens // kept.shape[1]), axis=1)
    out = base
    for t in range(p.turns):
        for c in range(p.r2):
            moved = pltpu.roll(padded, (c - t) * p.n2 % p.tokens, 1)
            here = (lane >= c * p.n2) & (lane < (c + 1) * p.n2)
            out = jnp.where(here & ((label + DIL1 * t) % p.r2 == c), moved, out)
    return out


def by_rows(p, flat):
    count = flat.shape[1] // p.heads
    return jnp.concatenate([flat[:, h * count : (h + 1) * count] for h in range(p.heads)], axis=0)


def along(p, stat):
    return jnp.concatenate([stat[h : h + 1, :] for h in range(p.heads)], axis=1)


def call(kernel, outs, scratch=(), flops=0, **specs):
    return pl.pallas_call(
        kernel,
        out_shape=[jax.ShapeDtypeStruct(s, d) for s, d in outs],
        scratch_shapes=[pltpu.VMEM(*s) if isinstance(s, tuple) else s for s in scratch],
        compiler_params=pltpu.CompilerParams(vmem_limit_bytes=VMEM_BYTES),
        cost_estimate=pl.CostEstimate(flops=flops, bytes_accessed=2**20, transcendentals=0),
        **specs,
    )


def slab(p, g_ref, b):
    start = pl.multiple_of(jnp.bitwise_xor(lax.axis_index("head"), b) * p.width, LANES)
    return g_ref.at[:, pl.ds(start, p.width)]


def pack_kernel(p, q_ref, k_ref, v_ref, g_ref, qp, kp, vp, q1, kv1, kv2, *refs):
    gz, (q_in, k_in, v_in, sems) = refs[: p.zcount], refs[p.zcount :]
    loads = [(k_ref, k_in), (v_ref, v_in), (q_ref, q_in)]
    loads += [(slab(p, g_ref, b), gz[b]) for b in range(p.zcount)]
    copies = [pltpu.make_async_copy(src, dst, sems.at[i]) for i, (src, dst) in enumerate(loads)]
    for copy in copies:
        copy.start()
    order = phase_order(p)
    label = column_class(p)
    copies[0].wait()
    k = nn(order, k_in[...])
    kp[...] = k.astype(BF16)
    k_kept = pick(p, k, label)
    copies[1].wait()
    v = nn(order, v_in[...])
    vp[...] = v.astype(BF16)
    v_kept = pick(p, v, label)
    kv1[...] = jnp.concatenate([k_kept, v_kept], axis=0).astype(BF16)
    kv2[...] = jnp.concatenate([k_kept[: p.n2], v_kept[: p.n2]], axis=0).astype(BF16)
    copies[2].wait()
    q = nn(order, q_in[...])
    qp[...] = q.astype(BF16)
    q1[...] = pick(p, q, label).astype(BF16)
    for copy in copies[3:]:
        copy.wait()


def own_scores_kernel(p, qp, kp, after, weight, lse0, lse01):
    bias = own_bias(p)
    rows = []
    for h in range(p.heads):
        low, high = window(h)
        mask = jnp.where(window_mask(h, low, high), 1.0, 0.0).astype(BF16)
        s = nt(kp[:, low:high], qp[:, low:high] * mask) * SCALE2 + bias
        top = jnp.max(s, axis=0, keepdims=True)
        e = jnp.exp2(s - top)
        denom = jnp.sum(e, axis=0, keepdims=True)
        weight[h * p.tokens : (h + 1) * p.tokens, :] = e * (1.0 / denom)
        rows.append(top + jnp.log2(denom))
    lse = jnp.concatenate(rows, axis=0)
    lse0[...] = lse
    lse01[...] = pick_stat(p, lse, LOWEST)


def gather_kernel(p, after, *refs):
    gz, (gp, g1, natural) = refs[: p.zcount], refs[p.zcount :]
    z = lax.axis_index("head")
    share = p.tokens // p.zcount
    for b in range(p.zcount):
        start = pl.multiple_of(jnp.bitwise_xor(z, b) * share, share)
        natural[pl.ds(start, share), :] = gz[p.zcount - 1 - b][...]
    g = nn(phase_order(p), natural[...])
    gp[...] = g.astype(BF16)
    g1[...] = pick(p, g, column_class(p)).astype(BF16)


def own_delta_kernel(p, vp, weight, gp, dprob, d0, d01):
    sums = []
    for h in range(p.heads):
        low, high = window(h)
        rows = slice(h * p.tokens, (h + 1) * p.tokens)
        mask = jnp.where(window_mask(h, low, high), 1.0, 0.0).astype(BF16)
        dp = nt(vp[:, low:high], gp[:, low:high] * mask)
        dprob[rows, :] = dp
        sums.append(jnp.sum(weight[rows, :] * dp, axis=0, keepdims=True))
    d = jnp.concatenate(sums, axis=0)
    d0[...] = d
    d01[...] = pick_stat(p, d, 0.0)


def cut(p, block, start, count):
    if start % 16 or count % 16:
        block = block.astype(F32)
    return block[start : start + count]


def both_cores(own, other):
    return jnp.concatenate([own[...], other[...]], axis=0)


def by_head(rows, group):
    first, end, low, high = group
    parts = []
    for h in range(first, end):
        mask = jnp.where(window_mask(h, low, high), 1.0, 0.0).astype(BF16)
        parts.append(rows[:, low:high] * mask)
    return jnp.concatenate(parts, axis=0)


def against(p, cols, rows):
    parts = []
    for group in head_groups(p):
        low, high = group[2:]
        parts.append(nt(cols[:, low:high], by_head(rows, group)))
    return jnp.concatenate(parts, axis=1)


def collect(p, weights, rows, out):
    count = rows.shape[0]
    for group in head_groups(p):
        first, end, low, high = group
        part = nn(weights[:, first * count : end * count], by_head(rows, group))
        out[:, low:high] += part


def near_blocks(p, half, kv):
    blocks = [cut(p, ref[...], half * p.n1, p.n1) for ref in kv[: p.g1 // 2]]
    return jnp.concatenate(blocks, axis=0).astype(BF16)


def wide_blocks(p, half, kv):
    blocks = [cut(p, ref[...], half * ref.shape[0] // 2, p.n2) for ref in kv]
    return jnp.concatenate(blocks, axis=0).astype(BF16)


def soft(p, scores, e, tops, sums):
    top = jnp.maximum(jnp.max(scores, axis=0, keepdims=True), LOWEST)
    weight = jnp.exp2(scores - top)
    e[...] = weight
    tops[...] = by_rows(p, top)
    sums[...] = by_rows(p, jnp.sum(weight, axis=0, keepdims=True))


def near_kernel(p, q_own, q_other, *refs):
    kv, outs = refs[: p.g1 // 2], refs[p.g1 // 2 :]
    d = lax.axis_index("seq")
    n1, n2 = p.n1, p.n2
    row = iota((p.g1 // 2 * n1, 1), 0)
    col = iota((1, 2 * p.heads * n1), 1)
    head = first_head(p) + col // (2 * n1)
    own = col % n1
    device = jnp.bitwise_xor(d, col // n1 % 2)
    qpos = p.tokens * device + p.r2 * (own % n2) + (head + DIL1 * (own // n2)) % p.r2
    other = row % n1
    kbase = p.tokens * jnp.bitwise_xor(d, 2 * (row // n1)) + p.r2 * (other % n2)
    kpos = kbase + jnp.bitwise_and(head + DIL1 * (other // n2), p.r2 - 1)
    s = against(p, near_blocks(p, 0, kv), both_cores(q_own, q_other)) * SCALE2
    soft(p, jnp.where(kpos <= qpos, s, -jnp.inf), *outs)


def wide_kernel(p, q_own, q_other, *refs):
    kv, outs = refs[: p.g2 // 2], refs[p.g2 // 2 :]
    d = lax.axis_index("seq")
    n1, n2 = p.n1, p.n2
    row = iota((p.g2 // 2 * n2, 1), 0)
    row = jnp.bitwise_xor(d, 2 * (row // n2)) * n2 + row % n2
    col = iota((1, 2 * p.heads * n1), 1)
    last = jnp.bitwise_xor(d, col // n1 % 2) * n2 + col % n1
    last = jnp.where(col % n1 < n2, last, -1)
    s = against(p, wide_blocks(p, 0, kv), both_cores(q_own, q_other)) * SCALE2
    soft(p, jnp.where(row <= last, s, -jnp.inf), *outs)


def delta_kernel(p, g_own, g_other, e1, e2, top1, sum1, top2, sum2, lse01, d01, *refs):
    kv, (dp1, dp2, stats) = refs[: p.g2 // 2], refs[p.g2 // 2 :]
    g = both_cores(g_own, g_other)
    dp = against(p, near_blocks(p, 1, kv), g)
    dp1[...] = dp
    near = by_rows(p, jnp.sum(e1[...] * dp, axis=0, keepdims=True))
    dp = against(p, wide_blocks(p, 1, kv), g)
    dp2[...] = dp
    wide = by_rows(p, jnp.sum(e2[...] * dp, axis=0, keepdims=True))

    peak = jnp.maximum(top1[...], top2[...])
    up1, up2 = jnp.exp2(top1[...] - peak), jnp.exp2(top2[...] - peak)
    both = jnp.maximum(sum1[...] * up1 + sum2[...] * up2, TINY)
    d = (near * up1 + wide * up2) / both
    total, delta = join(lse01[...], d01[...], peak + jnp.log2(both), d)
    stats[...] = jnp.concatenate([total, delta], axis=0)


def join(lse_a, d_a, lse_b, d_b):
    peak = jnp.maximum(lse_a, lse_b)
    total = peak + jnp.log2(jnp.exp2(lse_a - peak) + jnp.exp2(lse_b - peak))
    return total, jnp.exp2(lse_a - total) * d_a + jnp.exp2(lse_b - total) * d_b


def levels_kernel(
    p, q_own, q_other, g_own, g_other, e1, e2, top1, top2, dp1, dp2, mine, theirs, *refs
):
    ds1, ds2, total1, delta1, own_part = refs[:5]
    outs, (dk1, dv1, dk2, dv2) = refs[5:-4], refs[-4:]
    n1, n2 = p.n1, p.n2
    came = pltpu.roll(theirs[...], n1, 1)
    total, delta = join(mine[: p.heads, :], mine[p.heads :, :], came[: p.heads], came[p.heads :])
    total1[...] = total
    delta1[...] = delta
    delta = along(p, delta)
    q, g = both_cores(q_own, q_other), both_cores(g_own, g_other)
    for ref in (dk1, dv1, dk2, dv2):
        ref[...] = jnp.zeros_like(ref)
    for e, top, dp, kept, dk, dv in ((e1, top1, dp1, ds1, dk1, dv1), (e2, top2, dp2, ds2, dk2, dv2)):
        prob = e[...] * along(p, jnp.exp2(top[...] - total))
        ds = (prob * (dp[...] - delta) * SCALE).astype(BF16)
        kept[...] = ds
        collect(p, prob.astype(BF16), g, dv)
        collect(p, ds, q, dk)
    for i in range(p.g2 // 2):
        rows = slice(i * n2, (i + 1) * n2)
        if 2 * i < p.g1:
            head = slice(i * n1, i * n1 + n2)
            rest = slice(i * n1 + n2, (i + 1) * n1)
            part = []
            for near, wide in ((dk1, dk2), (dv1, dv2)):
                part += [near[head, :] + wide[rows, :], near[rest, :]]
        else:
            part = [dk2[rows, :], dv2[rows, :]]
        part = jnp.concatenate(part, axis=0)
        ref = outs[i - 1] if i else own_part
        ref[...] = part.astype(ref.dtype)


def queries_kernel(p, ds1, ds2, *refs):
    kv, (dq_own, dq_low, dq_high, dq) = refs[: p.g2 // 2], refs[p.g2 // 2 :]
    k1, k2 = near_blocks(p, 0, kv), wide_blocks(p, 0, kv)
    count = 2 * p.n1
    for first, end, low, high in head_groups(p):
        columns = slice(first * count, end * count)
        part = tn(ds1[:, columns], k1[:, low:high]) + tn(ds2[:, columns], k2[:, low:high])
        for h in range(first, end):
            low_h, high_h = window(h)
            at = (h - first) * count
            piece = part[at : at + count, low_h - low : high_h - low]
            hit = window_mask(h, low_h, high_h)
            dq[:, low_h:high_h] = jnp.where(hit, piece, dq[:, low_h:high_h])
    dq_own[...] = dq[: p.n1, :]
    half = p.n1 // 2
    dq_low[...] = dq[p.n1 : p.n1 + half, :].astype(BF16)
    dq_high[...] = dq[p.n1 + half :, :].astype(BF16)


def own_grad_kernel(
    p, qp, kp, gp, weight, dprob, lse0, d0, total1, delta1, own_part, dq, dk0, dv0
):
    lse = lse0[...]
    share = jnp.exp2(lse - spread_stat(p, total1[...], lse))
    delta = spread_stat(p, delta1[...], d0[...])
    zero = jnp.zeros((p.tokens, p.width), F32)
    dk0[...] = spread(p, own_part[: p.n1, :], column_class(p), zero)
    dv0[...] = spread(p, own_part[p.n1 :, :], column_class(p), zero)
    for h in range(p.heads):
        low, high = window(h)
        rows = slice(h * p.tokens, (h + 1) * p.tokens)
        hit = window_mask(h, low, high)
        mask = jnp.where(hit, 1.0, 0.0).astype(BF16)
        prob = weight[rows, :] * share[h : h + 1, :]
        ds = (prob * (dprob[rows, :] - delta[h : h + 1, :]) * SCALE).astype(BF16)
        dq[:, low:high] = jnp.where(hit, tn(ds, kp[:, low:high]), dq[:, low:high])
        dk0[:, low:high] += nn(ds, qp[:, low:high] * mask)
        dv0[:, low:high] += nn(prob.astype(BF16), gp[:, low:high] * mask)


def finish_kernel(p, dq, dq_own, dq_low, dq_high, grad_q):
    kept = dq_own[...] + both_cores(dq_low, dq_high).astype(F32)
    zero = jnp.zeros((p.tokens, p.width), F32)
    whole = dq[...] + spread(p, kept, column_class(p), zero)
    grad_q[...] = nn(phase_order(p, True), whole.astype(BF16)).astype(BF16)


def last_kernel(p, dk0, dv0, *refs):
    came, (grad_k, grad_v, out_k, out_v, sems) = refs[:-5], refs[-5:]
    order = phase_order(p, True)
    label = column_class(p)
    zero = jnp.zeros((p.tokens, p.width), F32)
    copies = []
    for index, (base, out, grad) in enumerate(((dk0, out_k, grad_k), (dv0, out_v, grad_v))):
        first = jnp.zeros((p.n2, p.width), F32)
        rest = jnp.zeros((p.n1 - p.n2, p.width), F32)
        for ref in came:
            half = ref.shape[0] // 2
            block = ref[...].astype(F32)
            first = first + block[index * half : index * half + p.n2]
            if half == p.n1:
                rest = rest + block[index * half + p.n2 : (index + 1) * half]
        kept = jnp.concatenate([first, rest], axis=0)
        whole = base[...] + spread(p, kept, label, zero)
        out[...] = nn(order, whole.astype(BF16)).astype(BF16)
        copies.append(pltpu.make_async_copy(out, grad, sems.at[index]))
        copies[-1].start()
    for copy in copies:
        copy.wait()


def swap(block, axis, bits):
    count = lax.axis_size(axis)
    return lax.ppermute(block, axis, [(i, i ^ bits) for i in range(count)])


def body(queries, keys, values, grad_out):
    tokens, width = queries.shape
    queries, keys, values, grad_out = (
        pltpu.with_memory_space_constraint(field, pltpu.HBM)
        for field in (queries, keys, values, grad_out)
    )
    p = Plan(tokens, width, lax.axis_size("seq"), lax.axis_size("head"))
    n1, n2 = p.n1, p.n2
    run = lambda kernel: functools.partial(kernel, p)
    row, kept = (tokens, width), (n1, width)
    share = (tokens // p.zcount, width)
    stat, stat1 = (p.heads, tokens), (p.heads, 2 * n1)
    flat = lambda count: (count, tokens)
    even = range(0, p.g2, 2)
    half_rows = sum(p.rows[::2])
    hbm = pl.BlockSpec(memory_space=pltpu.HBM)

    outs = call(
        run(pack_kernel),
        [(row, BF16)] * 3
        + [(kept, BF16), ((2 * n1, width), BF16), ((2 * n2, width), BF16)]
        + [(share, BF16)] * p.zcount,
        [(row, BF16)] * 3 + [pltpu.SemaphoreType.DMA((p.zcount + 3,))],
        in_specs=[hbm] * 4,
    )(queries, keys, values, grad_out)
    qp, kp, vp, q1, kv1, kv2 = outs[:6]
    gz = outs[6:]
    gz = [gz[0]] + [swap(gz[b], "head", b) for b in range(1, p.zcount)]

    kv = [kv1] + [swap(kv1 if b < p.g1 else kv2, "seq", b) for b in even[1:]]

    q_other = swap(q1, "seq", 1)
    weight, lse0, lse01 = call(
        run(own_scores_kernel), [(flat(p.heads * tokens), F32), (stat, F32), (stat1, F32)]
    )(qp, kp, q_other)
    near = (p.g1 // 2 * n1, 2 * p.heads * n1)
    wide = (p.g2 // 2 * n2, 2 * p.heads * n1)
    e1, top1, sum1 = call(run(near_kernel), [(near, F32)] + [(stat1, F32)] * 2)(
        q1, q_other, *kv[: p.g1 // 2]
    )
    e2, top2, sum2 = call(run(wide_kernel), [(wide, F32)] + [(stat1, F32)] * 2)(
        q1, q_other, *kv
    )
    gp, g1 = call(run(gather_kernel), [(row, BF16), (kept, BF16)], [(row, BF16)])(
        lse01, *gz[::-1]
    )
    g_other = swap(g1, "seq", 1)
    dprob, d0, d01 = call(
        run(own_delta_kernel), [(flat(p.heads * tokens), F32), (stat, F32), (stat1, F32)]
    )(vp, weight, gp)
    dp1, dp2, mine = call(
        run(delta_kernel), [(near, F32), (wide, F32), ((2 * p.heads, 2 * n1), F32)]
    )(g1, g_other, e1, e2, top1, sum1, top2, sum2, lse01, d01, *kv)
    theirs = swap(mine, "seq", 1)
    part = lambda b, dtype: ((p.rows[b], width), dtype)
    outs = call(
        run(levels_kernel),
        [(near, BF16), (wide, BF16), (stat1, F32), (stat1, F32), part(0, F32)]
        + [part(b, BF16) for b in even[1:]],
        [((near[0], width), F32)] * 2 + [((wide[0], width), F32)] * 2,
    )(q1, q_other, g1, g_other, e1, e2, top1, top2, dp1, dp2, mine, theirs)
    ds1, ds2, total1, delta1, own_part = outs[:5]
    parts = [swap(s, "seq", b) for s, b in zip(outs[5:], even[1:])]
    dq_own, *dq_other = call(
        run(queries_kernel),
        [(kept, F32)] + [((n1 // 2, width), BF16)] * 2,
        [((2 * n1, width), F32)],
    )(ds1, ds2, *kv)
    dq_came = [swap(half, "seq", 1) for half in dq_other]
    dq, dk0, dv0 = call(run(own_grad_kernel), [(row, F32)] * 3)(
        qp, kp, gp, weight, dprob, lse0, d0, total1, delta1, own_part
    )
    (grad_q,) = call(run(finish_kernel), [(row, BF16)])(dq, dq_own, *dq_came)
    grad_k, grad_v = call(
        run(last_kernel),
        [(row, BF16)] * 2,
        [(row, BF16)] * 2 + [pltpu.SemaphoreType.DMA((2,))],
        out_specs=[hbm] * 2,
    )(dk0, dv0, *parts)
    return grad_q, grad_k, grad_v


def solution(mesh):
    return jax.shard_map(
        body,
        mesh=mesh,
        in_specs=(P("seq", "head"), P("seq", "head"), P("seq", "head"), P(("seq", "head"), None)),
        out_specs=(P("seq", "head"), P("seq", "head"), P("seq", "head")),
        check_vma=False,
    )
```

```python
import functools
import math

import jax
import jax.numpy as jnp
from jax import lax
from jax.experimental import pallas as pl
from jax.experimental.pallas import tpu as pltpu
from jax.sharding import PartitionSpec as P

HD = 80
SPAN1 = 4
DIL1 = 4
WIDEST = 32
LANES = 128
BF16 = jnp.bfloat16
F32 = jnp.float32
SCALE = HD**-0.5
SCALE2 = SCALE * math.log2(math.e)
VMEM_BYTES = 28 * 2**20
LOWEST = -1e30
TINY = 1e-30


class Plan:
    def __init__(self, tokens, width, seq_count, head_count):
        self.tokens = tokens
        self.width = width
        self.heads = width // HD
        self.g1 = SPAN1
        self.g2 = min(WIDEST, seq_count)
        self.r2 = self.g2
        self.n1 = tokens // DIL1
        self.n2 = tokens // self.r2
        self.turns = self.r2 // DIL1
        self.zcount = head_count
        self.rows = [2 * (self.n1 if b < self.g1 else self.n2) for b in range(self.g2)]


def nt(a, b):
    return lax.dot_general(a, b, (((1,), (1,)), ((), ())), preferred_element_type=F32)


def nn(a, b):
    return lax.dot_general(a, b, (((1,), (0,)), ((), ())), preferred_element_type=F32)


def tn(a, b):
    return lax.dot_general(a, b, (((0,), (0,)), ((), ())), preferred_element_type=F32)


def iota(shape, dim):
    return lax.broadcasted_iota(jnp.int32, shape, dim)


def phase_order(p, inverse=False):
    shape = (p.tokens, p.tokens)
    row, col = (iota(shape, 1), iota(shape, 0)) if inverse else (iota(shape, 0), iota(shape, 1))
    return jnp.where(col == p.r2 * (row % p.n2) + row // p.n2, 1.0, 0.0).astype(BF16)


def first_head(p):
    return lax.axis_index("head") * p.heads


def column_class(p):
    return (first_head(p) + iota((1, p.width), 1) // HD) % p.r2


def row_class(p):
    return (first_head(p) + iota((p.heads, 1), 0)) % p.r2


def tiles(p):
    out = []
    for low in range(0, p.width, LANES):
        high = min(low + LANES, p.width)
        out.append((low, high, range(low // HD, -(-high // HD))))
    return out


def pick(p, whole, label):
    parts = []
    for t in range(p.turns):
        if p.heads % p.r2 == 0:
            lanes = []
            for low, high, heads in tiles(p):
                lane = low + iota((1, high - low), 1)
                part = None
                for h in heads:
                    c = (h + DIL1 * t) % p.r2
                    rows = whole[c * p.n2 : (c + 1) * p.n2, low:high]
                    part = rows if part is None else jnp.where(lane >= h * HD, rows, part)
                lanes.append(part)
            parts.append(jnp.concatenate(lanes, axis=1))
            continue
        want = (label + DIL1 * t) % p.r2
        part = jnp.zeros((p.n2, whole.shape[1]), F32)
        for c in range(p.r2):
            part = jnp.where(want == c, whole[c * p.n2 : (c + 1) * p.n2], part)
        parts.append(part)
    return jnp.concatenate(parts, axis=0)


def spread(p, kept, label, base):
    parts = []
    for c in range(p.r2):
        rows = slice(c * p.n2, (c + 1) * p.n2)
        if p.heads % p.r2 == 0:
            lanes = []
            for low, high, heads in tiles(p):
                lane = low + iota((1, high - low), 1)
                part = base[rows, low:high]
                for t in range(p.turns):
                    for h in heads:
                        if (h + DIL1 * t) % p.r2 == c:
                            hit = (lane >= h * HD) & (lane < (h + 1) * HD)
                            moved = kept[t * p.n2 : (t + 1) * p.n2, low:high]
                            part = jnp.where(hit, moved, part)
                lanes.append(part)
            parts.append(jnp.concatenate(lanes, axis=1))
            continue
        part = base[rows]
        for t in range(p.turns):
            hit = (label + DIL1 * t) % p.r2 == c
            part = jnp.where(hit, kept[t * p.n2 : (t + 1) * p.n2], part)
        parts.append(part)
    return jnp.concatenate(parts, axis=0)


def window(h):
    low = h * HD // LANES * LANES
    high = -(-(h + 1) * HD // LANES) * LANES
    return low, high


def window_mask(h, low, high):
    lane = low + iota((1, high - low), 1)
    return (lane >= h * HD) & (lane < (h + 1) * HD)


def head_groups(p):
    groups, h = [], 0
    while h < p.heads:
        low, high = window(h)
        end = h + 1
        while end < p.heads and window(end)[1] - low <= 2 * LANES:
            high = window(end)[1]
            end += 1
        groups.append((h, end, low, high))
        h = end
    return groups


def head_mask(p, h):
    lane = iota((1, p.width), 1)
    return (lane >= h * HD) & (lane < (h + 1) * HD)


def own_bias(p):
    shape = (p.tokens, p.tokens)
    key, query = iota(shape, 0), iota(shape, 1)
    qpos = p.r2 * (query % p.n2) + query // p.n2
    kpos = p.r2 * (key % p.n2) + key // p.n2
    return jnp.where(qpos >= kpos, 0.0, -jnp.inf)


def pick_stat(p, stat, fill):
    lane = iota((1, 2 * p.n1), 1)
    label = row_class(p)
    out = jnp.full((p.heads, 2 * p.n1), fill, F32)
    for t in range(p.turns):
        here = (lane >= t * p.n2) & (lane < (t + 1) * p.n2)
        for c in range(p.r2):
            moved = pltpu.roll(stat, (t - c) * p.n2 % p.tokens, 1)[:, : 2 * p.n1]
            out = jnp.where(here & ((label + DIL1 * t) % p.r2 == c), moved, out)
    return out


def spread_stat(p, kept, base):
    lane = iota((1, p.tokens), 1)
    label = row_class(p)
    padded = jnp.concatenate([kept] * (p.tokens // kept.shape[1]), axis=1)
    out = base
    for t in range(p.turns):
        for c in range(p.r2):
            moved = pltpu.roll(padded, (c - t) * p.n2 % p.tokens, 1)
            here = (lane >= c * p.n2) & (lane < (c + 1) * p.n2)
            out = jnp.where(here & ((label + DIL1 * t) % p.r2 == c), moved, out)
    return out


def by_rows(p, flat):
    count = flat.shape[1] // p.heads
    return jnp.concatenate([flat[:, h * count : (h + 1) * count] for h in range(p.heads)], axis=0)


def along(p, stat):
    return jnp.concatenate([stat[h : h + 1, :] for h in range(p.heads)], axis=1)


def call(kernel, outs, scratch=(), flops=0, **specs):
    return pl.pallas_call(
        kernel,
        out_shape=[jax.ShapeDtypeStruct(s, d) for s, d in outs],
        scratch_shapes=[pltpu.VMEM(*s) if isinstance(s, tuple) else s for s in scratch],
        compiler_params=pltpu.CompilerParams(vmem_limit_bytes=VMEM_BYTES),
        cost_estimate=pl.CostEstimate(flops=flops, bytes_accessed=2**20, transcendentals=0),
        **specs,
    )


def slab(p, g_ref, b):
    start = pl.multiple_of(jnp.bitwise_xor(lax.axis_index("head"), b) * p.width, LANES)
    return g_ref.at[:, pl.ds(start, p.width)]


def pack_kernel(p, q_ref, k_ref, v_ref, g_ref, qp, kp, vp, q1, kv1, kv2, *refs):
    gz, (q_in, k_in, v_in, sems) = refs[: p.zcount], refs[p.zcount :]
    loads = [(k_ref, k_in), (v_ref, v_in), (q_ref, q_in)]
    loads += [(slab(p, g_ref, b), gz[b]) for b in range(p.zcount)]
    copies = [pltpu.make_async_copy(src, dst, sems.at[i]) for i, (src, dst) in enumerate(loads)]
    for copy in copies:
        copy.start()
    order = phase_order(p)
    label = column_class(p)
    copies[0].wait()
    k = nn(order, k_in[...])
    kp[...] = k.astype(BF16)
    k_kept = pick(p, k, label)
    copies[1].wait()
    v = nn(order, v_in[...])
    vp[...] = v.astype(BF16)
    v_kept = pick(p, v, label)
    kv1[...] = jnp.concatenate([k_kept, v_kept], axis=0).astype(BF16)
    kv2[...] = jnp.concatenate([k_kept[: p.n2], v_kept[: p.n2]], axis=0).astype(BF16)
    copies[2].wait()
    q = nn(order, q_in[...])
    qp[...] = q.astype(BF16)
    q1[...] = pick(p, q, label).astype(BF16)
    for copy in copies[3:]:
        copy.wait()


def own_scores_kernel(p, qp, kp, after, weight, lse0, lse01):
    bias = own_bias(p)
    rows = []
    for h in range(p.heads):
        low, high = window(h)
        mask = jnp.where(window_mask(h, low, high), 1.0, 0.0).astype(BF16)
        s = nt(kp[:, low:high], qp[:, low:high] * mask) * SCALE2 + bias
        top = jnp.max(s, axis=0, keepdims=True)
        e = jnp.exp2(s - top)
        denom = jnp.sum(e, axis=0, keepdims=True)
        weight[h * p.tokens : (h + 1) * p.tokens, :] = e * (1.0 / denom)
        rows.append(top + jnp.log2(denom))
    lse = jnp.concatenate(rows, axis=0)
    lse0[...] = lse
    lse01[...] = pick_stat(p, lse, LOWEST)


def block_order(p):
    half = p.zcount // 2
    return [half, *range(1, half), *range(half + 1, p.zcount), 0]


def gather_kernel(p, after, *refs):
    gz, (gp, g1, natural) = refs[: p.zcount], refs[p.zcount :]
    z = lax.axis_index("head")
    share = p.tokens // p.zcount
    for b, ref in zip(block_order(p), gz):
        start = pl.multiple_of(jnp.bitwise_xor(z, b) * share, share)
        natural[pl.ds(start, share), :] = ref[...]
    g = nn(phase_order(p), natural[...])
    gp[...] = g.astype(BF16)
    g1[...] = pick(p, g, column_class(p)).astype(BF16)


def own_delta_kernel(p, vp, weight, gp, dprob, d0, d01):
    sums = []
    for h in range(p.heads):
        low, high = window(h)
        rows = slice(h * p.tokens, (h + 1) * p.tokens)
        mask = jnp.where(window_mask(h, low, high), 1.0, 0.0).astype(BF16)
        dp = nt(vp[:, low:high], gp[:, low:high] * mask)
        dprob[rows, :] = dp
        sums.append(jnp.sum(weight[rows, :] * dp, axis=0, keepdims=True))
    d = jnp.concatenate(sums, axis=0)
    d0[...] = d
    d01[...] = pick_stat(p, d, 0.0)


def cut(p, block, start, count):
    if start % 16 or count % 16:
        block = block.astype(F32)
    return block[start : start + count]


def both_cores(own, other):
    return jnp.concatenate([own[...], other[...]], axis=0)


def by_head(rows, group):
    first, end, low, high = group
    parts = []
    for h in range(first, end):
        mask = jnp.where(window_mask(h, low, high), 1.0, 0.0).astype(BF16)
        parts.append(rows[:, low:high] * mask)
    return jnp.concatenate(parts, axis=0)


def against(p, cols, rows):
    parts = []
    for group in head_groups(p):
        low, high = group[2:]
        parts.append(nt(cols[:, low:high], by_head(rows, group)))
    return jnp.concatenate(parts, axis=1)


def collect(p, weights, rows, out):
    count = rows.shape[0]
    for group in head_groups(p):
        first, end, low, high = group
        part = nn(weights[:, first * count : end * count], by_head(rows, group))
        out[:, low:high] += part


def near_blocks(p, half, kv):
    blocks = [cut(p, ref[...], half * p.n1, p.n1) for ref in kv[: p.g1 // 2]]
    return jnp.concatenate(blocks, axis=0).astype(BF16)


def wide_blocks(p, half, kv):
    blocks = [cut(p, ref[...], half * ref.shape[0] // 2, p.n2) for ref in kv]
    return jnp.concatenate(blocks, axis=0).astype(BF16)


def soft(p, scores, e, tops, sums):
    top = jnp.maximum(jnp.max(scores, axis=0, keepdims=True), LOWEST)
    weight = jnp.exp2(scores - top)
    e[...] = weight
    tops[...] = by_rows(p, top)
    sums[...] = by_rows(p, jnp.sum(weight, axis=0, keepdims=True))


def near_kernel(p, q_own, q_other, *refs):
    kv, outs = refs[: p.g1 // 2], refs[p.g1 // 2 :]
    d = lax.axis_index("seq")
    n1, n2 = p.n1, p.n2
    row = iota((p.g1 // 2 * n1, 1), 0)
    col = iota((1, 2 * p.heads * n1), 1)
    head = first_head(p) + col // (2 * n1)
    own = col % n1
    device = jnp.bitwise_xor(d, col // n1 % 2)
    qpos = p.tokens * device + p.r2 * (own % n2) + (head + DIL1 * (own // n2)) % p.r2
    other = row % n1
    kbase = p.tokens * jnp.bitwise_xor(d, 2 * (row // n1)) + p.r2 * (other % n2)
    kpos = kbase + jnp.bitwise_and(head + DIL1 * (other // n2), p.r2 - 1)
    s = against(p, near_blocks(p, 0, kv), both_cores(q_own, q_other)) * SCALE2
    soft(p, jnp.where(kpos <= qpos, s, -jnp.inf), *outs)


def wide_kernel(p, q_own, q_other, *refs):
    kv, outs = refs[: p.g2 // 2], refs[p.g2 // 2 :]
    d = lax.axis_index("seq")
    n1, n2 = p.n1, p.n2
    row = iota((p.g2 // 2 * n2, 1), 0)
    row = jnp.bitwise_xor(d, 2 * (row // n2)) * n2 + row % n2
    col = iota((1, 2 * p.heads * n1), 1)
    last = jnp.bitwise_xor(d, col // n1 % 2) * n2 + col % n1
    last = jnp.where(col % n1 < n2, last, -1)
    s = against(p, wide_blocks(p, 0, kv), both_cores(q_own, q_other)) * SCALE2
    soft(p, jnp.where(row <= last, s, -jnp.inf), *outs)


def delta_kernel(p, g_own, g_other, e1, e2, top1, sum1, top2, sum2, lse01, d01, *refs):
    kv, (dp1, dp2, stats) = refs[: p.g2 // 2], refs[p.g2 // 2 :]
    g = both_cores(g_own, g_other)
    dp = against(p, near_blocks(p, 1, kv), g)
    dp1[...] = dp
    near = by_rows(p, jnp.sum(e1[...] * dp, axis=0, keepdims=True))
    dp = against(p, wide_blocks(p, 1, kv), g)
    dp2[...] = dp
    wide = by_rows(p, jnp.sum(e2[...] * dp, axis=0, keepdims=True))

    peak = jnp.maximum(top1[...], top2[...])
    up1, up2 = jnp.exp2(top1[...] - peak), jnp.exp2(top2[...] - peak)
    both = jnp.maximum(sum1[...] * up1 + sum2[...] * up2, TINY)
    d = (near * up1 + wide * up2) / both
    total, delta = join(lse01[...], d01[...], peak + jnp.log2(both), d)
    stats[...] = jnp.concatenate([total, delta], axis=0)


def join(lse_a, d_a, lse_b, d_b):
    peak = jnp.maximum(lse_a, lse_b)
    total = peak + jnp.log2(jnp.exp2(lse_a - peak) + jnp.exp2(lse_b - peak))
    return total, jnp.exp2(lse_a - total) * d_a + jnp.exp2(lse_b - total) * d_b


def levels_kernel(
    p, q_own, q_other, g_own, g_other, e1, e2, top1, top2, dp1, dp2, mine, theirs, *refs
):
    ds1, ds2, total1, delta1, own_part = refs[:5]
    outs, (dk1, dv1, dk2, dv2) = refs[5:-4], refs[-4:]
    n1, n2 = p.n1, p.n2
    came = pltpu.roll(theirs[...], n1, 1)
    total, delta = join(mine[: p.heads, :], mine[p.heads :, :], came[: p.heads], came[p.heads :])
    total1[...] = total
    delta1[...] = delta
    delta = along(p, delta)
    q, g = both_cores(q_own, q_other), both_cores(g_own, g_other)
    for ref in (dk1, dv1, dk2, dv2):
        ref[...] = jnp.zeros_like(ref)
    for e, top, dp, kept, dk, dv in ((e1, top1, dp1, ds1, dk1, dv1), (e2, top2, dp2, ds2, dk2, dv2)):
        prob = e[...] * along(p, jnp.exp2(top[...] - total))
        ds = (prob * (dp[...] - delta) * SCALE).astype(BF16)
        kept[...] = ds
        collect(p, prob.astype(BF16), g, dv)
        collect(p, ds, q, dk)
    for i in range(p.g2 // 2):
        rows = slice(i * n2, (i + 1) * n2)
        if 2 * i < p.g1:
            head = slice(i * n1, i * n1 + n2)
            rest = slice(i * n1 + n2, (i + 1) * n1)
            part = []
            for near, wide in ((dk1, dk2), (dv1, dv2)):
                part += [near[head, :] + wide[rows, :], near[rest, :]]
        else:
            part = [dk2[rows, :], dv2[rows, :]]
        part = jnp.concatenate(part, axis=0)
        ref = outs[i - 1] if i else own_part
        ref[...] = part.astype(ref.dtype)


def queries_kernel(p, ds1, ds2, *refs):
    kv, (dq_own, dq_low, dq_high, dq) = refs[: p.g2 // 2], refs[p.g2 // 2 :]
    k1, k2 = near_blocks(p, 0, kv), wide_blocks(p, 0, kv)
    count = 2 * p.n1
    for first, end, low, high in head_groups(p):
        columns = slice(first * count, end * count)
        part = tn(ds1[:, columns], k1[:, low:high]) + tn(ds2[:, columns], k2[:, low:high])
        for h in range(first, end):
            low_h, high_h = window(h)
            at = (h - first) * count
            piece = part[at : at + count, low_h - low : high_h - low]
            hit = window_mask(h, low_h, high_h)
            dq[:, low_h:high_h] = jnp.where(hit, piece, dq[:, low_h:high_h])
    dq_own[...] = dq[: p.n1, :]
    half = p.n1 // 2
    dq_low[...] = dq[p.n1 : p.n1 + half, :].astype(BF16)
    dq_high[...] = dq[p.n1 + half :, :].astype(BF16)


def own_grad_kernel(
    p, qp, kp, gp, weight, dprob, lse0, d0, total1, delta1, own_part, dq, dk0, dv0
):
    lse = lse0[...]
    share = jnp.exp2(lse - spread_stat(p, total1[...], lse))
    delta = spread_stat(p, delta1[...], d0[...])
    zero = jnp.zeros((p.tokens, p.width), F32)
    dk0[...] = spread(p, own_part[: p.n1, :], column_class(p), zero)
    dv0[...] = spread(p, own_part[p.n1 :, :], column_class(p), zero)
    for h in range(p.heads):
        low, high = window(h)
        rows = slice(h * p.tokens, (h + 1) * p.tokens)
        hit = window_mask(h, low, high)
        mask = jnp.where(hit, 1.0, 0.0).astype(BF16)
        prob = weight[rows, :] * share[h : h + 1, :]
        ds = (prob * (dprob[rows, :] - delta[h : h + 1, :]) * SCALE).astype(BF16)
        dq[:, low:high] = jnp.where(hit, tn(ds, kp[:, low:high]), dq[:, low:high])
        dk0[:, low:high] += nn(ds, qp[:, low:high] * mask)
        dv0[:, low:high] += nn(prob.astype(BF16), gp[:, low:high] * mask)


def finish_kernel(p, dq, dq_own, dq_low, dq_high, grad_q):
    kept = dq_own[...] + both_cores(dq_low, dq_high).astype(F32)
    zero = jnp.zeros((p.tokens, p.width), F32)
    whole = dq[...] + spread(p, kept, column_class(p), zero)
    grad_q[...] = nn(phase_order(p, True), whole.astype(BF16)).astype(BF16)


def last_kernel(p, dk0, dv0, *refs):
    came, (grad_k, grad_v, out_k, out_v, sems) = refs[:-5], refs[-5:]
    order = phase_order(p, True)
    label = column_class(p)
    zero = jnp.zeros((p.tokens, p.width), F32)
    copies = []
    for index, (base, out, grad) in enumerate(((dk0, out_k, grad_k), (dv0, out_v, grad_v))):
        first = jnp.zeros((p.n2, p.width), F32)
        rest = jnp.zeros((p.n1 - p.n2, p.width), F32)
        for ref in came:
            half = ref.shape[0] // 2
            block = ref[...].astype(F32)
            first = first + block[index * half : index * half + p.n2]
            if half == p.n1:
                rest = rest + block[index * half + p.n2 : (index + 1) * half]
        kept = jnp.concatenate([first, rest], axis=0)
        whole = base[...] + spread(p, kept, label, zero)
        out[...] = nn(order, whole.astype(BF16)).astype(BF16)
        copies.append(pltpu.make_async_copy(out, grad, sems.at[index]))
        copies[-1].start()
    for copy in copies:
        copy.wait()


def swap(block, axis, bits):
    count = lax.axis_size(axis)
    return lax.ppermute(block, axis, [(i, i ^ bits) for i in range(count)])


def body(queries, keys, values, grad_out):
    tokens, width = queries.shape
    queries, keys, values, grad_out = (
        pltpu.with_memory_space_constraint(field, pltpu.HBM)
        for field in (queries, keys, values, grad_out)
    )
    p = Plan(tokens, width, lax.axis_size("seq"), lax.axis_size("head"))
    n1, n2 = p.n1, p.n2
    run = lambda kernel: functools.partial(kernel, p)
    row, kept = (tokens, width), (n1, width)
    share = (tokens // p.zcount, width)
    stat, stat1 = (p.heads, tokens), (p.heads, 2 * n1)
    flat = lambda count: (count, tokens)
    even = range(0, p.g2, 2)
    half_rows = sum(p.rows[::2])
    hbm = pl.BlockSpec(memory_space=pltpu.HBM)

    outs = call(
        run(pack_kernel),
        [(row, BF16)] * 3
        + [(kept, BF16), ((2 * n1, width), BF16), ((2 * n2, width), BF16)]
        + [(share, BF16)] * p.zcount,
        [(row, BF16)] * 3 + [pltpu.SemaphoreType.DMA((p.zcount + 3,))],
        in_specs=[hbm] * 4,
    )(queries, keys, values, grad_out)
    qp, kp, vp, q1, kv1, kv2 = outs[:6]
    gz = outs[6:]
    gz = [gz[0]] + [swap(gz[b], "head", b) for b in range(1, p.zcount)]

    kv = [kv1] + [swap(kv1 if b < p.g1 else kv2, "seq", b) for b in even[1:]]

    q_other = swap(q1, "seq", 1)
    weight, lse0, lse01 = call(
        run(own_scores_kernel), [(flat(p.heads * tokens), F32), (stat, F32), (stat1, F32)]
    )(qp, kp, q_other)
    near = (p.g1 // 2 * n1, 2 * p.heads * n1)
    wide = (p.g2 // 2 * n2, 2 * p.heads * n1)
    e1, top1, sum1 = call(run(near_kernel), [(near, F32)] + [(stat1, F32)] * 2)(
        q1, q_other, *kv[: p.g1 // 2]
    )
    e2, top2, sum2 = call(run(wide_kernel), [(wide, F32)] + [(stat1, F32)] * 2)(
        q1, q_other, *kv
    )
    gp, g1 = call(run(gather_kernel), [(row, BF16), (kept, BF16)], [(row, BF16)])(
        lse01, *[gz[b] for b in block_order(p)]
    )
    g_other = swap(g1, "seq", 1)
    dprob, d0, d01 = call(
        run(own_delta_kernel), [(flat(p.heads * tokens), F32), (stat, F32), (stat1, F32)]
    )(vp, weight, gp)
    dp1, dp2, mine = call(
        run(delta_kernel), [(near, F32), (wide, F32), ((2 * p.heads, 2 * n1), F32)]
    )(g1, g_other, e1, e2, top1, sum1, top2, sum2, lse01, d01, *kv)
    theirs = swap(mine, "seq", 1)
    part = lambda b, dtype: ((p.rows[b], width), dtype)
    outs = call(
        run(levels_kernel),
        [(near, BF16), (wide, BF16), (stat1, F32), (stat1, F32), part(0, F32)]
        + [part(b, BF16) for b in even[1:]],
        [((near[0], width), F32)] * 2 + [((wide[0], width), F32)] * 2,
    )(q1, q_other, g1, g_other, e1, e2, top1, top2, dp1, dp2, mine, theirs)
    ds1, ds2, total1, delta1, own_part = outs[:5]
    parts = [swap(s, "seq", b) for s, b in zip(outs[5:], even[1:])]
    dq_own, *dq_other = call(
        run(queries_kernel),
        [(kept, F32)] + [((n1 // 2, width), BF16)] * 2,
        [((2 * n1, width), F32)],
    )(ds1, ds2, *kv)
    dq_came = [swap(half, "seq", 1) for half in dq_other]
    dq, dk0, dv0 = call(run(own_grad_kernel), [(row, F32)] * 3)(
        qp, kp, gp, weight, dprob, lse0, d0, total1, delta1, own_part
    )
    (grad_q,) = call(run(finish_kernel), [(row, BF16)])(dq, dq_own, *dq_came)
    grad_k, grad_v = call(
        run(last_kernel),
        [(row, BF16)] * 2,
        [(row, BF16)] * 2 + [pltpu.SemaphoreType.DMA((2,))],
        out_specs=[hbm] * 2,
    )(dk0, dv0, *parts)
    return grad_q, grad_k, grad_v


def solution(mesh):
    return jax.shard_map(
        body,
        mesh=mesh,
        in_specs=(P("seq", "head"), P("seq", "head"), P("seq", "head"), P(("seq", "head"), None)),
        out_specs=(P("seq", "head"), P("seq", "head"), P("seq", "head")),
        check_vma=False,
    )
```

```python
import functools
import math

import jax
import jax.numpy as jnp
from jax import lax
from jax.experimental import pallas as pl
from jax.experimental.pallas import tpu as pltpu
from jax.sharding import PartitionSpec as P

HD = 80
SPAN1 = 4
DIL1 = 4
WIDEST = 32
LANES = 128
BF16 = jnp.bfloat16
F32 = jnp.float32
SCALE = HD**-0.5
SCALE2 = SCALE * math.log2(math.e)
VMEM_BYTES = 28 * 2**20
LOWEST = -1e30
TINY = 1e-30


class Plan:
    def __init__(self, tokens, width, seq_count, head_count):
        self.tokens = tokens
        self.width = width
        self.heads = width // HD
        self.g1 = SPAN1
        self.g2 = min(WIDEST, seq_count)
        self.r2 = self.g2
        self.n1 = tokens // DIL1
        self.n2 = tokens // self.r2
        self.turns = self.r2 // DIL1
        self.zcount = head_count
        self.rows = [2 * (self.n1 if b < self.g1 else self.n2) for b in range(self.g2)]


def nt(a, b):
    return lax.dot_general(a, b, (((1,), (1,)), ((), ())), preferred_element_type=F32)


def nn(a, b):
    return lax.dot_general(a, b, (((1,), (0,)), ((), ())), preferred_element_type=F32)


def tn(a, b):
    return lax.dot_general(a, b, (((0,), (0,)), ((), ())), preferred_element_type=F32)


def iota(shape, dim):
    return lax.broadcasted_iota(jnp.int32, shape, dim)


def phase_order(p, inverse=False):
    shape = (p.tokens, p.tokens)
    row, col = (iota(shape, 1), iota(shape, 0)) if inverse else (iota(shape, 0), iota(shape, 1))
    return jnp.where(col == p.r2 * (row % p.n2) + row // p.n2, 1.0, 0.0).astype(BF16)


def first_head(p):
    return lax.axis_index("head") * p.heads


def column_class(p):
    return (first_head(p) + iota((1, p.width), 1) // HD) % p.r2


def row_class(p):
    return (first_head(p) + iota((p.heads, 1), 0)) % p.r2


def tiles(p):
    out = []
    for low in range(0, p.width, LANES):
        high = min(low + LANES, p.width)
        out.append((low, high, range(low // HD, -(-high // HD))))
    return out


def pick(p, whole, label):
    parts = []
    for t in range(p.turns):
        if p.heads % p.r2 == 0:
            lanes = []
            for low, high, heads in tiles(p):
                lane = low + iota((1, high - low), 1)
                part = None
                for h in heads:
                    c = (h + DIL1 * t) % p.r2
                    rows = whole[c * p.n2 : (c + 1) * p.n2, low:high]
                    part = rows if part is None else jnp.where(lane >= h * HD, rows, part)
                lanes.append(part)
            parts.append(jnp.concatenate(lanes, axis=1))
            continue
        want = (label + DIL1 * t) % p.r2
        part = jnp.zeros((p.n2, whole.shape[1]), F32)
        for c in range(p.r2):
            part = jnp.where(want == c, whole[c * p.n2 : (c + 1) * p.n2], part)
        parts.append(part)
    return jnp.concatenate(parts, axis=0)


def spread(p, kept, label, base):
    parts = []
    for c in range(p.r2):
        rows = slice(c * p.n2, (c + 1) * p.n2)
        if p.heads % p.r2 == 0:
            lanes = []
            for low, high, heads in tiles(p):
                lane = low + iota((1, high - low), 1)
                part = base[rows, low:high]
                for t in range(p.turns):
                    for h in heads:
                        if (h + DIL1 * t) % p.r2 == c:
                            hit = (lane >= h * HD) & (lane < (h + 1) * HD)
                            moved = kept[t * p.n2 : (t + 1) * p.n2, low:high]
                            part = jnp.where(hit, moved, part)
                lanes.append(part)
            parts.append(jnp.concatenate(lanes, axis=1))
            continue
        part = base[rows]
        for t in range(p.turns):
            hit = (label + DIL1 * t) % p.r2 == c
            part = jnp.where(hit, kept[t * p.n2 : (t + 1) * p.n2], part)
        parts.append(part)
    return jnp.concatenate(parts, axis=0)


def window(h):
    low = h * HD // LANES * LANES
    high = -(-(h + 1) * HD // LANES) * LANES
    return low, high


def window_mask(h, low, high):
    lane = low + iota((1, high - low), 1)
    return (lane >= h * HD) & (lane < (h + 1) * HD)


def head_groups(p):
    groups, h = [], 0
    while h < p.heads:
        low, high = window(h)
        end = h + 1
        while end < p.heads and window(end)[1] - low <= 2 * LANES:
            high = window(end)[1]
            end += 1
        groups.append((h, end, low, high))
        h = end
    return groups


def head_mask(p, h):
    lane = iota((1, p.width), 1)
    return (lane >= h * HD) & (lane < (h + 1) * HD)


def own_bias(p):
    shape = (p.tokens, p.tokens)
    key, query = iota(shape, 0), iota(shape, 1)
    qpos = p.r2 * (query % p.n2) + query // p.n2
    kpos = p.r2 * (key % p.n2) + key // p.n2
    return jnp.where(qpos >= kpos, 0.0, -jnp.inf)


def pick_stat(p, stat, fill):
    lane = iota((1, 2 * p.n1), 1)
    label = row_class(p)
    out = jnp.full((p.heads, 2 * p.n1), fill, F32)
    for t in range(p.turns):
        here = (lane >= t * p.n2) & (lane < (t + 1) * p.n2)
        for c in range(p.r2):
            moved = pltpu.roll(stat, (t - c) * p.n2 % p.tokens, 1)[:, : 2 * p.n1]
            out = jnp.where(here & ((label + DIL1 * t) % p.r2 == c), moved, out)
    return out


def spread_stat(p, kept, base):
    lane = iota((1, p.tokens), 1)
    label = row_class(p)
    padded = jnp.concatenate([kept] * (p.tokens // kept.shape[1]), axis=1)
    out = base
    for t in range(p.turns):
        for c in range(p.r2):
            moved = pltpu.roll(padded, (c - t) * p.n2 % p.tokens, 1)
            here = (lane >= c * p.n2) & (lane < (c + 1) * p.n2)
            out = jnp.where(here & ((label + DIL1 * t) % p.r2 == c), moved, out)
    return out


def by_rows(p, flat):
    count = flat.shape[1] // p.heads
    return jnp.concatenate([flat[:, h * count : (h + 1) * count] for h in range(p.heads)], axis=0)


def along(p, stat):
    return jnp.concatenate([stat[h : h + 1, :] for h in range(p.heads)], axis=1)


def call(kernel, outs, scratch=(), flops=0, **specs):
    return pl.pallas_call(
        kernel,
        out_shape=[jax.ShapeDtypeStruct(s, d) for s, d in outs],
        scratch_shapes=[pltpu.VMEM(*s) if isinstance(s, tuple) else s for s in scratch],
        compiler_params=pltpu.CompilerParams(vmem_limit_bytes=VMEM_BYTES),
        cost_estimate=pl.CostEstimate(flops=flops, bytes_accessed=2**20, transcendentals=0),
        **specs,
    )


def slab(p, g_ref, b):
    start = pl.multiple_of(jnp.bitwise_xor(lax.axis_index("head"), b) * p.width, LANES)
    return g_ref.at[:, pl.ds(start, p.width)]


def pack_kernel(p, q_ref, k_ref, v_ref, g_ref, qp, kp, vp, q1, kv1, kv2, *refs):
    gz, (q_in, k_in, v_in, sems) = refs[: p.zcount], refs[p.zcount :]
    loads = [(k_ref, k_in), (v_ref, v_in), (q_ref, q_in)]
    loads += [(slab(p, g_ref, b), gz[b]) for b in range(p.zcount)]
    copies = [pltpu.make_async_copy(src, dst, sems.at[i]) for i, (src, dst) in enumerate(loads)]
    for copy in copies:
        copy.start()
    order = phase_order(p)
    label = column_class(p)
    copies[0].wait()
    k = nn(order, k_in[...])
    kp[...] = k.astype(BF16)
    k_kept = pick(p, k, label)
    copies[1].wait()
    v = nn(order, v_in[...])
    vp[...] = v.astype(BF16)
    v_kept = pick(p, v, label)
    kv1[...] = jnp.concatenate([k_kept, v_kept], axis=0).astype(BF16)
    kv2[...] = jnp.concatenate([k_kept[: p.n2], v_kept[: p.n2]], axis=0).astype(BF16)
    copies[2].wait()
    q = nn(order, q_in[...])
    qp[...] = q.astype(BF16)
    q1[...] = pick(p, q, label).astype(BF16)
    for copy in copies[3:]:
        copy.wait()


def own_scores_kernel(p, first, end, qp, kp, after, weight, lse0):
    bias = own_bias(p)
    rows = []
    for h in range(first, end):
        low, high = window(h)
        mask = jnp.where(window_mask(h, low, high), 1.0, 0.0).astype(BF16)
        s = nt(kp[:, low:high], qp[:, low:high] * mask) * SCALE2 + bias
        top = jnp.max(s, axis=0, keepdims=True)
        e = jnp.exp2(s - top)
        denom = jnp.sum(e, axis=0, keepdims=True)
        at = (h - first) * p.tokens
        weight[at : at + p.tokens, :] = e * (1.0 / denom)
        rows.append(top + jnp.log2(denom))
    lse0[...] = jnp.concatenate(rows, axis=0)


def own_weight(p, low, high, h):
    half = p.heads // 2
    ref, at = (low, h) if h < half else (high, h - half)
    return ref[at * p.tokens : (at + 1) * p.tokens, :]


def block_order(p):
    half = p.zcount // 2
    return [half, *range(1, half), *range(half + 1, p.zcount), 0]


def gather_kernel(p, after, *refs):
    gz, (gp, g1, natural) = refs[: p.zcount], refs[p.zcount :]
    z = lax.axis_index("head")
    share = p.tokens // p.zcount
    for b, ref in zip(block_order(p), gz):
        start = pl.multiple_of(jnp.bitwise_xor(z, b) * share, share)
        natural[pl.ds(start, share), :] = ref[...]
    g = nn(phase_order(p), natural[...])
    gp[...] = g.astype(BF16)
    g1[...] = pick(p, g, column_class(p)).astype(BF16)


def own_delta_kernel(
    p, vp, weight_a, weight_b, lse_a, lse_b, gp, dprob, d0, d01, lse0, lse01
):
    sums = []
    for h in range(p.heads):
        low, high = window(h)
        rows = slice(h * p.tokens, (h + 1) * p.tokens)
        mask = jnp.where(window_mask(h, low, high), 1.0, 0.0).astype(BF16)
        dp = nt(vp[:, low:high], gp[:, low:high] * mask)
        dprob[rows, :] = dp
        weight = own_weight(p, weight_a, weight_b, h)
        sums.append(jnp.sum(weight * dp, axis=0, keepdims=True))
    d = jnp.concatenate(sums, axis=0)
    d0[...] = d
    d01[...] = pick_stat(p, d, 0.0)
    lse = jnp.concatenate([lse_a[...], lse_b[...]], axis=0)
    lse0[...] = lse
    lse01[...] = pick_stat(p, lse, LOWEST)


def cut(p, block, start, count):
    if start % 16 or count % 16:
        block = block.astype(F32)
    return block[start : start + count]


def both_cores(own, other):
    return jnp.concatenate([own[...], other[...]], axis=0)


def by_head(rows, group):
    first, end, low, high = group
    parts = []
    for h in range(first, end):
        mask = jnp.where(window_mask(h, low, high), 1.0, 0.0).astype(BF16)
        parts.append(rows[:, low:high] * mask)
    return jnp.concatenate(parts, axis=0)


def against(p, cols, rows):
    parts = []
    for group in head_groups(p):
        low, high = group[2:]
        parts.append(nt(cols[:, low:high], by_head(rows, group)))
    return jnp.concatenate(parts, axis=1)


def collect(p, weights, rows, out):
    count = rows.shape[0]
    for group in head_groups(p):
        first, end, low, high = group
        part = nn(weights[:, first * count : end * count], by_head(rows, group))
        out[:, low:high] += part


def near_blocks(p, half, kv):
    blocks = [cut(p, ref[...], half * p.n1, p.n1) for ref in kv[: p.g1 // 2]]
    return jnp.concatenate(blocks, axis=0).astype(BF16)


def wide_blocks(p, half, kv):
    blocks = [cut(p, ref[...], half * ref.shape[0] // 2, p.n2) for ref in kv]
    return jnp.concatenate(blocks, axis=0).astype(BF16)


def soft(p, scores, e, tops, sums):
    top = jnp.maximum(jnp.max(scores, axis=0, keepdims=True), LOWEST)
    weight = jnp.exp2(scores - top)
    e[...] = weight
    tops[...] = by_rows(p, top)
    sums[...] = by_rows(p, jnp.sum(weight, axis=0, keepdims=True))


def near_kernel(p, q_own, q_other, *refs):
    kv, outs = refs[: p.g1 // 2], refs[p.g1 // 2 :]
    d = lax.axis_index("seq")
    n1, n2 = p.n1, p.n2
    row = iota((p.g1 // 2 * n1, 1), 0)
    col = iota((1, 2 * p.heads * n1), 1)
    head = first_head(p) + col // (2 * n1)
    own = col % n1
    device = jnp.bitwise_xor(d, col // n1 % 2)
    qpos = p.tokens * device + p.r2 * (own % n2) + (head + DIL1 * (own // n2)) % p.r2
    other = row % n1
    kbase = p.tokens * jnp.bitwise_xor(d, 2 * (row // n1)) + p.r2 * (other % n2)
    kpos = kbase + jnp.bitwise_and(head + DIL1 * (other // n2), p.r2 - 1)
    s = against(p, near_blocks(p, 0, kv), both_cores(q_own, q_other)) * SCALE2
    soft(p, jnp.where(kpos <= qpos, s, -jnp.inf), *outs)


def wide_kernel(p, q_own, q_other, *refs):
    kv, outs = refs[: p.g2 // 2], refs[p.g2 // 2 :]
    d = lax.axis_index("seq")
    n1, n2 = p.n1, p.n2
    row = iota((p.g2 // 2 * n2, 1), 0)
    row = jnp.bitwise_xor(d, 2 * (row // n2)) * n2 + row % n2
    col = iota((1, 2 * p.heads * n1), 1)
    last = jnp.bitwise_xor(d, col // n1 % 2) * n2 + col % n1
    last = jnp.where(col % n1 < n2, last, -1)
    s = against(p, wide_blocks(p, 0, kv), both_cores(q_own, q_other)) * SCALE2
    soft(p, jnp.where(row <= last, s, -jnp.inf), *outs)


def delta_kernel(p, g_own, g_other, e1, e2, top1, sum1, top2, sum2, lse01, d01, *refs):
    kv, (dp1, dp2, stats) = refs[: p.g2 // 2], refs[p.g2 // 2 :]
    g = both_cores(g_own, g_other)
    dp = against(p, near_blocks(p, 1, kv), g)
    dp1[...] = dp
    near = by_rows(p, jnp.sum(e1[...] * dp, axis=0, keepdims=True))
    dp = against(p, wide_blocks(p, 1, kv), g)
    dp2[...] = dp
    wide = by_rows(p, jnp.sum(e2[...] * dp, axis=0, keepdims=True))

    peak = jnp.maximum(top1[...], top2[...])
    up1, up2 = jnp.exp2(top1[...] - peak), jnp.exp2(top2[...] - peak)
    both = jnp.maximum(sum1[...] * up1 + sum2[...] * up2, TINY)
    d = (near * up1 + wide * up2) / both
    total, delta = join(lse01[...], d01[...], peak + jnp.log2(both), d)
    stats[...] = jnp.concatenate([total, delta], axis=0)


def join(lse_a, d_a, lse_b, d_b):
    peak = jnp.maximum(lse_a, lse_b)
    total = peak + jnp.log2(jnp.exp2(lse_a - peak) + jnp.exp2(lse_b - peak))
    return total, jnp.exp2(lse_a - total) * d_a + jnp.exp2(lse_b - total) * d_b


def levels_kernel(
    p, q_own, q_other, g_own, g_other, e1, e2, top1, top2, dp1, dp2, mine, theirs, *refs
):
    ds1, ds2, total1, delta1, own_part = refs[:5]
    outs, (dk1, dv1, dk2, dv2) = refs[5:-4], refs[-4:]
    n1, n2 = p.n1, p.n2
    came = pltpu.roll(theirs[...], n1, 1)
    total, delta = join(mine[: p.heads, :], mine[p.heads :, :], came[: p.heads], came[p.heads :])
    total1[...] = total
    delta1[...] = delta
    delta = along(p, delta)
    q, g = both_cores(q_own, q_other), both_cores(g_own, g_other)
    for ref in (dk1, dv1, dk2, dv2):
        ref[...] = jnp.zeros_like(ref)
    for e, top, dp, kept, dk, dv in ((e1, top1, dp1, ds1, dk1, dv1), (e2, top2, dp2, ds2, dk2, dv2)):
        prob = e[...] * along(p, jnp.exp2(top[...] - total))
        ds = (prob * (dp[...] - delta) * SCALE).astype(BF16)
        kept[...] = ds
        collect(p, prob.astype(BF16), g, dv)
        collect(p, ds, q, dk)
    for i in range(p.g2 // 2):
        rows = slice(i * n2, (i + 1) * n2)
        if 2 * i < p.g1:
            head = slice(i * n1, i * n1 + n2)
            rest = slice(i * n1 + n2, (i + 1) * n1)
            part = []
            for near, wide in ((dk1, dk2), (dv1, dv2)):
                part += [near[head, :] + wide[rows, :], near[rest, :]]
        else:
            part = [dk2[rows, :], dv2[rows, :]]
        part = jnp.concatenate(part, axis=0)
        ref = outs[i - 1] if i else own_part
        ref[...] = part.astype(ref.dtype)


def queries_kernel(p, ds1, ds2, *refs):
    kv, (dq_own, dq_low, dq_high, dq) = refs[: p.g2 // 2], refs[p.g2 // 2 :]
    k1, k2 = near_blocks(p, 0, kv), wide_blocks(p, 0, kv)
    count = 2 * p.n1
    for first, end, low, high in head_groups(p):
        columns = slice(first * count, end * count)
        part = tn(ds1[:, columns], k1[:, low:high]) + tn(ds2[:, columns], k2[:, low:high])
        for h in range(first, end):
            low_h, high_h = window(h)
            at = (h - first) * count
            piece = part[at : at + count, low_h - low : high_h - low]
            hit = window_mask(h, low_h, high_h)
            dq[:, low_h:high_h] = jnp.where(hit, piece, dq[:, low_h:high_h])
    dq_own[...] = dq[: p.n1, :]
    half = p.n1 // 2
    dq_low[...] = dq[p.n1 : p.n1 + half, :].astype(BF16)
    dq_high[...] = dq[p.n1 + half :, :].astype(BF16)


def own_grad_kernel(
    p, qp, kp, gp, weight_a, weight_b, dprob, lse0, d0, total1, delta1, own_part, dq, dk0, dv0
):
    lse = lse0[...]
    share = jnp.exp2(lse - spread_stat(p, total1[...], lse))
    delta = spread_stat(p, delta1[...], d0[...])
    zero = jnp.zeros((p.tokens, p.width), F32)
    dk0[...] = spread(p, own_part[: p.n1, :], column_class(p), zero)
    dv0[...] = spread(p, own_part[p.n1 :, :], column_class(p), zero)
    for h in range(p.heads):
        low, high = window(h)
        rows = slice(h * p.tokens, (h + 1) * p.tokens)
        hit = window_mask(h, low, high)
        mask = jnp.where(hit, 1.0, 0.0).astype(BF16)
        prob = own_weight(p, weight_a, weight_b, h) * share[h : h + 1, :]
        ds = (prob * (dprob[rows, :] - delta[h : h + 1, :]) * SCALE).astype(BF16)
        dq[:, low:high] = jnp.where(hit, tn(ds, kp[:, low:high]), dq[:, low:high])
        dk0[:, low:high] += nn(ds, qp[:, low:high] * mask)
        dv0[:, low:high] += nn(prob.astype(BF16), gp[:, low:high] * mask)


def finish_kernel(p, dq, dq_own, dq_low, dq_high, grad_q):
    kept = dq_own[...] + both_cores(dq_low, dq_high).astype(F32)
    zero = jnp.zeros((p.tokens, p.width), F32)
    whole = dq[...] + spread(p, kept, column_class(p), zero)
    grad_q[...] = nn(phase_order(p, True), whole.astype(BF16)).astype(BF16)


def last_kernel(p, dk0, dv0, *refs):
    came, (grad_k, grad_v, out_k, out_v, sems) = refs[:-5], refs[-5:]
    order = phase_order(p, True)
    label = column_class(p)
    zero = jnp.zeros((p.tokens, p.width), F32)
    copies = []
    for index, (base, out, grad) in enumerate(((dk0, out_k, grad_k), (dv0, out_v, grad_v))):
        first = jnp.zeros((p.n2, p.width), F32)
        rest = jnp.zeros((p.n1 - p.n2, p.width), F32)
        for ref in came:
            half = ref.shape[0] // 2
            block = ref[...].astype(F32)
            first = first + block[index * half : index * half + p.n2]
            if half == p.n1:
                rest = rest + block[index * half + p.n2 : (index + 1) * half]
        kept = jnp.concatenate([first, rest], axis=0)
        whole = base[...] + spread(p, kept, label, zero)
        out[...] = nn(order, whole.astype(BF16)).astype(BF16)
        copies.append(pltpu.make_async_copy(out, grad, sems.at[index]))
        copies[-1].start()
    for copy in copies:
        copy.wait()


def swap(block, axis, bits):
    count = lax.axis_size(axis)
    return lax.ppermute(block, axis, [(i, i ^ bits) for i in range(count)])


def body(queries, keys, values, grad_out):
    tokens, width = queries.shape
    queries, keys, values, grad_out = (
        pltpu.with_memory_space_constraint(field, pltpu.HBM)
        for field in (queries, keys, values, grad_out)
    )
    p = Plan(tokens, width, lax.axis_size("seq"), lax.axis_size("head"))
    n1, n2 = p.n1, p.n2
    run = lambda kernel: functools.partial(kernel, p)
    row, kept = (tokens, width), (n1, width)
    share = (tokens // p.zcount, width)
    stat, stat1 = (p.heads, tokens), (p.heads, 2 * n1)
    flat = lambda count: (count, tokens)
    even = range(0, p.g2, 2)
    half_rows = sum(p.rows[::2])
    hbm = pl.BlockSpec(memory_space=pltpu.HBM)

    outs = call(
        run(pack_kernel),
        [(row, BF16)] * 3
        + [(kept, BF16), ((2 * n1, width), BF16), ((2 * n2, width), BF16)]
        + [(share, BF16)] * p.zcount,
        [(row, BF16)] * 3 + [pltpu.SemaphoreType.DMA((p.zcount + 3,))],
        in_specs=[hbm] * 4,
    )(queries, keys, values, grad_out)
    qp, kp, vp, q1, kv1, kv2 = outs[:6]
    gz = outs[6:]
    gz = [gz[0]] + [swap(gz[b], "head", b) for b in range(1, p.zcount)]

    kv = [kv1] + [swap(kv1 if b < p.g1 else kv2, "seq", b) for b in even[1:]]

    q_other = swap(q1, "seq", 1)
    half = p.heads // 2
    lows = [(flat(half * tokens), F32), ((half, tokens), F32)]
    weight_a, lse_a = call(functools.partial(own_scores_kernel, p, 0, half), lows)(qp, kp, q_other)
    weight_b, lse_b = call(functools.partial(own_scores_kernel, p, half, p.heads), lows)(
        qp, kp, q_other
    )
    near = (p.g1 // 2 * n1, 2 * p.heads * n1)
    wide = (p.g2 // 2 * n2, 2 * p.heads * n1)
    e1, top1, sum1 = call(run(near_kernel), [(near, F32)] + [(stat1, F32)] * 2)(
        q1, q_other, *kv[: p.g1 // 2]
    )
    e2, top2, sum2 = call(run(wide_kernel), [(wide, F32)] + [(stat1, F32)] * 2)(
        q1, q_other, *kv
    )
    gp, g1 = call(run(gather_kernel), [(row, BF16), (kept, BF16)], [(row, BF16)])(
        lse_a, *[gz[b] for b in block_order(p)]
    )
    g_other = swap(g1, "seq", 1)
    dprob, d0, d01, lse0, lse01 = call(
        run(own_delta_kernel),
        [(flat(p.heads * tokens), F32)] + [(stat, F32), (stat1, F32)] * 2,
    )(vp, weight_a, weight_b, lse_a, lse_b, gp)
    dp1, dp2, mine = call(
        run(delta_kernel), [(near, F32), (wide, F32), ((2 * p.heads, 2 * n1), F32)]
    )(g1, g_other, e1, e2, top1, sum1, top2, sum2, lse01, d01, *kv)
    theirs = swap(mine, "seq", 1)
    part = lambda b, dtype: ((p.rows[b], width), dtype)
    outs = call(
        run(levels_kernel),
        [(near, BF16), (wide, BF16), (stat1, F32), (stat1, F32), part(0, F32)]
        + [part(b, BF16) for b in even[1:]],
        [((near[0], width), F32)] * 2 + [((wide[0], width), F32)] * 2,
    )(q1, q_other, g1, g_other, e1, e2, top1, top2, dp1, dp2, mine, theirs)
    ds1, ds2, total1, delta1, own_part = outs[:5]
    parts = [swap(s, "seq", b) for s, b in zip(outs[5:], even[1:])]
    dq_own, *dq_other = call(
        run(queries_kernel),
        [(kept, F32)] + [((n1 // 2, width), BF16)] * 2,
        [((2 * n1, width), F32)],
    )(ds1, ds2, *kv)
    dq_came = [swap(half, "seq", 1) for half in dq_other]
    dq, dk0, dv0 = call(run(own_grad_kernel), [(row, F32)] * 3)(
        qp, kp, gp, weight_a, weight_b, dprob, lse0, d0, total1, delta1, own_part
    )
    (grad_q,) = call(run(finish_kernel), [(row, BF16)])(dq, dq_own, *dq_came)
    grad_k, grad_v = call(
        run(last_kernel),
        [(row, BF16)] * 2,
        [(row, BF16)] * 2 + [pltpu.SemaphoreType.DMA((2,))],
        out_specs=[hbm] * 2,
    )(dk0, dv0, *parts)
    return grad_q, grad_k, grad_v


def solution(mesh):
    return jax.shard_map(
        body,
        mesh=mesh,
        in_specs=(P("seq", "head"), P("seq", "head"), P("seq", "head"), P(("seq", "head"), None)),
        out_specs=(P("seq", "head"), P("seq", "head"), P("seq", "head")),
        check_vma=False,
    )
```
